256 devices in a mesh: gx: 8 (over z), gy: 8 (over y, core), gz: 4 (over x).
Axes of the slice: x: 4, y: 4, z: 8, core: 2. Of those that a mesh axis runs over, the one named last changes fastest.
Arguments:
- right_side: float32 [128, 128, 512], P('gx', 'gy', 'gz'), may hold values from -10 to 10
- initial: float32 [128, 128, 512], P('gx', 'gy', 'gz'), may hold values from -8 to 8
- shift: float32 [128, 128, 512], P('gx', 'gy', 'gz'), may hold values from 0.05 to 0.5
- beta: float32 [128, 128, 512], P('gx', 'gy', 'gz'), may hold values from 0.5 to 5
Outputs:
- solution_field: float32 [128, 128, 512], P('gx', 'gy', 'gz')
- residual: float32 [128, 128, 512], P('gx', 'gy', 'gz')
The draws below stay inside these ranges and needn't reach their ends.
All inputs are finite; a program needn't handle non-finite values.
Results may differ from the reference program's by a relative error of at most 0.0003.
Values sent between devices are 32-bit elements; how exact they have to be, the bound alone decides.
A program may use at most 128 MiB of HBM per device.

```python
import math
import jax
import jax.numpy as jnp
from jax import lax

SWEEPS = 2
CG_ITERS = 8
NX = 128
NY = 128
NZ = 512


def draw_right_side(key, part):
    key = jax.random.fold_in(key, 11)
    shape = (NX, NY, NZ)
    position = lax.broadcasted_iota(jnp.int32, shape, 0).astype(jnp.float32) / float(max(NX - 1, 1))
    noise = jnp.clip(jax.random.normal(key, shape, jnp.float32), -2.5, 2.5)
    ramp = jnp.exp(jnp.log(4.0) * position)
    return jnp.clip(noise * ramp, -10.0, 10.0)


def block_levels(rng, extent, cuts, smallest, largest):
    def one(axis_at, parts):
        draws = jax.random.uniform(jax.random.fold_in(jax.random.fold_in(rng, 6), axis_at), (parts,), jnp.float32, smallest / len(cuts), largest / len(cuts))
        return jnp.repeat(jnp.exp(draws), extent[axis_at] // parts).reshape((-1,) + (1,) * (len(extent) - axis_at - 1))

    loudness = one(*cuts[0])
    for cut in cuts[1:]:
        loudness = loudness * one(*cut)
    return loudness


def gaussian(key, shape, deviation, reach, pieces=(), held_as=jnp.bfloat16):
    drawn = jax.random.normal(key, shape, jnp.float32) * deviation
    if len(pieces) > 0:
        drawn = block_levels(key, shape, pieces, -0.22, 0.18) * drawn
    return jnp.clip(drawn, min=-reach, max=reach).astype(held_as)


def setup_inputs(seed: int = 0) -> dict:
    seeds = jax.random.split(jax.random.key(seed), 5)
    return {
        "right_side": draw_right_side(jax.random.fold_in(seeds[4], 71), 0),
        "initial": gaussian(seeds[1], (NX, NY, NZ), 1.0, 8.0, ((0, 8), (1, 8), (2, 4)), jnp.float32),
        "shift": jnp.clip(jnp.exp(math.log(0.5) - 2.3025851 * jax.random.uniform(seeds[2], (NX, NY, NZ), jnp.float32) ** block_levels(seeds[2], (NX, NY, NZ), ((0, 8), (1, 8), (2, 4)), -0.2, 0.2)), 0.05, 0.5),
        "beta": jnp.clip(jnp.exp(math.log(5.0) - 2.3025851 * jax.random.uniform(seeds[3], (NX, NY, NZ), jnp.float32) ** block_levels(seeds[3], (NX, NY, NZ), ((0, 8), (1, 8), (2, 4)), -0.2, 0.2)), 0.5, 5.0),
    }


def face_weights(padded):
    center = padded[1:-1, 1:-1, 1:-1]
    return (0.5 * (center + padded[2:, 1:-1, 1:-1]), 0.5 * (center + padded[:-2, 1:-1, 1:-1]),
            0.5 * (center + padded[1:-1, 2:, 1:-1]), 0.5 * (center + padded[1:-1, :-2, 1:-1]),
            0.5 * (center + padded[1:-1, 1:-1, 2:]), 0.5 * (center + padded[1:-1, 1:-1, :-2]))


def nearby(padded):
    return (padded[2:, 1:-1, 1:-1], padded[:-2, 1:-1, 1:-1], padded[1:-1, 2:, 1:-1],
            padded[1:-1, :-2, 1:-1], padded[1:-1, 1:-1, 2:], padded[1:-1, 1:-1, :-2])


def relax_core(padded, source, shift_term, weight_list, scale):
    values = nearby(padded)
    upper_sum = weight_list[0] * values[0]
    lower_sum = weight_list[0]
    for position in range(1, 6):
        upper_sum = upper_sum + weight_list[position] * values[position]
        lower_sum = lower_sum + weight_list[position]
    return (source + scale * upper_sum) / (shift_term + scale * lower_sum)


def operate(padded, shift_term, weight_list, scale):
    center = padded[1:-1, 1:-1, 1:-1]
    values = nearby(padded)
    total = weight_list[0] * (center - values[0])
    for position in range(1, 6):
        total = total + weight_list[position] * (center - values[position])
    return shift_term * center + scale * total


def parity(shape, offset):
    first_index = lax.broadcasted_iota(jnp.int32, shape, 0)
    second_index = lax.broadcasted_iota(jnp.int32, shape, 1)
    third_index = lax.broadcasted_iota(jnp.int32, shape, 2)
    return (first_index + second_index + third_index + offset) % 2 == 0


def restrict(values):
    size_a, size_b, size_c = values.shape
    return values.reshape(size_a // 2, 2, size_b // 2, 2, size_c // 2, 2).mean(axis=(1, 3, 5))


def prolong(values):
    return jnp.repeat(jnp.repeat(jnp.repeat(values, 2, axis=0), 2, axis=1), 2, axis=2)


def smooth(field, source, shift_term, weight_list, scale):
    red = parity(field.shape, 0)
    for repeat_index in range(SWEEPS):
        for colour in (red, jnp.logical_not(red)):
            field = jnp.where(colour, relax_core(jnp.pad(field, 1), source, shift_term, weight_list, scale), field)
    return field


def conjugate(source, shift_term, weight_list, scale):
    solution = jnp.zeros_like(source)
    remain = source
    direction = source
    norm_now = jnp.sum(remain * remain)
    for repeat_index in range(CG_ITERS):
        image = operate(jnp.pad(direction, 1), shift_term, weight_list, scale)
        step_size = norm_now / jnp.sum(direction * image)
        solution = solution + step_size * direction
        remain = remain - step_size * image
        norm_next = jnp.sum(remain * remain)
        direction = remain + (norm_next / norm_now) * direction
        norm_now = norm_next
    return solution


def reference(right_side, initial, shift, beta):
    shift_one = restrict(shift)
    shift_two = restrict(shift_one)
    beta_one = restrict(beta)
    beta_two = restrict(beta_one)
    weights_zero = face_weights(jnp.pad(beta, 1))
    weights_one = face_weights(jnp.pad(beta_one, 1))
    weights_two = face_weights(jnp.pad(beta_two, 1))
    pre_zero = smooth(initial, right_side, shift, weights_zero, 1.0)
    source_one = restrict(right_side - operate(jnp.pad(pre_zero, 1), shift, weights_zero, 1.0))
    pre_one = smooth(jnp.zeros_like(source_one), source_one, shift_one, weights_one, 0.25)
    source_two = restrict(source_one - operate(jnp.pad(pre_one, 1), shift_one, weights_one, 0.25))
    bottom = conjugate(source_two, shift_two, weights_two, 0.0625)
    post_one = smooth(pre_one + prolong(bottom), source_one, shift_one, weights_one, 0.25)
    solution_field = smooth(pre_zero + prolong(post_one), right_side, shift, weights_zero, 1.0)
    residual = right_side - operate(jnp.pad(solution_field, 1), shift, weights_zero, 1.0)
    return solution_field, residual
```

```python
import itertools

import jax
import jax.numpy as jnp
from jax import lax
from jax.experimental import pallas as pl
from jax.experimental.pallas import tpu as pltpu
from jax.sharding import PartitionSpec as P

CG_ITERS = 8
MESH = pl.DeviceIdType.MESH
AXES = ("gx", "gy", "gz")
SIZES = (8, 8, 4)
F32 = jnp.float32
BF16 = jnp.bfloat16

ALL26 = [o for o in itertools.product((-1, 0, 1), repeat=3) if o != (0, 0, 0)]
XY8 = [o for o in ALL26 if o[2] == 0]
Z18 = [o for o in ALL26 if o[2] != 0]
Z2 = [(0, 0, -1), (0, 0, 1)]
RING7 = [(k, 0, 0) for k in range(1, 8)]
PLANE31 = [(0, j, k) for j in range(8) for k in range(4) if (j, k) != (0, 0)]


def canonical(offset):
    return tuple(o % n for o, n in zip(offset, SIZES))


PARTNERS = sorted({canonical(o) for o in ALL26 + RING7 + PLANE31})


def source_span(d, start, count, halo):
    if d == 0:
        return pl.ds(start, count)
    return pl.ds(start + count - halo, halo) if d > 0 else pl.ds(start, halo)


def target_span(d, start, count, halo):
    if d == 0:
        return pl.ds(start, count)
    return pl.ds(start - halo, halo) if d > 0 else pl.ds(start + count, halo)


def iota(shape, dim):
    return lax.broadcasted_iota(jnp.int32, shape, dim)


def pick(values, matrix):
    high = values.astype(BF16)
    rest = values - high.astype(F32)
    middle = rest.astype(BF16)
    low = (rest - middle.astype(F32)).astype(BF16)
    out = jnp.dot(low, matrix, preferred_element_type=F32)
    out = out + jnp.dot(middle, matrix, preferred_element_type=F32)
    return out + jnp.dot(high, matrix, preferred_element_type=F32)


def roll(value, shift):
    shift = shift % 128
    return value if shift == 0 else pltpu.roll(value, shift, 1)


def kernel(f_in, u_in, s_in, b_in, x_out, r_out, E0, M0, ZR0, V0, PB0, A0, D0, DG0, FD0,
           C1, R1s, RZ1, S1, M1, ZR1, PS, V1, PB1, A1, D1, DG1, FD1,
           EU, MU, ZU, T16, T8, T4, X16, XB, GC, GS, S2, B2, A2, DG2, PD, RM, AP, XL,
           sem_in, s_e0, r_e0, s_c1z, r_c1z, s_c1, r_c1, s_e2, r_e2, s_uz, r_uz, s_u, r_u,
           s_ps, r_ps, s_gc1, r_gc1, s_gc2, r_gc2, s_gs1, r_gs1, s_gs2, r_gs2):
    gx, gy, gz = (lax.axis_index(a) for a in AXES)
    me = (gx, gy, gz)

    def device(offset):
        return tuple(lax.rem(m + (o % n), n) if o % n else m for m, o, n in zip(me, offset, SIZES))

    def send(src, dst, ssem, rsem, offset):
        copy = pltpu.make_async_remote_copy(src_ref=src, dst_ref=dst, send_sem=ssem, recv_sem=rsem,
                                            device_id=device(offset), device_id_type=MESH)
        copy.start()
        return copy

    def wait(copies):
        for copy in copies:
            copy.wait()

    local = [pltpu.make_async_copy(src, E0.at[k, pl.ds(6, 16), pl.ds(8, 16)], sem_in.at[k])
             for k, src in enumerate((f_in, s_in, u_in, b_in))]
    for copy in local:
        copy.start()
    barrier = pltpu.get_barrier_semaphore()
    for offset in PARTNERS:
        pl.semaphore_signal(barrier, inc=1, device_id=device(offset), device_id_type=MESH)

    q24 = (iota((24, 128), 0) + iota((24, 128), 1)) % 2 == 1
    q32 = (iota((32, 128), 0) + iota((32, 128), 1)) % 2 == 1
    q16 = (iota((16, 128), 0) + iota((16, 128), 1)) % 2 == 1
    lane24 = iota((24, 128), 1)
    one, zero = jnp.float32(1.0), jnp.float32(0.0)

    def y_mask(rows, own_start, own_count):
        row = iota((rows, 128), 0)
        low = jnp.where(gy == 0, zero, one)
        high = jnp.where(gy == 7, zero, one)
        return jnp.where(row < own_start, low, jnp.where(row >= own_start + own_count, high, one))

    def z_mask(rows, low_at, high_at):
        lane = iota((rows, 128), 1)
        low = jnp.where(gz == 0, zero, one)
        high = jnp.where(gz == 3, zero, one)
        return jnp.where(low_at(lane), low, jnp.where(high_at(lane), high, one))

    y32 = y_mask(32, 8, 16)
    mask0 = (y32, y32 * z_mask(32, lambda l: l >= 64, lambda l: l < 64))
    mask1 = (y_mask(40, 16, 8) * z_mask(40, lambda l: l < 32, lambda l: l >= 96),)

    def x_scalar(p, low_end, high_start):
        outside = ((gx == 0) & (p < low_end)) | ((gx == 7) & (p >= high_start))
        return jnp.where(outside, zero, one)

    PD[...] = jnp.zeros_like(PD)
    B2[...] = jnp.zeros_like(B2)
    V1[...] = jnp.zeros_like(V1)
    PB1[...] = jnp.zeros_like(PB1)

    row, col = iota((128, 128), 0), iota((128, 128), 1)
    to_one = jnp.where((col >= 32) & (col < 96) & (col - 32 == row // 2), 0.125, 0.0).astype(BF16)
    to_two = jnp.where((row >= 32) & (row < 96) & (col == (row - 32) // 2), 0.125, 0.0).astype(BF16)
    from_two = jnp.where((col - 32 + 64 * gz + 128) // 2 - 64 == row, 1.0, 0.0).astype(BF16)
    from_one = jnp.where(row - 32 == col // 2, 1.0, 0.0).astype(BF16)
    from_one_edge = jnp.where(
        ((col < 64) & (row == 96 + col // 2)) | ((col >= 64) & (row == col // 2 - 32)), 1.0, 0.0
    ).astype(BF16)

    def restrict_one(sums):
        T16[...] = sums
        folded = T16[:, pl.ds(0, 8, stride=2), :] + T16[:, pl.ds(1, 8, stride=2), :]
        return pick(folded.reshape(64, 128), to_one).reshape(8, 8, 128)

    def restrict_two(sums):
        T8[...] = sums
        total = None
        for x in range(4):
            folded = T8[x, pl.ds(0, 4, stride=2), :] + T8[x, pl.ds(1, 4, stride=2), :]
            T4[x, 0:4] = folded
        full = pick(T4[...].reshape(32, 128), to_two).reshape(4, 8, 128)
        for x in range(4):
            term = roll(full[x], 32 * x)
            total = term if total is None else total + term
        return total[0:4]

    for copy in local:
        copy.wait()

    lane16 = iota((16, 128), 1)
    group = lane16 // 16

    def pack_rows(k, carry):
        total = jnp.zeros((16, 128), F32)
        for odd in range(2):
            for a in range(4):
                value = E0[a, 6 + 2 * k + odd, pl.ds(8, 16), :]
                total = jnp.where(group == 4 * odd + a, roll(value, 8 + 16 * a + 64 * odd), total)
        M0[k] = total
        return carry

    lax.fori_loop(0, 8, pack_rows, 0)
    pl.semaphore_wait(barrier, len(PARTNERS))

    e0 = []
    for n, (dx, dy, dz) in enumerate(ALL26):
        if dz == 0:
            hx = 4 if dx and dy else 5
            e0.append(send(E0.at[:, source_span(dx, 6, 16, hx), source_span(dy, 8, 16, 8)],
                           E0.at[:, target_span(dx, 6, 16, hx), target_span(dy, 8, 16, 8)],
                           s_e0.at[n], r_e0.at[n], (dx, dy, dz)))
        else:
            side = 0 if dz > 0 else 1
            e0.append(send(M0.at[source_span(dx, 0, 8, 2), source_span(dy, 0, 16, 8)],
                           ZR0.at[side, target_span(dx, 2, 8, 2), target_span(dy, 8, 16, 8)],
                           s_e0.at[n], r_e0.at[n], (dx, dy, dz)))

    for k, a in ((0, 1), (1, 3)):
        sums = jnp.stack([E0[a, 6 + 2 * x, pl.ds(8, 16), :] + E0[a, 7 + 2 * x, pl.ds(8, 16), :] for x in range(8)])
        C1[k, pl.ds(8, 8), pl.ds(8, 8)] = restrict_one(sums)
        for x in range(8):
            R1s[k, x] = roll(C1[k, 8 + x, pl.ds(8, 8), :], 64)
    c1z = [send(R1s, RZ1.at[n], s_c1z.at[n], r_c1z.at[n], (0, 0, 1 if n == 0 else -1)) for n in range(2)]
    mine = gy * 4 + gz
    for k in range(2):
        sums = jnp.stack([C1[k, 8 + 2 * x, pl.ds(8, 8), :] + C1[k, 9 + 2 * x, pl.ds(8, 8), :] for x in range(4)])
        GC[mine, gx, k] = restrict_two(sums)
    gc1 = [send(GC.at[mine, gx], GC.at[mine, gx], s_gc1.at[n], r_gc1.at[n], o) for n, o in enumerate(RING7)]
    wait(c1z)
    lane8 = iota((8, 128), 1)
    for k in range(2):
        for x in range(8):
            own = C1[k, 8 + x, pl.ds(8, 8), :]
            C1[k, 8 + x, pl.ds(8, 8), :] = jnp.where(
                lane8 < 32, RZ1[0, k, x], jnp.where(lane8 < 96, own, RZ1[1, k, x]))
    c1 = [send(C1.at[:, source_span(dx, 8, 8, 8), source_span(dy, 8, 8, 8)],
               C1.at[:, target_span(dx, 8, 8, 8), target_span(dy, 8, 8, 8)],
               s_c1.at[n], r_c1.at[n], (dx, dy, 0)) for n, (dx, dy, _) in enumerate(XY8)]

    def around(O, tiles, c, i, r0, q):
        out = []
        centre = [O[t, 1 - c, i + 1, pl.ds(r0, 24), :] for t in range(tiles)]
        ups = [roll(v, -1) for v in centre]
        downs = [roll(v, 1) for v in centre]
        for t in range(tiles):
            low = O[t, 1 - c, i, pl.ds(r0, 24), :]
            high = O[t, 1 - c, i + 2, pl.ds(r0, 24), :]
            other = jnp.where(q, high, low) if c == 0 else jnp.where(q, low, high)
            yp = O[t, 1 - c, i + 1, pl.ds(r0 + 1, 24), :]
            ym = O[t, 1 - c, i + 1, pl.ds(r0 - 1, 24), :]
            if tiles == 2:
                zp = jnp.where(lane24 == 127, ups[1 - t], ups[t])
                zm = jnp.where(lane24 == 0, downs[1 - t], downs[t])
            else:
                zp, zm = ups[0], downs[0]
            out.append((centre[t], other, yp, ym, zp, zm))
        return out

    def coefficients(PB, A, D, DG, tiles, r0, scale, shift_of, mask, x_of):
        for c in range(2):
            def body(i, carry):
                near = around(PB, tiles, c, i, r0, q24)
                for t in range(tiles):
                    b = PB[t, c, i + 1, pl.ds(r0, 24), :]
                    total = shift_of(t, c, i)
                    weights = [(0.5 * scale) * (b + v) for v in near[t]]
                    for w in weights:
                        total = total + w
                    inverse = (1.0 / total) * (mask[t][r0:r0 + 24] * x_of(i + 1))
                    DG[t, c, i] = total
                    D[t, c, i] = inverse
                    for k, w in enumerate(weights):
                        A[t, c, k, i] = w * inverse
                return carry
            lax.fori_loop(0, 12, body, 0)

    def relaxed(V, A, FD, tiles, c, i, r0):
        near = around(V, tiles, c, i, r0, q24)
        out = []
        for t in range(tiles):
            total = FD[t, c, i]
            for k, v in enumerate(near[t]):
                total = total + A[t, c, k, i] * v
            out.append(total)
        return out

    def half(V, A, FD, tiles, c, r0, lo, hi):
        def body(i, carry):
            new = relaxed(V, A, FD, tiles, c, i, r0)
            for t in range(tiles):
                V[t, c, i + 1, pl.ds(r0, 24), :] = new[t]
            return carry
        lax.fori_loop(lo, hi, body, 0)

    def sweeps(V, A, FD, tiles, r0, lo=0, hi=12, first=0):
        for step in range(first, 4):
            half(V, A, FD, tiles, step % 2, r0, lo, hi)

    def residual_pair(V, A, FD, DG, tiles, i, r0):
        out = []
        for c in range(2):
            new = relaxed(V, A, FD, tiles, c, i, r0)[0]
            out.append(DG[0, c, i] * (new - V[0, c, i + 1, pl.ds(r0, 24), :]))
        return out

    def unpack(red, black, q):
        return jnp.where(q, black, red), jnp.where(q, red, black)

    wait(e0)

    lane32 = iota((32, 128), 1)

    def edge_of(a, p):
        merged = jnp.where(lane32 % 16 < 8, ZR0[0, p - 1], ZR0[1, p - 1])
        return roll(merged, -(16 * a + 8)), roll(merged, -(16 * a + 72))

    x0 = lambda p: x_scalar(p, 3, 11)
    x1 = lambda p: x_scalar(p, 5, 9)

    def pack0(p, carry):
        xs = x0(p)
        for dst, a in ((V0, 2), (PB0, 3)):
            even, odd = E0[a, 2 * p], E0[a, 2 * p + 1]
            m = mask0[0] * xs
            dst[0, 0, p] = jnp.where(q32, odd, even) * m
            dst[0, 1, p] = jnp.where(q32, even, odd) * m
        return carry

    lax.fori_loop(0, 14, pack0, 0)
    for p in (0, 13):
        for dst in (V0, PB0):
            for c in range(2):
                dst[1, c, p] = jnp.zeros((32, 128), F32)

    def pack0_edge(p, carry):
        xs = x0(p)
        for dst, a in ((V0, 2), (PB0, 3)):
            even, odd = edge_of(a, p)
            m = mask0[1] * xs
            dst[1, 0, p] = jnp.where(q32, odd, even) * m
            dst[1, 1, p] = jnp.where(q32, even, odd) * m
        for dst, a in ((FD0, 0), (DG0, 1)):
            even, odd = edge_of(a, p)
            dst[1, 0, p - 1] = jnp.where(q32, odd, even)[4:28]
            dst[1, 1, p - 1] = jnp.where(q32, even, odd)[4:28]
            even, odd = E0[a, 2 * p, pl.ds(4, 24), :], E0[a, 2 * p + 1, pl.ds(4, 24), :]
            dst[0, 0, p - 1] = jnp.where(q24, odd, even)
            dst[0, 1, p - 1] = jnp.where(q24, even, odd)
        return carry

    lax.fori_loop(1, 13, pack0_edge, 0)
    coefficients(PB0, A0, D0, DG0, 2, 4, 1.0, lambda t, c, i: DG0[t, c, i], mask0, x0)

    def scale_rhs0(i, carry):
        for t in range(2):
            for c in range(2):
                FD0[t, c, i] = FD0[t, c, i] * D0[t, c, i]
        return carry

    lax.fori_loop(0, 12, scale_rhs0, 0)
    sweeps(V0, A0, FD0, 2, 4)

    sums = []
    for i in range(2, 10):
        red, black = residual_pair(V0, A0, FD0, DG0, 2, i, 4)
        sums.append((red + black)[4:20])
    S1[pl.ds(8, 8), pl.ds(8, 8)] = restrict_one(jnp.stack(sums))
    slot = iota((8, 128), 1) // 16
    for g in range(2):
        total = jnp.zeros((8, 128), F32)
        for k in range(4):
            value = roll(S1[8 + 4 * g + k, pl.ds(8, 8), :], 64 + 32 * k)
            total = jnp.where((slot == 1 + 2 * k) | (slot == (6 + 2 * k) % 8), value, total)
        M1[g] = total
    e2 = []
    for n, (dx, dy, dz) in enumerate(ALL26):
        if dz == 0:
            e2.append(send(S1.at[source_span(dx, 8, 8, 4), source_span(dy, 8, 8, 8)],
                           S1.at[target_span(dx, 8, 8, 4), target_span(dy, 8, 8, 8)],
                           s_e2.at[n], r_e2.at[n], (dx, dy, dz)))
        else:
            side = 0 if dz > 0 else 1
            e2.append(send(M1.at[source_span(dx, 0, 2, 1), source_span(dy, 0, 8, 8)],
                           ZR1.at[side, target_span(dx, 1, 2, 1), target_span(dy, 8, 8, 8)],
                           s_e2.at[n], r_e2.at[n], (dx, dy, dz)))

    wait(gc1)
    gc2 = [send(GC.at[mine], GC.at[mine], s_gc2.at[n], r_gc2.at[n], o) for n, o in enumerate(PLANE31)]
    for i in range(2, 10):
        red, black = V0[0, 0, i + 1, pl.ds(8, 16), :], V0[0, 1, i + 1, pl.ds(8, 16), :]
        EU[0, 2 * i + 2, pl.ds(8, 16)], EU[0, 2 * i + 3, pl.ds(8, 16)] = unpack(red, black, q16)
    for g in range(2):
        total = jnp.zeros((16, 128), F32)
        for k in range(8):
            total = jnp.where(group == k, roll(EU[0, 6 + 8 * g + k, pl.ds(8, 16), :], 8 + 16 * k), total)
        MU[g] = total
    uz = [send(MU, ZU.at[n], s_uz.at[n], r_uz.at[n], (0, 0, 1 if n == 0 else -1)) for n in range(2)]

    wait(c1)

    def pack1(p, carry):
        xs = x1(p)
        m = mask1[0][8:32] * xs
        even, odd = C1[1, 2 * p - 2], C1[1, 2 * p - 1]
        PB1[0, 0, p, pl.ds(8, 24), :] = jnp.where(q24, odd, even) * m
        PB1[0, 1, p, pl.ds(8, 24), :] = jnp.where(q24, even, odd) * m
        even, odd = C1[0, 2 * p - 2], C1[0, 2 * p - 1]
        DG1[0, 0, p - 1] = jnp.where(q24, odd, even)
        DG1[0, 1, p - 1] = jnp.where(q24, even, odd)
        return carry

    lax.fori_loop(1, 13, pack1, 0)
    coefficients(PB1, A1, D1, DG1, 1, 8, 0.25, lambda t, c, i: DG1[t, c, i], mask1, x1)

    wait(e2)
    slot24 = lane24 // 16
    for x in range(4, 20):
        g = (x - 4) // 4
        merged = jnp.where(slot24 % 2 == 1, ZR1[0, g], ZR1[1, g])
        halo = roll(merged, -32 * (x % 4))
        S1[x] = jnp.where((lane24 >= 32) & (lane24 < 96), S1[x], halo)
    PS[1, pl.ds(8, 8), pl.ds(8, 8)] = S1[pl.ds(8, 8), pl.ds(8, 8)]

    def rhs1(source, lo, hi):
        def body(i, carry):
            even, odd = source[2 * i], source[2 * i + 1]
            FD1[0, 0, i] = jnp.where(q24, odd, even) * D1[0, 0, i]
            FD1[0, 1, i] = jnp.where(q24, even, odd) * D1[0, 1, i]
            return carry
        lax.fori_loop(lo, hi, body, 0)

    rhs1(S1, 2, 10)
    for i in range(2, 10):
        V1[0, 0, i + 1, pl.ds(8, 24), :] = FD1[0, 0, i]
    sweeps(V1, A1, FD1, 1, 8, 2, 10, first=1)
    sums = []
    for i in range(4, 8):
        red, black = residual_pair(V1, A1, FD1, DG1, 1, i, 8)
        sums.append((red + black)[8:16])
    GS[mine, gx] = restrict_two(jnp.stack(sums))
    gs1 = [send(GS.at[mine, gx], GS.at[mine, gx], s_gs1.at[n], r_gs1.at[n], o) for n, o in enumerate(RING7)]

    q8 = (iota((8, 128), 0) + iota((8, 128), 1)) % 2 == 1
    for i in range(4, 8):
        red, black = V1[0, 0, i + 1, pl.ds(16, 8), :], V1[0, 1, i + 1, pl.ds(16, 8), :]
        PS[0, 2 * i, pl.ds(8, 8)], PS[0, 2 * i + 1, pl.ds(8, 8)] = unpack(red, black, q8)
    ps = [send(PS.at[:, source_span(dx, 8, 8, 8), source_span(dy, 8, 8, 8)],
               PS.at[:, target_span(dx, 8, 8, 8), target_span(dy, 8, 8, 8)],
               s_ps.at[n], r_ps.at[n], (dx, dy, 0)) for n, (dx, dy, _) in enumerate(XY8)]
    wait(uz)
    for x in range(16):
        merged = jnp.where(lane16 % 16 < 8, ZU[0, x // 8], ZU[1, x // 8])
        EU[1, 6 + x, pl.ds(8, 16)] = roll(merged, -(16 * (x % 8) + 8))
    wait(gs1)
    gs2 = [send(GS.at[mine], GS.at[mine], s_gs2.at[n], r_gs2.at[n], o) for n, o in enumerate(PLANE31)]
    eu = [send(EU.at[:, source_span(dx, 6, 16, 5), source_span(dy, 8, 16, 8)],
               EU.at[:, target_span(dx, 6, 16, 5), target_span(dy, 8, 16, 8)],
               s_u.at[n], r_u.at[n], (dx, dy, 0)) for n, (dx, dy, _) in enumerate(XY8)]

    lane_group = lane8 // 32

    def spread(load, store):
        def body(g, carry):
            for pair in range(4):
                blocks = [jnp.concatenate([load(8 * pair + k, g), load(8 * pair + 4 + k, g)], axis=0)
                          for k in range(4)]
                for x in range(4):
                    total = roll(blocks[0], -32 * x)
                    for k in range(1, 4):
                        total = jnp.where(lane_group == k, roll(blocks[k], 32 * (k - x)), total)
                    store(4 * g + x, 8 * pair, total)
            return carry
        lax.fori_loop(0, 8, body, 0)

    def store_s2(x, y, v):
        S2[x, pl.ds(y, 8), :] = v

    def store_b2(x, y, v):
        B2[x + 4, pl.ds(y + 8, 8), :] = v

    def store_source(x, y, v):
        PD[x + 4, pl.ds(y + 8, 8), :] = v
        RM[x, pl.ds(y, 8), :] = v

    wait(gc2)
    spread(lambda j, g: GC[j, g, 0], store_s2)
    spread(lambda j, g: GC[j, g, 1], store_b2)

    def shifts(O, x):
        centre = O[x + 4, pl.ds(8, 32), :]
        return (centre, (O[x + 5, pl.ds(8, 32), :], O[x + 3, pl.ds(8, 32), :], O[x + 4, pl.ds(9, 32), :],
                         O[x + 4, pl.ds(7, 32), :], roll(centre, -1), roll(centre, 1)))

    def weights2(x, carry):
        b, near = shifts(B2, x)
        total = S2[x]
        for k, v in enumerate(near):
            if k == 4:
                v = jnp.where(lane32 == 127, 0.0, v)
            if k == 5:
                v = jnp.where(lane32 == 0, 0.0, v)
            w = (0.5 * 0.0625) * (b + v)
            total = total + w
            if k == 4:
                w = jnp.where(lane32 == 127, 0.0, w)
            if k == 5:
                w = jnp.where(lane32 == 0, 0.0, w)
            A2[k, x] = w
        DG2[x] = total
        return carry

    lax.fori_loop(0, 32, weights2, 0)

    wait(ps)

    def pack1_post(p, carry):
        m = mask1[0][8:32] * x1(p)
        even, odd = PS[0, 2 * p - 2], PS[0, 2 * p - 1]
        V1[0, 0, p, pl.ds(8, 24), :] = jnp.where(q24, odd, even) * m
        V1[0, 1, p, pl.ds(8, 24), :] = jnp.where(q24, even, odd) * m
        return carry

    lax.fori_loop(1, 13, pack1_post, 0)
    rhs1(PS.at[1], 0, 12)

    wait(eu)

    def pack0_post(p, carry):
        xs = x0(p)
        for t in range(2):
            m = mask0[t] * xs
            even, odd = EU[t, 2 * p], EU[t, 2 * p + 1]
            V0[t, 0, p] = jnp.where(q32, odd, even) * m
            V0[t, 1, p] = jnp.where(q32, even, odd) * m
        return carry

    lax.fori_loop(0, 14, pack0_post, 0)

    wait(gs2)
    spread(lambda j, g: GS[j, g], store_source)
    XL[...] = jnp.zeros_like(XL)

    def whole(total):
        return jnp.sum(jnp.sum(total, axis=0, keepdims=True), axis=1, keepdims=True)

    def square(x, total):
        return total + RM[x] * RM[x]

    acc = jnp.zeros((32, 128), F32)
    rr = whole(lax.fori_loop(0, 32, square, acc))
    for step in range(CG_ITERS):
        def image(x, total):
            p, near = shifts(PD, x)
            value = DG2[x] * p
            for k, v in enumerate(near):
                value = value - A2[k, x] * v
            AP[x] = value
            return total + p * value

        alpha = rr / whole(lax.fori_loop(0, 32, image, acc))

        def gain(x, carry):
            XL[x] = XL[x] + alpha * PD[4 * gx + x, pl.ds(4 * gy + 4, 16), :]
            return carry

        lax.fori_loop(0, 12, gain, 0)
        if step < CG_ITERS - 1:
            def update(x, total):
                value = RM[x] - alpha * AP[x]
                RM[x] = value
                return total + value * value

            new = whole(lax.fori_loop(0, 32, update, acc))
            ratio = new / rr

            def turn(x, carry):
                PD[x + 4, pl.ds(8, 32), :] = RM[x] + ratio * PD[x + 4, pl.ds(8, 32), :]
                return carry

            lax.fori_loop(0, 32, turn, 0)
            rr = new

    fine = pick(XL[...].reshape(192, 128), from_two).reshape(12, 16, 128)
    X16[:, pl.ds(0, 16, stride=2), :] = fine
    X16[:, pl.ds(1, 16, stride=2), :] = fine

    def correct1(i, carry):
        for c in range(2):
            V1[0, c, i + 1, pl.ds(8, 24), :] = V1[0, c, i + 1, pl.ds(8, 24), :] + X16[i, 0:24]
        return carry

    lax.fori_loop(0, 12, correct1, 0)
    sweeps(V1, A1, FD1, 1, 8)

    planes = []
    for p in range(14):
        k = (p + 7) // 2
        red, black = V1[0, 0, k, pl.ds(12, 16), :], V1[0, 1, k, pl.ds(12, 16), :]
        planes.append(unpack(red, black, q16)[0 if p % 2 else 1])
    coarse = jnp.stack(planes).reshape(224, 128)
    for t, matrix in enumerate((from_one, from_one_edge)):
        fine = pick(coarse, matrix).reshape(14, 16, 128)
        XB[:, pl.ds(0, 16, stride=2), :] = fine
        XB[:, pl.ds(1, 16, stride=2), :] = fine

        def correct0(p, carry):
            for c in range(2):
                V0[t, c, p] = V0[t, c, p] + XB[p]
            return carry

        lax.fori_loop(0, 14, correct0, 0)
    sweeps(V0, A0, FD0, 2, 4)

    def finish(i, carry):
        red, black = residual_pair(V0, A0, FD0, DG0, 2, i, 4)
        even, odd = unpack(red, black, q24)
        r_out[2 * i - 4] = even[4:20]
        r_out[2 * i - 3] = odd[4:20]
        even, odd = unpack(V0[0, 0, i + 1, pl.ds(8, 16), :], V0[0, 1, i + 1, pl.ds(8, 16), :], q16)
        x_out[2 * i - 4] = even
        x_out[2 * i - 3] = odd
        return carry

    lax.fori_loop(2, 10, finish, 0)


def vmem(*shape):
    return pltpu.VMEM(shape, F32)


def dma(*shape):
    return pltpu.SemaphoreType.DMA(shape)


SCRATCH = [
    vmem(4, 28, 32, 128), vmem(8, 16, 128), vmem(2, 12, 32, 128),
    vmem(2, 2, 14, 32, 128), vmem(2, 2, 14, 32, 128), vmem(2, 2, 6, 12, 24, 128),
    vmem(2, 2, 12, 24, 128), vmem(2, 2, 12, 24, 128), vmem(2, 2, 12, 24, 128),
    vmem(2, 24, 24, 128), vmem(2, 8, 8, 128), vmem(2, 2, 8, 8, 128),
    vmem(24, 24, 128), vmem(2, 8, 128), vmem(2, 4, 24, 128), vmem(2, 24, 24, 128),
    vmem(1, 2, 14, 40, 128), vmem(1, 2, 14, 40, 128), vmem(1, 2, 6, 12, 24, 128),
    vmem(1, 2, 12, 24, 128), vmem(1, 2, 12, 24, 128), vmem(1, 2, 12, 24, 128),
    vmem(2, 28, 32, 128), vmem(2, 16, 128), vmem(2, 2, 16, 128),
    vmem(8, 16, 128), vmem(4, 8, 128), vmem(4, 8, 128), vmem(12, 32, 128), vmem(14, 32, 128),
    vmem(32, 8, 2, 4, 128), vmem(32, 8, 4, 128),
    vmem(32, 32, 128), vmem(40, 48, 128), vmem(6, 32, 32, 128), vmem(32, 32, 128),
    vmem(40, 48, 128), vmem(32, 32, 128), vmem(32, 32, 128), vmem(12, 16, 128),
    dma(4), dma(26), dma(26), dma(2), dma(2), dma(8), dma(8), dma(26), dma(26), dma(2), dma(2), dma(8), dma(8),
    dma(8), dma(8), dma(7), dma(7), dma(31), dma(31), dma(7), dma(7), dma(31), dma(31),
]


def solution(mesh):
    def local(right_side, initial, shift, beta):
        shape = jax.ShapeDtypeStruct(right_side.shape, F32)
        return pl.pallas_call(
            kernel,
            out_shape=(shape, shape),
            in_specs=[pl.BlockSpec(memory_space=pl.ANY)] * 4,
            out_specs=(pl.BlockSpec(memory_space=pltpu.VMEM),) * 2,
            scratch_shapes=SCRATCH,
            compiler_params=pltpu.CompilerParams(
                collective_id=0, has_side_effects=True, vmem_limit_bytes=56 * 2**20),
        )(right_side, initial, shift, beta)

    spec = P(*AXES)
    return jax.shard_map(local, mesh=mesh, in_specs=(spec,) * 4, out_specs=(spec, spec), check_vma=False)
```

```python
import itertools

import jax
import jax.numpy as jnp
from jax import lax
from jax.experimental import pallas as pl
from jax.experimental.pallas import tpu as pltpu
from jax.sharding import PartitionSpec as P

CG_ITERS = 8
MESH = pl.DeviceIdType.MESH
AXES = ("gx", "gy", "gz")
SIZES = (8, 8, 4)
F32 = jnp.float32
BF16 = jnp.bfloat16

ALL26 = [o for o in itertools.product((-1, 0, 1), repeat=3) if o != (0, 0, 0)]
XY8 = [o for o in ALL26 if o[2] == 0]
X6 = [o for o in XY8 if o[0] != 0]
RING7 = [(k, 0, 0) for k in range(1, 8)]
ROW3 = [(0, 0, k) for k in range(1, 4)]
CHIPS3 = [(0, j, 0) for j in (2, 4, 6)]
SAME15 = sorted(((0, j, k) for j in (0, 2, 4, 6) for k in range(4) if (j, k) != (0, 0)),
                key=lambda o: min(o[1], 8 - o[1]) // 2 + min(o[2], 4 - o[2]))


def canonical(offset):
    return tuple(o % n for o, n in zip(offset, SIZES))


PARTNERS = sorted({canonical(o) for o in ALL26 + RING7 + [(0, 4, 0)]})


def source_span(d, start, count, halo):
    if d == 0:
        return pl.ds(start, count)
    return pl.ds(start + count - halo, halo) if d > 0 else pl.ds(start, halo)


def target_span(d, start, count, halo):
    if d == 0:
        return pl.ds(start, count)
    return pl.ds(start - halo, halo) if d > 0 else pl.ds(start + count, halo)


def iota(shape, dim):
    return lax.broadcasted_iota(jnp.int32, shape, dim)


def loop(lo, hi, body, init, unroll):
    def chunk(k, carry):
        for j in range(unroll):
            carry = body(lo + k * unroll + j, carry)
        return carry

    return lax.fori_loop(0, (hi - lo) // unroll, chunk, init)


def pick(values, matrix):
    high = values.astype(BF16)
    rest = values - high.astype(F32)
    middle = rest.astype(BF16)
    low = (rest - middle.astype(F32)).astype(BF16)
    out = jnp.dot(low, matrix, preferred_element_type=F32)
    out = out + jnp.dot(middle, matrix, preferred_element_type=F32)
    return out + jnp.dot(high, matrix, preferred_element_type=F32)


def roll(value, shift):
    shift = shift % 128
    return value if shift == 0 else pltpu.roll(value, shift, 1)


def kernel(f_in, u_in, s_in, b_in, x_out, r_out, E0, M0, ZR0, V0, PB0, A0, D0, DG0, FD0,
           C1, R1s, RZ1, S1, M1, ZR1, PS, V1, PB1, A1, D1, DG1, FD1,
           EU, MU, ZU, T16, T8, T4, X16, XB, GC, GS, S2, B2, A2, DG2, PD, RM, AP, XL,
           sem_in, s_e0, r_e0, s_c1z, r_c1z, s_c1, r_c1, s_e2, r_e2, s_uz, r_uz, s_u, r_u,
           s_ps, r_ps, s_gc1, r_gc1, s_gc2, r_gc2, s_gs1, r_gs1, s_gs2, r_gs2,
           s_gc3, r_gc3, s_gc4, r_gc4, s_gs3, r_gs3, s_c1b, r_c1b):
    gx, gy, gz = (lax.axis_index(a) for a in AXES)
    me = (gx, gy, gz)
    core = lax.rem(gy, 2)
    twin = (gx, gy + 1 - 2 * core, gz)

    def device(offset):
        return tuple(lax.rem(m + (o % n), n) if o % n else m for m, o, n in zip(me, offset, SIZES))

    def send(src, dst, ssem, rsem, offset=None):
        copy = pltpu.make_async_remote_copy(src_ref=src, dst_ref=dst, send_sem=ssem, recv_sem=rsem,
                                            device_id=twin if offset is None else device(offset),
                                            device_id_type=MESH)
        copy.start()
        return copy

    def wait(copies):
        for copy in copies:
            copy.wait()

    local = [pltpu.make_async_copy(src, E0.at[k, pl.ds(6, 16), pl.ds(8, 16)], sem_in.at[k])
             for k, src in enumerate((f_in, s_in, u_in, b_in))]
    for copy in local:
        copy.start()
    barrier = pltpu.get_barrier_semaphore()
    for offset in PARTNERS:
        pl.semaphore_signal(barrier, inc=1, device_id=device(offset), device_id_type=MESH)

    q24 = (iota((24, 128), 0) + iota((24, 128), 1)) % 2 == 1
    q32 = (iota((32, 128), 0) + iota((32, 128), 1)) % 2 == 1
    q16 = (iota((16, 128), 0) + iota((16, 128), 1)) % 2 == 1
    lane24 = iota((24, 128), 1)
    one, zero = jnp.float32(1.0), jnp.float32(0.0)

    def y_mask(rows, own_start, own_count):
        row = iota((rows, 128), 0)
        low = jnp.where(gy == 0, zero, one)
        high = jnp.where(gy == 7, zero, one)
        return jnp.where(row < own_start, low, jnp.where(row >= own_start + own_count, high, one))

    def z_mask(rows, low_at, high_at):
        lane = iota((rows, 128), 1)
        low = jnp.where(gz == 0, zero, one)
        high = jnp.where(gz == 3, zero, one)
        return jnp.where(low_at(lane), low, jnp.where(high_at(lane), high, one))

    y32 = y_mask(32, 8, 16)
    mask0 = (y32, y32 * z_mask(32, lambda l: l >= 64, lambda l: l < 64))
    mask1 = (y_mask(40, 16, 8) * z_mask(40, lambda l: l < 32, lambda l: l >= 96),)

    def x_scalar(p, low_end, high_start):
        outside = ((gx == 0) & (p < low_end)) | ((gx == 7) & (p >= high_start))
        return jnp.where(outside, zero, one)

    row, col = iota((128, 128), 0), iota((128, 128), 1)
    to_one = jnp.where((col >= 32) & (col < 96) & (col - 32 == row // 2), 0.125, 0.0).astype(BF16)
    to_two = jnp.where((row >= 32) & (row < 96) & (col == (row - 32) // 2), 0.125, 0.0).astype(BF16)
    from_two = jnp.where((col - 32 + 64 * gz + 128) // 2 - 64 == row, 1.0, 0.0).astype(BF16)
    from_one = jnp.where(row - 32 == col // 2, 1.0, 0.0).astype(BF16)
    from_one_edge = jnp.where(
        ((col < 64) & (row == 96 + col // 2)) | ((col >= 64) & (row == col // 2 - 32)), 1.0, 0.0
    ).astype(BF16)

    def restrict_one(sums):
        T16[...] = sums
        folded = T16[:, pl.ds(0, 8, stride=2), :] + T16[:, pl.ds(1, 8, stride=2), :]
        return pick(folded.reshape(64, 128), to_one).reshape(8, 8, 128)

    def restrict_two(sums):
        T8[...] = sums
        total = None
        for x in range(4):
            folded = T8[x, pl.ds(0, 4, stride=2), :] + T8[x, pl.ds(1, 4, stride=2), :]
            T4[x, 0:4] = folded
        full = pick(T4[...].reshape(32, 128), to_two).reshape(4, 8, 128)
        for x in range(4):
            term = roll(full[x], 32 * x)
            total = term if total is None else total + term
        return total[0:4]

    for copy in local:
        copy.wait()
    pl.semaphore_wait(barrier, len(PARTNERS))
    e0 = []
    for n, (dx, dy, dz) in enumerate(ALL26):
        if dz == 0:
            hx = 4 if dx and dy else 5
            e0.append(send(E0.at[:, source_span(dx, 6, 16, hx), source_span(dy, 8, 16, 8)],
                           E0.at[:, target_span(dx, 6, 16, hx), target_span(dy, 8, 16, 8)],
                           s_e0.at[n], r_e0.at[n], (dx, dy, dz)))

    lane16 = iota((16, 128), 1)
    group = lane16 // 16

    def pack_rows(k, carry):
        total = jnp.zeros((16, 128), F32)
        for odd in range(2):
            for a in range(4):
                value = E0[a, 6 + 2 * k + odd, pl.ds(8, 16), :]
                total = jnp.where(group == 4 * odd + a, roll(value, 8 + 16 * a + 64 * odd), total)
        M0[k] = total
        return carry

    loop(0, 8, pack_rows, 0, 4)
    for n, (dx, dy, dz) in enumerate(ALL26):
        if dz != 0:
            side = 0 if dz > 0 else 1
            e0.append(send(M0.at[source_span(dx, 0, 8, 2), source_span(dy, 0, 16, 8)],
                           ZR0.at[side, target_span(dx, 2, 8, 2), target_span(dy, 8, 16, 8)],
                           s_e0.at[n], r_e0.at[n], (dx, dy, dz)))

    PD[...] = jnp.zeros_like(PD)
    B2[...] = jnp.zeros_like(B2)
    V1[...] = jnp.zeros_like(V1)
    PB1[...] = jnp.zeros_like(PB1)

    for k, a in ((0, 1), (1, 3)):
        sums = jnp.stack([E0[a, 6 + 2 * x, pl.ds(8, 16), :] + E0[a, 7 + 2 * x, pl.ds(8, 16), :] for x in range(8)])
        C1[k, pl.ds(8, 8), pl.ds(8, 8)] = restrict_one(sums)
        for x in range(8):
            R1s[k, x] = roll(C1[k, 8 + x, pl.ds(8, 8), :], 64)
    c1z = [send(R1s, RZ1.at[n], s_c1z.at[n], r_c1z.at[n], (0, 0, 1 if n == 0 else -1)) for n in range(2)]
    mine = gy * 4 + gz
    for k in range(2):
        sums = jnp.stack([C1[k, 8 + 2 * x, pl.ds(8, 8), :] + C1[k, 9 + 2 * x, pl.ds(8, 8), :] for x in range(4)])
        GC[mine, gx, k] = restrict_two(sums)
    gc1 = [send(GC.at[mine, gx], GC.at[mine, gx], s_gc1.at[n], r_gc1.at[n], o) for n, o in enumerate(RING7)]
    wait(c1z)
    lane8 = iota((8, 128), 1)
    for k in range(2):
        for x in range(8):
            own = C1[k, 8 + x, pl.ds(8, 8), :]
            C1[k, 8 + x, pl.ds(8, 8), :] = jnp.where(
                lane8 < 32, RZ1[0, k, x], jnp.where(lane8 < 96, own, RZ1[1, k, x]))
    c1 = [send(C1.at[:, source_span(dx, 8, 8, 4), source_span(dy, 8, 8, 8)],
               C1.at[:, target_span(dx, 8, 8, 4), target_span(dy, 8, 8, 8)],
               s_c1.at[n], r_c1.at[n], (dx, dy, 0)) for n, (dx, dy, _) in enumerate(XY8)]
    def around(O, tiles, c, i, r0, q):
        out = []
        centre = [O[t, 1 - c, i + 1, pl.ds(r0, 24), :] for t in range(tiles)]
        ups = [roll(v, -1) for v in centre]
        downs = [roll(v, 1) for v in centre]
        for t in range(tiles):
            low = O[t, 1 - c, i, pl.ds(r0, 24), :]
            high = O[t, 1 - c, i + 2, pl.ds(r0, 24), :]
            other = jnp.where(q, high, low) if c == 0 else jnp.where(q, low, high)
            yp = O[t, 1 - c, i + 1, pl.ds(r0 + 1, 24), :]
            ym = O[t, 1 - c, i + 1, pl.ds(r0 - 1, 24), :]
            if tiles == 2:
                zp = jnp.where(lane24 == 127, ups[1 - t], ups[t])
                zm = jnp.where(lane24 == 0, downs[1 - t], downs[t])
            else:
                zp, zm = ups[0], downs[0]
            out.append((centre[t], other, yp, ym, zp, zm))
        return out

    def coefficients(PB, A, D, DG, tiles, r0, scale, shift_of, mask, x_of, lo=0, hi=12):
        for c in range(2):
            def body(i, carry):
                near = around(PB, tiles, c, i, r0, q24)
                for t in range(tiles):
                    b = PB[t, c, i + 1, pl.ds(r0, 24), :]
                    total = shift_of(t, c, i)
                    weights = [(0.5 * scale) * (b + v) for v in near[t]]
                    for w in weights:
                        total = total + w
                    inverse = (1.0 / total) * (mask[t][r0:r0 + 24] * x_of(i + 1))
                    DG[t, c, i] = total
                    D[t, c, i] = inverse
                    for k, w in enumerate(weights):
                        A[t, c, k, i] = w * inverse
                return carry
            loop(lo, hi, body, 0, 2)

    def relaxed(V, A, FD, tiles, c, i, r0):
        near = around(V, tiles, c, i, r0, q24)
        out = []
        for t in range(tiles):
            total = FD[t, c, i]
            for k, v in enumerate(near[t]):
                total = total + A[t, c, k, i] * v
            out.append(total)
        return out

    def half(V, A, FD, tiles, c, r0, lo, hi):
        unroll = 4 if tiles == 1 else 2

        def body(k, carry):
            first = lo + k * unroll
            news = [relaxed(V, A, FD, tiles, c, first + j, r0) for j in range(unroll)]
            for j, new in enumerate(news):
                for t in range(tiles):
                    V[t, c, first + j + 1, pl.ds(r0, 24), :] = new[t]
            return carry
        lax.fori_loop(0, (hi - lo) // unroll, body, 0)

    def sweeps(V, A, FD, tiles, r0, lo=0, hi=12, first=0):
        for step in range(first, 4):
            half(V, A, FD, tiles, step % 2, r0, lo, hi)

    def residual_pair(V, A, FD, DG, tiles, i, r0):
        out = []
        for c in range(2):
            new = relaxed(V, A, FD, tiles, c, i, r0)[0]
            out.append(DG[0, c, i] * (new - V[0, c, i + 1, pl.ds(r0, 24), :]))
        return out

    def unpack(red, black, q):
        return jnp.where(q, black, red), jnp.where(q, red, black)

    wait(e0)

    lane32 = iota((32, 128), 1)

    def edge_of(a, p):
        merged = jnp.where(lane32 % 16 < 8, ZR0[0, p - 1], ZR0[1, p - 1])
        return roll(merged, -(16 * a + 8)), roll(merged, -(16 * a + 72))

    x0 = lambda p: x_scalar(p, 3, 11)
    x1 = lambda p: x_scalar(p, 5, 9)

    def pack0(p, carry):
        xs = x0(p)
        for dst, a in ((V0, 2), (PB0, 3)):
            even, odd = E0[a, 2 * p], E0[a, 2 * p + 1]
            m = mask0[0] * xs
            dst[0, 0, p] = jnp.where(q32, odd, even) * m
            dst[0, 1, p] = jnp.where(q32, even, odd) * m
        return carry

    loop(0, 14, pack0, 0, 2)
    for p in (0, 13):
        for dst in (V0, PB0):
            for c in range(2):
                dst[1, c, p] = jnp.zeros((32, 128), F32)

    def pack0_edge(p, carry):
        xs = x0(p)
        for dst, a in ((V0, 2), (PB0, 3)):
            even, odd = edge_of(a, p)
            m = mask0[1] * xs
            dst[1, 0, p] = jnp.where(q32, odd, even) * m
            dst[1, 1, p] = jnp.where(q32, even, odd) * m
        for dst, a in ((FD0, 0), (DG0, 1)):
            even, odd = edge_of(a, p)
            dst[1, 0, p - 1] = jnp.where(q32, odd, even)[4:28]
            dst[1, 1, p - 1] = jnp.where(q32, even, odd)[4:28]
            even, odd = E0[a, 2 * p, pl.ds(4, 24), :], E0[a, 2 * p + 1, pl.ds(4, 24), :]
            dst[0, 0, p - 1] = jnp.where(q24, odd, even)
            dst[0, 1, p - 1] = jnp.where(q24, even, odd)
        return carry

    loop(1, 13, pack0_edge, 0, 2)
    coefficients(PB0, A0, D0, DG0, 2, 4, 1.0, lambda t, c, i: DG0[t, c, i], mask0, x0)

    def scale_rhs0(i, carry):
        for t in range(2):
            for c in range(2):
                FD0[t, c, i] = FD0[t, c, i] * D0[t, c, i]
        return carry

    loop(0, 12, scale_rhs0, 0, 4)
    wait(gc1)
    gc2 = [send(GC.at[mine], GC.at[mine], s_gc2.at[n], r_gc2.at[n], o) for n, o in enumerate(ROW3)]
    sweeps(V0, A0, FD0, 2, 4)

    sums = []
    for i in range(2, 10):
        red, black = residual_pair(V0, A0, FD0, DG0, 2, i, 4)
        sums.append((red + black)[4:20])
    own = restrict_one(jnp.stack(sums))
    wait(c1)

    def pack1(p, carry):
        xs = x1(p)
        m = mask1[0][8:32] * xs
        even, odd = C1[1, 2 * p - 2], C1[1, 2 * p - 1]
        PB1[0, 0, p, pl.ds(8, 24), :] = jnp.where(q24, odd, even) * m
        PB1[0, 1, p, pl.ds(8, 24), :] = jnp.where(q24, even, odd) * m
        even, odd = C1[0, 2 * p - 2], C1[0, 2 * p - 1]
        DG1[0, 0, p - 1] = jnp.where(q24, odd, even)
        DG1[0, 1, p - 1] = jnp.where(q24, even, odd)
        return carry

    def coefficients1(lo, hi):
        loop(lo + 1, hi + 1, pack1, 0, 4)
        coefficients(PB1, A1, D1, DG1, 1, 8, 0.25, lambda t, c, i: DG1[t, c, i], mask1, x1, lo, hi)

    coefficients1(2, 10)
    q8 = (iota((8, 128), 0) + iota((8, 128), 1)) % 2 == 1
    for i in range(4, 8):
        even, odd = own[2 * i - 8], own[2 * i - 7]
        red = jnp.where(q8, odd, even) * D1[0, 0, i, pl.ds(8, 8), :]
        black = jnp.where(q8, even, odd) * D1[0, 1, i, pl.ds(8, 8), :]
        S1[2 * i, pl.ds(8, 8)], S1[2 * i + 1, pl.ds(8, 8)] = unpack(red, black, q8)
    slot = iota((8, 128), 1) // 16
    for g in range(2):
        total = jnp.zeros((8, 128), F32)
        for k in range(4):
            value = roll(S1[8 + 4 * g + k, pl.ds(8, 8), :], 64 + 32 * k)
            total = jnp.where((slot == 1 + 2 * k) | (slot == (6 + 2 * k) % 8), value, total)
        M1[g] = total
    e2 = []
    for n, (dx, dy, dz) in enumerate(ALL26):
        if dz == 0:
            e2.append(send(S1.at[source_span(dx, 8, 8, 4), source_span(dy, 8, 8, 8)],
                           S1.at[target_span(dx, 8, 8, 4), target_span(dy, 8, 8, 8)],
                           s_e2.at[n], r_e2.at[n], (dx, dy, dz)))
        else:
            side = 0 if dz > 0 else 1
            e2.append(send(M1.at[source_span(dx, 0, 2, 1), source_span(dy, 0, 8, 8)],
                           ZR1.at[side, target_span(dx, 1, 2, 1), target_span(dy, 8, 8, 8)],
                           s_e2.at[n], r_e2.at[n], (dx, dy, dz)))

    for i in range(2, 10):
        red, black = V0[0, 0, i + 1, pl.ds(8, 16), :], V0[0, 1, i + 1, pl.ds(8, 16), :]
        EU[0, 2 * i + 2, pl.ds(8, 16)], EU[0, 2 * i + 3, pl.ds(8, 16)] = unpack(red, black, q16)
    for g in range(2):
        total = jnp.zeros((16, 128), F32)
        for k in range(8):
            total = jnp.where(group == k, roll(EU[0, 6 + 8 * g + k, pl.ds(8, 16), :], 8 + 16 * k), total)
        MU[g] = total
    uz = [send(MU, ZU.at[n], s_uz.at[n], r_uz.at[n], (0, 0, 1 if n == 0 else -1)) for n in range(2)]

    wait(gc2)
    row_of = GC.at[pl.ds(gy * 4, 4)]
    gc3 = [send(row_of, row_of, s_gc3.at[n], r_gc3.at[n], o) for n, o in enumerate(CHIPS3)]
    c1b = [send(C1.at[:, source_span(-dx, 8, 8, 4), source_span(dy, 8, 8, 8)],
                C1.at[:, pl.ds(0 if dx > 0 else 20, 4), target_span(dy, 8, 8, 8)],
                s_c1b.at[n], r_c1b.at[n], (dx, dy, 0)) for n, (dx, dy, _) in enumerate(X6)]
    wait(e2)
    slot24 = lane24 // 16
    for x in range(4, 20):
        g = (x - 4) // 4
        merged = jnp.where(slot24 % 2 == 1, ZR1[0, g], ZR1[1, g])
        halo = roll(merged, -32 * (x % 4))
        S1[x] = jnp.where((lane24 >= 32) & (lane24 < 96), S1[x], halo)
    PS[1, pl.ds(8, 8), pl.ds(8, 8)] = S1[pl.ds(8, 8), pl.ds(8, 8)]

    def rhs1(source, lo, hi):
        def body(i, carry):
            even, odd = source[2 * i], source[2 * i + 1]
            m = mask1[0][8:32] * x1(i + 1)
            FD1[0, 0, i] = jnp.where(q24, odd, even) * m
            FD1[0, 1, i] = jnp.where(q24, even, odd) * m
            return carry
        loop(lo, hi, body, 0, 4)

    rhs1(S1, 2, 10)
    for i in range(2, 10):
        V1[0, 0, i + 1, pl.ds(8, 24), :] = FD1[0, 0, i]
    sweeps(V1, A1, FD1, 1, 8, 2, 10, first=1)
    sums = []
    for i in range(4, 8):
        red, black = residual_pair(V1, A1, FD1, DG1, 1, i, 8)
        sums.append((red + black)[8:16])
    GS[mine, gx] = restrict_two(jnp.stack(sums))
    gs1 = [send(GS.at[mine, gx], GS.at[mine, gx], s_gs1.at[n], r_gs1.at[n], o) for n, o in enumerate(RING7)]

    wait(gc3)
    gc4 = []
    for n in range(4):
        rows = GC.at[pl.ds((core + 2 * n) * 4, 4)]
        gc4.append(send(rows, rows, s_gc4.at[n], r_gc4.at[n]))
    for i in range(4, 8):
        red, black = V1[0, 0, i + 1, pl.ds(16, 8), :], V1[0, 1, i + 1, pl.ds(16, 8), :]
        PS[0, 2 * i, pl.ds(8, 8)], PS[0, 2 * i + 1, pl.ds(8, 8)] = unpack(red, black, q8)
    wait(uz)
    for x in range(16):
        merged = jnp.where(lane16 % 16 < 8, ZU[0, x // 8], ZU[1, x // 8])
        EU[1, 6 + x, pl.ds(8, 16)] = roll(merged, -(16 * (x % 8) + 8))
    wait(gs1)
    gs2 = [send(GS.at[mine], GS.at[mine], s_gs2.at[n], r_gs2.at[n], o) for n, o in enumerate(SAME15)]
    gs3 = [send(GS.at[mine], GS.at[mine], s_gs3.at[15], r_gs3.at[15])]
    ps = [send(PS.at[:, source_span(dx, 8, 8, 8), source_span(dy, 8, 8, 8)],
               PS.at[:, target_span(dx, 8, 8, 8), target_span(dy, 8, 8, 8)],
               s_ps.at[n], r_ps.at[n], (dx, dy, 0)) for n, (dx, dy, _) in enumerate(XY8)]

    lane_group = lane8 // 32

    def spread(load, store):
        def body(g, carry):
            for pair in range(4):
                blocks = [jnp.concatenate([load(8 * pair + k, g), load(8 * pair + 4 + k, g)], axis=0)
                          for k in range(4)]
                for x in range(4):
                    total = roll(blocks[0], -32 * x)
                    for k in range(1, 4):
                        total = jnp.where(lane_group == k, roll(blocks[k], 32 * (k - x)), total)
                    store(4 * g + x, 8 * pair, total)
            return carry
        loop(0, 8, body, 0, 2)

    def store_s2(x, y, v):
        S2[x, pl.ds(y, 8), :] = v

    def store_b2(x, y, v):
        B2[x + 4, pl.ds(y + 8, 8), :] = v

    def store_source(x, y, v):
        PD[x + 4, pl.ds(y + 8, 8), :] = v
        RM[x, pl.ds(y, 8), :] = v

    wait(gc4)
    spread(lambda j, g: GC[j, g, 0], store_s2)
    spread(lambda j, g: GC[j, g, 1], store_b2)

    def shifts(O, x):
        centre = O[x + 4, pl.ds(8, 32), :]
        return (centre, (O[x + 5, pl.ds(8, 32), :], O[x + 3, pl.ds(8, 32), :], O[x + 4, pl.ds(9, 32), :],
                         O[x + 4, pl.ds(7, 32), :], roll(centre, -1), roll(centre, 1)))

    def weights2(x, carry):
        b, near = shifts(B2, x)
        total = S2[x]
        for k, v in enumerate(near):
            if k == 4:
                v = jnp.where(lane32 == 127, 0.0, v)
            if k == 5:
                v = jnp.where(lane32 == 0, 0.0, v)
            w = (0.5 * 0.0625) * (b + v)
            total = total + w
            if k == 4:
                w = jnp.where(lane32 == 127, 0.0, w)
            if k == 5:
                w = jnp.where(lane32 == 0, 0.0, w)
            A2[k, x] = w
        DG2[x] = total
        return carry

    loop(0, 32, weights2, 0, 4)

    wait(c1b)
    coefficients1(0, 12)

    for n, (_, j, k) in enumerate(SAME15):
        gs2[n].wait()
        came = GS.at[lax.rem(gy + 8 - j, 8) * 4 + lax.rem(gz + 4 - k, 4)]
        gs3.append(send(came, came, s_gs3.at[n], r_gs3.at[n]))
    wait(gs3)
    eu = [send(EU.at[:, source_span(dx, 6, 16, 5), source_span(dy, 8, 16, 8)],
               EU.at[:, target_span(dx, 6, 16, 5), target_span(dy, 8, 16, 8)],
               s_u.at[n], r_u.at[n], (dx, dy, 0)) for n, (dx, dy, _) in enumerate(XY8)]
    spread(lambda j, g: GS[j, g], store_source)
    XL[...] = jnp.zeros_like(XL)

    def whole(total):
        return jnp.sum(jnp.sum(total, axis=0, keepdims=True), axis=1, keepdims=True)

    def square(x, total):
        return total + RM[x] * RM[x]

    acc = jnp.zeros((32, 128), F32)
    rr = whole(loop(0, 32, square, acc, 8))
    for step in range(CG_ITERS):
        def image(x, total):
            p, near = shifts(PD, x)
            value = DG2[x] * p
            for k, v in enumerate(near):
                value = value - A2[k, x] * v
            AP[x] = value
            return total + p * value

        alpha = rr / whole(loop(0, 32, image, acc, 8))

        def gain(x, carry):
            XL[x] = XL[x] + alpha * PD[4 * gx + x, pl.ds(4 * gy + 4, 16), :]
            return carry

        loop(0, 12, gain, 0, 12)
        if step < CG_ITERS - 1:
            def update(x, total):
                value = RM[x] - alpha * AP[x]
                RM[x] = value
                return total + value * value

            new = whole(loop(0, 32, update, acc, 8))
            ratio = new / rr

            def turn(x, carry):
                PD[x + 4, pl.ds(8, 32), :] = RM[x] + ratio * PD[x + 4, pl.ds(8, 32), :]
                return carry

            loop(0, 32, turn, 0, 8)
            rr = new

    wait(ps)

    def pack1_post(p, carry):
        m = mask1[0][8:32] * x1(p)
        even, odd = PS[0, 2 * p - 2], PS[0, 2 * p - 1]
        V1[0, 0, p, pl.ds(8, 24), :] = jnp.where(q24, odd, even) * m
        V1[0, 1, p, pl.ds(8, 24), :] = jnp.where(q24, even, odd) * m
        return carry

    loop(1, 13, pack1_post, 0, 4)
    rhs1(PS.at[1], 0, 12)

    wait(eu)

    def pack0_post(p, carry):
        xs = x0(p)
        for t in range(2):
            m = mask0[t] * xs
            even, odd = EU[t, 2 * p], EU[t, 2 * p + 1]
            V0[t, 0, p] = jnp.where(q32, odd, even) * m
            V0[t, 1, p] = jnp.where(q32, even, odd) * m
        return carry

    loop(0, 14, pack0_post, 0, 2)

    fine = pick(XL[...].reshape(192, 128), from_two).reshape(12, 16, 128)
    X16[:, pl.ds(0, 16, stride=2), :] = fine
    X16[:, pl.ds(1, 16, stride=2), :] = fine

    def correct1(i, carry):
        for c in range(2):
            V1[0, c, i + 1, pl.ds(8, 24), :] = V1[0, c, i + 1, pl.ds(8, 24), :] + X16[i, 0:24]
        return carry

    loop(0, 12, correct1, 0, 4)
    sweeps(V1, A1, FD1, 1, 8)

    planes = []
    for p in range(14):
        k = (p + 7) // 2
        red, black = V1[0, 0, k, pl.ds(12, 16), :], V1[0, 1, k, pl.ds(12, 16), :]
        planes.append(unpack(red, black, q16)[0 if p % 2 else 1])
    coarse = jnp.stack(planes).reshape(224, 128)
    for t, matrix in enumerate((from_one, from_one_edge)):
        fine = pick(coarse, matrix).reshape(14, 16, 128)
        XB[:, pl.ds(0, 16, stride=2), :] = fine
        XB[:, pl.ds(1, 16, stride=2), :] = fine

        def correct0(p, carry):
            for c in range(2):
                V0[t, c, p] = V0[t, c, p] + XB[p]
            return carry

        loop(0, 14, correct0, 0, 2)
    sweeps(V0, A0, FD0, 2, 4)

    def finish(i, carry):
        red, black = residual_pair(V0, A0, FD0, DG0, 2, i, 4)
        even, odd = unpack(red, black, q24)
        r_out[2 * i - 4] = even[4:20]
        r_out[2 * i - 3] = odd[4:20]
        even, odd = unpack(V0[0, 0, i + 1, pl.ds(8, 16), :], V0[0, 1, i + 1, pl.ds(8, 16), :], q16)
        x_out[2 * i - 4] = even
        x_out[2 * i - 3] = odd
        return carry

    loop(2, 10, finish, 0, 2)


def vmem(*shape):
    return pltpu.VMEM(shape, F32)


def dma(*shape):
    return pltpu.SemaphoreType.DMA(shape)


SCRATCH = [
    vmem(4, 28, 32, 128), vmem(8, 16, 128), vmem(2, 12, 32, 128),
    vmem(2, 2, 14, 32, 128), vmem(2, 2, 14, 32, 128), vmem(2, 2, 6, 12, 24, 128),
    vmem(2, 2, 12, 24, 128), vmem(2, 2, 12, 24, 128), vmem(2, 2, 12, 24, 128),
    vmem(2, 24, 24, 128), vmem(2, 8, 8, 128), vmem(2, 2, 8, 8, 128),
    vmem(24, 24, 128), vmem(2, 8, 128), vmem(2, 4, 24, 128), vmem(2, 24, 24, 128),
    vmem(1, 2, 14, 40, 128), vmem(1, 2, 14, 40, 128), vmem(1, 2, 6, 12, 24, 128),
    vmem(1, 2, 12, 24, 128), vmem(1, 2, 12, 24, 128), vmem(1, 2, 12, 24, 128),
    vmem(2, 28, 32, 128), vmem(2, 16, 128), vmem(2, 2, 16, 128),
    vmem(8, 16, 128), vmem(4, 8, 128), vmem(4, 8, 128), vmem(12, 32, 128), vmem(14, 32, 128),
    vmem(32, 8, 2, 4, 128), vmem(32, 8, 4, 128),
    vmem(32, 32, 128), vmem(40, 48, 128), vmem(6, 32, 32, 128), vmem(32, 32, 128),
    vmem(40, 48, 128), vmem(32, 32, 128), vmem(32, 32, 128), vmem(12, 16, 128),
    dma(4), dma(26), dma(26), dma(2), dma(2), dma(8), dma(8), dma(26), dma(26), dma(2), dma(2), dma(8), dma(8),
    dma(8), dma(8), dma(7), dma(7), dma(3), dma(3), dma(7), dma(7), dma(15), dma(15),
    dma(3), dma(3), dma(4), dma(4), dma(16), dma(16), dma(6), dma(6),
]


def solution(mesh):
    def local(right_side, initial, shift, beta):
        shape = jax.ShapeDtypeStruct(right_side.shape, F32)
        return pl.pallas_call(
            kernel,
            out_shape=(shape, shape),
            in_specs=[pl.BlockSpec(memory_space=pl.ANY)] * 4,
            out_specs=(pl.BlockSpec(memory_space=pltpu.VMEM),) * 2,
            scratch_shapes=SCRATCH,
            compiler_params=pltpu.CompilerParams(
                collective_id=0, has_side_effects=True, vmem_limit_bytes=56 * 2**20),
        )(right_side, initial, shift, beta)

    spec = P(*AXES)
    return jax.shard_map(local, mesh=mesh, in_specs=(spec,) * 4, out_specs=(spec, spec), check_vma=False)
```

```python
import itertools

import jax
import jax.numpy as jnp
from jax import lax
from jax.experimental import pallas as pl
from jax.experimental.pallas import tpu as pltpu
from jax.sharding import PartitionSpec as P

CG_ITERS = 8
MESH = pl.DeviceIdType.MESH
AXES = ("gx", "gy", "gz")
SIZES = (8, 8, 4)
F32 = jnp.float32
BF16 = jnp.bfloat16

ALL26 = sorted((o for o in itertools.product((-1, 0, 1), repeat=3) if o != (0, 0, 0)),
               key=lambda o: -sum(map(abs, o)))
XY8 = [o for o in ALL26 if o[2] == 0]
XY4 = [o for o in XY8 if o[0] * o[1] == 0]
CORNERS = [o for o in XY8 if o[0] * o[1] != 0]
X6 = [o for o in XY8 if o[0] != 0]
RING7 = [(k, 0, 0) for k in range(1, 8)]
ROW3 = [(0, 0, k) for k in range(1, 4)]
CHIPS3 = [(0, j, 0) for j in (2, 4, 6)]
SAME15 = sorted(((0, j, k) for j in (0, 2, 4, 6) for k in range(4) if (j, k) != (0, 0)),
                key=lambda o: min(o[1], 8 - o[1]) // 2 + min(o[2], 4 - o[2]))


def canonical(offset):
    return tuple(o % n for o, n in zip(offset, SIZES))


PARTNERS = sorted({canonical(o) for o in ALL26 + RING7 + [(0, 4, 0)]})


def source_span(d, start, count, halo):
    if d == 0:
        return pl.ds(start, count)
    return pl.ds(start + count - halo, halo) if d > 0 else pl.ds(start, halo)


def target_span(d, start, count, halo):
    if d == 0:
        return pl.ds(start, count)
    return pl.ds(start - halo, halo) if d > 0 else pl.ds(start + count, halo)


def iota(shape, dim):
    return lax.broadcasted_iota(jnp.int32, shape, dim)


def loop(lo, hi, body, init, unroll):
    def chunk(k, carry):
        for j in range(unroll):
            carry = body(lo + k * unroll + j, carry)
        return carry

    return lax.fori_loop(0, (hi - lo) // unroll, chunk, init)


def pick(values, matrix):
    high = values.astype(BF16)
    rest = values - high.astype(F32)
    middle = rest.astype(BF16)
    low = (rest - middle.astype(F32)).astype(BF16)
    out = jnp.dot(low, matrix, preferred_element_type=F32)
    out = out + jnp.dot(middle, matrix, preferred_element_type=F32)
    return out + jnp.dot(high, matrix, preferred_element_type=F32)


def roll(value, shift):
    shift = shift % 128
    return value if shift == 0 else pltpu.roll(value, shift, 1)


def kernel(f_in, u_in, s_in, b_in, x_out, r_out, E0, M0, MX, RZ0, CP, CR, V0, PB0, A0, D0, DG0, FD0,
           C1, R1s, RZ1, S1, M1, ZR1, PS, V1, PB1, A1, D1, DG1, FD1,
           EU, MU, ZU, T16, T8, T4, X16, XB, GC, GS, S2, B2, A2, DG2, PD, RM, AP, XL,
           sem_in, s_e0, r_e0, s_c1z, r_c1z, s_c1, r_c1, s_e2, r_e2, s_uz, r_uz, s_u, r_u,
           s_ps, r_ps, s_gc1, r_gc1, s_gc2, r_gc2, s_gs1, r_gs1, s_gs2, r_gs2,
           s_gc3, r_gc3, s_gc4, r_gc4, s_gs3, r_gs3, s_c1b, r_c1b,
           s_z0, r_z0, s_mx, r_mx):
    gx, gy, gz = (lax.axis_index(a) for a in AXES)
    me = (gx, gy, gz)
    core = lax.rem(gy, 2)
    twin = (gx, gy + 1 - 2 * core, gz)

    def device(offset):
        return tuple(lax.rem(m + (o % n), n) if o % n else m for m, o, n in zip(me, offset, SIZES))

    def send(src, dst, ssem, rsem, offset=None):
        copy = pltpu.make_async_remote_copy(src_ref=src, dst_ref=dst, send_sem=ssem, recv_sem=rsem,
                                            device_id=twin if offset is None else device(offset),
                                            device_id_type=MESH)
        copy.start()
        return copy

    def wait(copies):
        for copy in copies:
            copy.wait()

    local = [pltpu.make_async_copy(src, E0.at[k, pl.ds(6, 16), pl.ds(8, 16)], sem_in.at[k])
             for k, src in enumerate((f_in, s_in, u_in, b_in))]
    for copy in local:
        copy.start()
    barrier = pltpu.get_barrier_semaphore()
    for offset in PARTNERS:
        pl.semaphore_signal(barrier, inc=1, device_id=device(offset), device_id_type=MESH)

    q24 = (iota((24, 128), 0) + iota((24, 128), 1)) % 2 == 1
    q32 = (iota((32, 128), 0) + iota((32, 128), 1)) % 2 == 1
    q16 = (iota((16, 128), 0) + iota((16, 128), 1)) % 2 == 1
    lane24 = iota((24, 128), 1)
    one, zero = jnp.float32(1.0), jnp.float32(0.0)

    def y_mask(rows, own_start, own_count):
        row = iota((rows, 128), 0)
        low = jnp.where(gy == 0, zero, one)
        high = jnp.where(gy == 7, zero, one)
        return jnp.where(row < own_start, low, jnp.where(row >= own_start + own_count, high, one))

    def z_mask(rows, low_at, high_at):
        lane = iota((rows, 128), 1)
        low = jnp.where(gz == 0, zero, one)
        high = jnp.where(gz == 3, zero, one)
        return jnp.where(low_at(lane), low, jnp.where(high_at(lane), high, one))

    y32 = y_mask(32, 8, 16)
    mask0 = (y32, y32 * z_mask(32, lambda l: l >= 64, lambda l: l < 64))
    mask1 = (y_mask(40, 16, 8) * z_mask(40, lambda l: l < 32, lambda l: l >= 96),)

    def x_scalar(p, low_end, high_start):
        outside = ((gx == 0) & (p < low_end)) | ((gx == 7) & (p >= high_start))
        return jnp.where(outside, zero, one)

    row, col = iota((128, 128), 0), iota((128, 128), 1)
    to_one = jnp.where((col >= 32) & (col < 96) & (col - 32 == row // 2), 0.125, 0.0).astype(BF16)
    to_two = jnp.where((row >= 32) & (row < 96) & (col == (row - 32) // 2), 0.125, 0.0).astype(BF16)
    from_two = jnp.where((col - 32 + 64 * gz + 128) // 2 - 64 == row, 1.0, 0.0).astype(BF16)
    from_one = jnp.where(row - 32 == col // 2, 1.0, 0.0).astype(BF16)
    from_one_edge = jnp.where(
        ((col < 64) & (row == 96 + col // 2)) | ((col >= 64) & (row == col // 2 - 32)), 1.0, 0.0
    ).astype(BF16)

    def restrict_one(sums):
        T16[...] = sums
        folded = T16[:, pl.ds(0, 8, stride=2), :] + T16[:, pl.ds(1, 8, stride=2), :]
        return pick(folded.reshape(64, 128), to_one).reshape(8, 8, 128)

    def restrict_two(sums):
        T8[...] = sums
        total = None
        for x in range(4):
            folded = T8[x, pl.ds(0, 4, stride=2), :] + T8[x, pl.ds(1, 4, stride=2), :]
            T4[x, 0:4] = folded
        full = pick(T4[...].reshape(32, 128), to_two).reshape(4, 8, 128)
        for x in range(4):
            term = roll(full[x], 32 * x)
            total = term if total is None else total + term
        return total[0:4]

    for copy in local:
        copy.wait()
    pl.semaphore_wait(barrier, len(PARTNERS))
    e0 = [send(E0.at[:, source_span(dx, 6, 16, 5), source_span(dy, 8, 16, 8)],
               E0.at[:, target_span(dx, 6, 16, 5), target_span(dy, 8, 16, 8)],
               s_e0.at[n], r_e0.at[n], (dx, dy, 0)) for n, (dx, dy, _) in enumerate(XY4)]

    upper = iota((8, 128), 0) < 4
    for n, (dx, dy, _) in enumerate(CORNERS):
        x, y = (18 if dx > 0 else 6), (16 if dy > 0 else 8)
        for a in range(4):
            for k in range(2):
                first, second = E0[a, x + 2 * k, pl.ds(y, 8), :], E0[a, x + 2 * k + 1, pl.ds(y, 8), :]
                if dy > 0:
                    first = pltpu.roll(first, 4, 0)
                else:
                    second = pltpu.roll(second, 4, 0)
                CP[n, a, k] = jnp.where(upper, first, second)
        e0.append(send(CP.at[n], CR.at[n], s_e0.at[4 + n], r_e0.at[4 + n], (dx, dy, 0)))

    lane16 = iota((16, 128), 1)
    group = lane16 // 16

    def pack_rows(k, carry):
        total = jnp.zeros((16, 128), F32)
        for odd in range(2):
            for a in range(4):
                value = E0[a, 6 + 2 * k + odd, pl.ds(8, 16), :]
                total = jnp.where(group == 4 * odd + a, roll(value, 8 + 16 * a + 64 * odd), total)
        M0[k] = total
        return carry

    loop(0, 8, pack_rows, 0, 4)
    z0 = [send(M0, RZ0.at[n], s_z0.at[n], r_z0.at[n], (0, 0, 1 if n == 0 else -1)) for n in range(2)]

    PD[...] = jnp.zeros_like(PD)
    B2[...] = jnp.zeros_like(B2)
    V1[...] = jnp.zeros_like(V1)
    PB1[...] = jnp.zeros_like(PB1)

    for k, a in ((0, 1), (1, 3)):
        sums = jnp.stack([E0[a, 6 + 2 * x, pl.ds(8, 16), :] + E0[a, 7 + 2 * x, pl.ds(8, 16), :] for x in range(8)])
        C1[k, pl.ds(8, 8), pl.ds(8, 8)] = restrict_one(sums)
        for x in range(8):
            R1s[k, x] = roll(C1[k, 8 + x, pl.ds(8, 8), :], 64)
    c1z = [send(R1s, RZ1.at[n], s_c1z.at[n], r_c1z.at[n], (0, 0, 1 if n == 0 else -1)) for n in range(2)]
    mine = gy * 4 + gz
    for k in range(2):
        sums = jnp.stack([C1[k, 8 + 2 * x, pl.ds(8, 8), :] + C1[k, 9 + 2 * x, pl.ds(8, 8), :] for x in range(4)])
        GC[mine, gx, k] = restrict_two(sums)
    gc1 = [send(GC.at[mine, gx], GC.at[mine, gx], s_gc1.at[n], r_gc1.at[n], o) for n, o in enumerate(RING7)]
    wait(z0)
    for k in range(8):
        MX[2 + k, pl.ds(8, 16)] = jnp.where(lane16 % 16 < 8, RZ0[0, k], RZ0[1, k])
    mx = [send(MX.at[source_span(dx, 2, 8, 2), source_span(dy, 8, 16, 8)],
               MX.at[target_span(dx, 2, 8, 2), target_span(dy, 8, 16, 8)],
               s_mx.at[n], r_mx.at[n], (dx, dy, 0)) for n, (dx, dy, _) in enumerate(XY8)]
    wait(c1z)
    lane8 = iota((8, 128), 1)
    for k in range(2):
        for x in range(8):
            own = C1[k, 8 + x, pl.ds(8, 8), :]
            C1[k, 8 + x, pl.ds(8, 8), :] = jnp.where(
                lane8 < 32, RZ1[0, k, x], jnp.where(lane8 < 96, own, RZ1[1, k, x]))
    c1 = [send(C1.at[:, source_span(dx, 8, 8, 4), source_span(dy, 8, 8, 8)],
               C1.at[:, target_span(dx, 8, 8, 4), target_span(dy, 8, 8, 8)],
               s_c1.at[n], r_c1.at[n], (dx, dy, 0)) for n, (dx, dy, _) in enumerate(XY8)]
    def around(O, tiles, c, i, r0, q):
        out = []
        centre = [O[t, 1 - c, i + 1, pl.ds(r0, 24), :] for t in range(tiles)]
        ups = [roll(v, -1) for v in centre]
        downs = [roll(v, 1) for v in centre]
        for t in range(tiles):
            low = O[t, 1 - c, i, pl.ds(r0, 24), :]
            high = O[t, 1 - c, i + 2, pl.ds(r0, 24), :]
            other = jnp.where(q, high, low) if c == 0 else jnp.where(q, low, high)
            yp = O[t, 1 - c, i + 1, pl.ds(r0 + 1, 24), :]
            ym = O[t, 1 - c, i + 1, pl.ds(r0 - 1, 24), :]
            if tiles == 2:
                zp = jnp.where(lane24 == 127, ups[1 - t], ups[t])
                zm = jnp.where(lane24 == 0, downs[1 - t], downs[t])
            else:
                zp, zm = ups[0], downs[0]
            out.append((centre[t], other, yp, ym, zp, zm))
        return out

    def coefficients(PB, A, D, DG, tiles, r0, scale, shift_of, mask, x_of, lo=0, hi=12):
        for c in range(2):
            def body(i, carry):
                near = around(PB, tiles, c, i, r0, q24)
                for t in range(tiles):
                    b = PB[t, c, i + 1, pl.ds(r0, 24), :]
                    total = shift_of(t, c, i)
                    weights = [(0.5 * scale) * (b + v) for v in near[t]]
                    for w in weights:
                        total = total + w
                    inverse = (1.0 / total) * (mask[t][r0:r0 + 24] * x_of(i + 1))
                    DG[t, c, i] = total
                    D[t, c, i] = inverse
                    for k, w in enumerate(weights):
                        A[t, c, k, i] = w * inverse
                return carry
            loop(lo, hi, body, 0, 2)

    def relaxed(V, A, FD, tiles, c, i, r0):
        near = around(V, tiles, c, i, r0, q24)
        out = []
        for t in range(tiles):
            total = FD[t, c, i]
            for k, v in enumerate(near[t]):
                total = total + A[t, c, k, i] * v
            out.append(total)
        return out

    def half(V, A, FD, tiles, c, r0, lo, hi):
        unroll = 4 if tiles == 1 else 4

        def body(k, carry):
            first = lo + k * unroll
            news = [relaxed(V, A, FD, tiles, c, first + j, r0) for j in range(unroll)]
            for j, new in enumerate(news):
                for t in range(tiles):
                    V[t, c, first + j + 1, pl.ds(r0, 24), :] = new[t]
            return carry
        lax.fori_loop(0, (hi - lo) // unroll, body, 0)

    def sweeps(V, A, FD, tiles, r0, lo=0, hi=12, first=0):
        for step in range(first, 4):
            half(V, A, FD, tiles, step % 2, r0, lo, hi)

    def residual_pair(V, A, FD, DG, tiles, i, r0):
        out = []
        for c in range(2):
            new = relaxed(V, A, FD, tiles, c, i, r0)[0]
            out.append(DG[0, c, i] * (new - V[0, c, i + 1, pl.ds(r0, 24), :]))
        return out

    def unpack(red, black, q):
        return jnp.where(q, black, red), jnp.where(q, red, black)

    wait(e0)
    for n, (dx, dy, _) in enumerate(CORNERS):
        x, y = (2 if dx > 0 else 22), (4 if dy > 0 else 24)
        for a in range(4):
            for k in range(4):
                E0[a, x + k, pl.ds(y, 4), :] = CR[n, a, k // 2, pl.ds(4 * (k % 2), 4), :]
    wait(mx)

    lane32 = iota((32, 128), 1)

    def edge_of(a, p):
        merged = MX[p - 1]
        return roll(merged, -(16 * a + 8)), roll(merged, -(16 * a + 72))

    x0 = lambda p: x_scalar(p, 3, 11)
    x1 = lambda p: x_scalar(p, 5, 9)

    def pack0(p, carry):
        xs = x0(p)
        for dst, a in ((V0, 2), (PB0, 3)):
            even, odd = E0[a, 2 * p], E0[a, 2 * p + 1]
            m = mask0[0] * xs
            dst[0, 0, p] = jnp.where(q32, odd, even) * m
            dst[0, 1, p] = jnp.where(q32, even, odd) * m
        return carry

    loop(0, 14, pack0, 0, 2)
    for p in (0, 13):
        for dst in (V0, PB0):
            for c in range(2):
                dst[1, c, p] = jnp.zeros((32, 128), F32)

    def pack0_edge(p, carry):
        xs = x0(p)
        for dst, a in ((V0, 2), (PB0, 3)):
            even, odd = edge_of(a, p)
            m = mask0[1] * xs
            dst[1, 0, p] = jnp.where(q32, odd, even) * m
            dst[1, 1, p] = jnp.where(q32, even, odd) * m
        for dst, a in ((FD0, 0), (DG0, 1)):
            even, odd = edge_of(a, p)
            dst[1, 0, p - 1] = jnp.where(q32, odd, even)[4:28]
            dst[1, 1, p - 1] = jnp.where(q32, even, odd)[4:28]
            even, odd = E0[a, 2 * p, pl.ds(4, 24), :], E0[a, 2 * p + 1, pl.ds(4, 24), :]
            dst[0, 0, p - 1] = jnp.where(q24, odd, even)
            dst[0, 1, p - 1] = jnp.where(q24, even, odd)
        return carry

    loop(1, 13, pack0_edge, 0, 2)
    coefficients(PB0, A0, D0, DG0, 2, 4, 1.0, lambda t, c, i: DG0[t, c, i], mask0, x0)

    def scale_rhs0(i, carry):
        for t in range(2):
            for c in range(2):
                FD0[t, c, i] = FD0[t, c, i] * D0[t, c, i]
        return carry

    loop(0, 12, scale_rhs0, 0, 4)
    wait(gc1)
    gc2 = [send(GC.at[mine], GC.at[mine], s_gc2.at[n], r_gc2.at[n], o) for n, o in enumerate(ROW3)]
    sweeps(V0, A0, FD0, 2, 4)

    sums = []
    for i in range(2, 10):
        red, black = residual_pair(V0, A0, FD0, DG0, 2, i, 4)
        sums.append((red + black)[4:20])
    own = restrict_one(jnp.stack(sums))
    wait(c1)

    def pack1(p, carry):
        xs = x1(p)
        m = mask1[0][8:32] * xs
        even, odd = C1[1, 2 * p - 2], C1[1, 2 * p - 1]
        PB1[0, 0, p, pl.ds(8, 24), :] = jnp.where(q24, odd, even) * m
        PB1[0, 1, p, pl.ds(8, 24), :] = jnp.where(q24, even, odd) * m
        even, odd = C1[0, 2 * p - 2], C1[0, 2 * p - 1]
        DG1[0, 0, p - 1] = jnp.where(q24, odd, even)
        DG1[0, 1, p - 1] = jnp.where(q24, even, odd)
        return carry

    def coefficients1(lo, hi):
        loop(lo + 1, hi + 1, pack1, 0, 4)
        coefficients(PB1, A1, D1, DG1, 1, 8, 0.25, lambda t, c, i: DG1[t, c, i], mask1, x1, lo, hi)

    coefficients1(2, 10)
    q8 = (iota((8, 128), 0) + iota((8, 128), 1)) % 2 == 1
    for i in range(4, 8):
        even, odd = own[2 * i - 8], own[2 * i - 7]
        red = jnp.where(q8, odd, even) * D1[0, 0, i, pl.ds(8, 8), :]
        black = jnp.where(q8, even, odd) * D1[0, 1, i, pl.ds(8, 8), :]
        S1[2 * i, pl.ds(8, 8)], S1[2 * i + 1, pl.ds(8, 8)] = unpack(red, black, q8)
    slot = iota((8, 128), 1) // 16
    for g in range(2):
        total = jnp.zeros((8, 128), F32)
        for k in range(4):
            value = roll(S1[8 + 4 * g + k, pl.ds(8, 8), :], 64 + 32 * k)
            total = jnp.where((slot == 1 + 2 * k) | (slot == (6 + 2 * k) % 8), value, total)
        M1[g] = total
    e2 = []
    for n, (dx, dy, dz) in enumerate(ALL26):
        if dz == 0:
            e2.append(send(S1.at[source_span(dx, 8, 8, 4), source_span(dy, 8, 8, 8)],
                           S1.at[target_span(dx, 8, 8, 4), target_span(dy, 8, 8, 8)],
                           s_e2.at[n], r_e2.at[n], (dx, dy, dz)))
        else:
            side = 0 if dz > 0 else 1
            e2.append(send(M1.at[source_span(dx, 0, 2, 1), source_span(dy, 0, 8, 8)],
                           ZR1.at[side, target_span(dx, 1, 2, 1), target_span(dy, 8, 8, 8)],
                           s_e2.at[n], r_e2.at[n], (dx, dy, dz)))

    for i in range(2, 10):
        red, black = V0[0, 0, i + 1, pl.ds(8, 16), :], V0[0, 1, i + 1, pl.ds(8, 16), :]
        EU[0, 2 * i + 2, pl.ds(8, 16)], EU[0, 2 * i + 3, pl.ds(8, 16)] = unpack(red, black, q16)
    for g in range(2):
        total = jnp.zeros((16, 128), F32)
        for k in range(8):
            total = jnp.where(group == k, roll(EU[0, 6 + 8 * g + k, pl.ds(8, 16), :], 8 + 16 * k), total)
        MU[g] = total
    uz = [send(MU, ZU.at[n], s_uz.at[n], r_uz.at[n], (0, 0, 1 if n == 0 else -1)) for n in range(2)]

    wait(gc2)
    row_of = GC.at[pl.ds(gy * 4, 4)]
    gc3 = [send(row_of, row_of, s_gc3.at[n], r_gc3.at[n], o) for n, o in enumerate(CHIPS3)]
    c1b = [send(C1.at[:, source_span(-dx, 8, 8, 4), source_span(dy, 8, 8, 8)],
                C1.at[:, pl.ds(0 if dx > 0 else 20, 4), target_span(dy, 8, 8, 8)],
                s_c1b.at[n], r_c1b.at[n], (dx, dy, 0)) for n, (dx, dy, _) in enumerate(X6)]
    wait(e2)
    slot24 = lane24 // 16
    for x in range(4, 20):
        g = (x - 4) // 4
        merged = jnp.where(slot24 % 2 == 1, ZR1[0, g], ZR1[1, g])
        halo = roll(merged, -32 * (x % 4))
        S1[x] = jnp.where((lane24 >= 32) & (lane24 < 96), S1[x], halo)
    PS[1, pl.ds(8, 8), pl.ds(8, 8)] = S1[pl.ds(8, 8), pl.ds(8, 8)]

    def rhs1(source, lo, hi):
        def body(i, carry):
            even, odd = source[2 * i], source[2 * i + 1]
            m = mask1[0][8:32] * x1(i + 1)
            FD1[0, 0, i] = jnp.where(q24, odd, even) * m
            FD1[0, 1, i] = jnp.where(q24, even, odd) * m
            return carry
        loop(lo, hi, body, 0, 4)

    rhs1(S1, 2, 10)
    for i in range(2, 10):
        V1[0, 0, i + 1, pl.ds(8, 24), :] = FD1[0, 0, i]
    sweeps(V1, A1, FD1, 1, 8, 2, 10, first=1)
    sums = []
    for i in range(4, 8):
        red, black = residual_pair(V1, A1, FD1, DG1, 1, i, 8)
        sums.append((red + black)[8:16])
    GS[mine, gx] = restrict_two(jnp.stack(sums))
    gs1 = [send(GS.at[mine, gx], GS.at[mine, gx], s_gs1.at[n], r_gs1.at[n], o) for n, o in enumerate(RING7)]

    wait(gc3)
    gc4 = []
    for n in range(4):
        rows = GC.at[pl.ds((core + 2 * n) * 4, 4)]
        gc4.append(send(rows, rows, s_gc4.at[n], r_gc4.at[n]))
    for i in range(4, 8):
        red, black = V1[0, 0, i + 1, pl.ds(16, 8), :], V1[0, 1, i + 1, pl.ds(16, 8), :]
        PS[0, 2 * i, pl.ds(8, 8)], PS[0, 2 * i + 1, pl.ds(8, 8)] = unpack(red, black, q8)
    wait(uz)
    for x in range(16):
        merged = jnp.where(lane16 % 16 < 8, ZU[0, x // 8], ZU[1, x // 8])
        EU[1, 6 + x, pl.ds(8, 16)] = roll(merged, -(16 * (x % 8) + 8))
    wait(gs1)
    gs2 = [send(GS.at[mine], GS.at[mine], s_gs2.at[n], r_gs2.at[n], o) for n, o in enumerate(SAME15)]
    gs3 = [send(GS.at[mine], GS.at[mine], s_gs3.at[15], r_gs3.at[15])]
    ps = [send(PS.at[:, source_span(dx, 8, 8, 8), source_span(dy, 8, 8, 8)],
               PS.at[:, target_span(dx, 8, 8, 8), target_span(dy, 8, 8, 8)],
               s_ps.at[n], r_ps.at[n], (dx, dy, 0)) for n, (dx, dy, _) in enumerate(XY8)]

    lane_group = lane8 // 32

    def spread(load, store):
        def body(g, carry):
            for pair in range(4):
                blocks = [jnp.concatenate([load(8 * pair + k, g), load(8 * pair + 4 + k, g)], axis=0)
                          for k in range(4)]
                for x in range(4):
                    total = roll(blocks[0], -32 * x)
                    for k in range(1, 4):
                        total = jnp.where(lane_group == k, roll(blocks[k], 32 * (k - x)), total)
                    store(4 * g + x, 8 * pair, total)
            return carry
        loop(0, 8, body, 0, 2)

    def store_s2(x, y, v):
        S2[x, pl.ds(y, 8), :] = v

    def store_b2(x, y, v):
        B2[x + 4, pl.ds(y + 8, 8), :] = v

    def store_source(x, y, v):
        PD[x + 4, pl.ds(y + 8, 8), :] = v
        RM[x, pl.ds(y, 8), :] = v

    wait(gc4)
    spread(lambda j, g: GC[j, g, 0], store_s2)
    spread(lambda j, g: GC[j, g, 1], store_b2)

    def shifts(O, x):
        centre = O[x + 4, pl.ds(8, 32), :]
        return (centre, (O[x + 5, pl.ds(8, 32), :], O[x + 3, pl.ds(8, 32), :], O[x + 4, pl.ds(9, 32), :],
                         O[x + 4, pl.ds(7, 32), :], roll(centre, -1), roll(centre, 1)))

    def weights2(x, carry):
        b, near = shifts(B2, x)
        total = S2[x]
        for k, v in enumerate(near):
            if k == 4:
                v = jnp.where(lane32 == 127, 0.0, v)
            if k == 5:
                v = jnp.where(lane32 == 0, 0.0, v)
            w = (0.5 * 0.0625) * (b + v)
            total = total + w
            if k == 4:
                w = jnp.where(lane32 == 127, 0.0, w)
            if k == 5:
                w = jnp.where(lane32 == 0, 0.0, w)
            A2[k, x] = w
        DG2[x] = total
        return carry

    loop(0, 32, weights2, 0, 4)

    wait(c1b)
    coefficients1(0, 12)

    for n, (_, j, k) in enumerate(SAME15):
        gs2[n].wait()
        came = GS.at[lax.rem(gy + 8 - j, 8) * 4 + lax.rem(gz + 4 - k, 4)]
        gs3.append(send(came, came, s_gs3.at[n], r_gs3.at[n]))
    wait(gs3)
    eu = [send(EU.at[:, source_span(dx, 6, 16, 5), source_span(dy, 8, 16, 8)],
               EU.at[:, target_span(dx, 6, 16, 5), target_span(dy, 8, 16, 8)],
               s_u.at[n], r_u.at[n], (dx, dy, 0)) for n, (dx, dy, _) in enumerate(XY8)]
    spread(lambda j, g: GS[j, g], store_source)
    XL[...] = jnp.zeros_like(XL)

    def whole(total):
        return jnp.sum(jnp.sum(total, axis=0, keepdims=True), axis=1, keepdims=True)

    def square(x, total):
        return total + RM[x] * RM[x]

    acc = jnp.zeros((32, 128), F32)
    rr = whole(loop(0, 32, square, acc, 8))
    for step in range(CG_ITERS):
        def image(x, total):
            p, near = shifts(PD, x)
            value = DG2[x] * p
            for k, v in enumerate(near):
                value = value - A2[k, x] * v
            AP[x] = value
            return total + p * value

        alpha = rr / whole(loop(0, 32, image, acc, 16))

        def gain(x, carry):
            XL[x] = XL[x] + alpha * PD[4 * gx + x, pl.ds(4 * gy + 4, 16), :]
            return carry

        loop(0, 12, gain, 0, 12)
        if step < CG_ITERS - 1:
            def update(x, total):
                value = RM[x] - alpha * AP[x]
                RM[x] = value
                return total + value * value

            new = whole(loop(0, 32, update, acc, 16))
            ratio = new / rr

            def turn(x, carry):
                PD[x + 4, pl.ds(8, 32), :] = RM[x] + ratio * PD[x + 4, pl.ds(8, 32), :]
                return carry

            loop(0, 32, turn, 0, 16)
            rr = new

    wait(ps)

    def pack1_post(p, carry):
        m = mask1[0][8:32] * x1(p)
        even, odd = PS[0, 2 * p - 2], PS[0, 2 * p - 1]
        V1[0, 0, p, pl.ds(8, 24), :] = jnp.where(q24, odd, even) * m
        V1[0, 1, p, pl.ds(8, 24), :] = jnp.where(q24, even, odd) * m
        return carry

    loop(1, 13, pack1_post, 0, 4)
    rhs1(PS.at[1], 0, 12)

    wait(eu)

    def pack0_post(p, carry):
        xs = x0(p)
        for t in range(2):
            m = mask0[t] * xs
            even, odd = EU[t, 2 * p], EU[t, 2 * p + 1]
            V0[t, 0, p] = jnp.where(q32, odd, even) * m
            V0[t, 1, p] = jnp.where(q32, even, odd) * m
        return carry

    loop(0, 14, pack0_post, 0, 2)

    fine = pick(XL[...].reshape(192, 128), from_two).reshape(12, 16, 128)
    X16[:, pl.ds(0, 16, stride=2), :] = fine
    X16[:, pl.ds(1, 16, stride=2), :] = fine

    def correct1(i, carry):
        for c in range(2):
            V1[0, c, i + 1, pl.ds(8, 24), :] = V1[0, c, i + 1, pl.ds(8, 24), :] + X16[i, 0:24]
        return carry

    loop(0, 12, correct1, 0, 4)
    sweeps(V1, A1, FD1, 1, 8)

    planes = []
    for p in range(14):
        k = (p + 7) // 2
        red, black = V1[0, 0, k, pl.ds(12, 16), :], V1[0, 1, k, pl.ds(12, 16), :]
        planes.append(unpack(red, black, q16)[0 if p % 2 else 1])
    coarse = jnp.stack(planes).reshape(224, 128)
    for t, matrix in enumerate((from_one, from_one_edge)):
        fine = pick(coarse, matrix).reshape(14, 16, 128)
        XB[:, pl.ds(0, 16, stride=2), :] = fine
        XB[:, pl.ds(1, 16, stride=2), :] = fine

        def correct0(p, carry):
            for c in range(2):
                V0[t, c, p] = V0[t, c, p] + XB[p]
            return carry

        loop(0, 14, correct0, 0, 2)
    sweeps(V0, A0, FD0, 2, 4)

    def finish(i, carry):
        red, black = residual_pair(V0, A0, FD0, DG0, 2, i, 4)
        even, odd = unpack(red, black, q24)
        r_out[2 * i - 4] = even[4:20]
        r_out[2 * i - 3] = odd[4:20]
        even, odd = unpack(V0[0, 0, i + 1, pl.ds(8, 16), :], V0[0, 1, i + 1, pl.ds(8, 16), :], q16)
        x_out[2 * i - 4] = even
        x_out[2 * i - 3] = odd
        return carry

    loop(2, 10, finish, 0, 2)


def vmem(*shape):
    return pltpu.VMEM(shape, F32)


def dma(*shape):
    return pltpu.SemaphoreType.DMA(shape)


SCRATCH = [
    vmem(4, 28, 32, 128), vmem(8, 16, 128), vmem(12, 32, 128), vmem(2, 8, 16, 128),
    vmem(4, 4, 2, 8, 128), vmem(4, 4, 2, 8, 128),
    vmem(2, 2, 14, 32, 128), vmem(2, 2, 14, 32, 128), vmem(2, 2, 6, 12, 24, 128),
    vmem(2, 2, 12, 24, 128), vmem(2, 2, 12, 24, 128), vmem(2, 2, 12, 24, 128),
    vmem(2, 24, 24, 128), vmem(2, 8, 8, 128), vmem(2, 2, 8, 8, 128),
    vmem(24, 24, 128), vmem(2, 8, 128), vmem(2, 4, 24, 128), vmem(2, 24, 24, 128),
    vmem(1, 2, 14, 40, 128), vmem(1, 2, 14, 40, 128), vmem(1, 2, 6, 12, 24, 128),
    vmem(1, 2, 12, 24, 128), vmem(1, 2, 12, 24, 128), vmem(1, 2, 12, 24, 128),
    vmem(2, 28, 32, 128), vmem(2, 16, 128), vmem(2, 2, 16, 128),
    vmem(8, 16, 128), vmem(4, 8, 128), vmem(4, 8, 128), vmem(12, 32, 128), vmem(14, 32, 128),
    vmem(32, 8, 2, 4, 128), vmem(32, 8, 4, 128),
    vmem(32, 32, 128), vmem(40, 48, 128), vmem(6, 32, 32, 128), vmem(32, 32, 128),
    vmem(40, 48, 128), vmem(32, 32, 128), vmem(32, 32, 128), vmem(12, 16, 128),
    dma(4), dma(8), dma(8), dma(2), dma(2), dma(8), dma(8), dma(26), dma(26), dma(2), dma(2), dma(8), dma(8),
    dma(8), dma(8), dma(7), dma(7), dma(3), dma(3), dma(7), dma(7), dma(15), dma(15),
    dma(3), dma(3), dma(4), dma(4), dma(16), dma(16), dma(6), dma(6),
    dma(2), dma(2), dma(8), dma(8),
]


def solution(mesh):
    def local(right_side, initial, shift, beta):
        shape = jax.ShapeDtypeStruct(right_side.shape, F32)
        return pl.pallas_call(
            kernel,
            out_shape=(shape, shape),
            in_specs=[pl.BlockSpec(memory_space=pl.ANY)] * 4,
            out_specs=(pl.BlockSpec(memory_space=pltpu.VMEM),) * 2,
            scratch_shapes=SCRATCH,
            compiler_params=pltpu.CompilerParams(
                collective_id=0, has_side_effects=True, vmem_limit_bytes=56 * 2**20),
        )(right_side, initial, shift, beta)

    spec = P(*AXES)
    return jax.shard_map(local, mesh=mesh, in_specs=(spec,) * 4, out_specs=(spec, spec), check_vma=False)
```

```python
import itertools

import jax
import jax.numpy as jnp
from jax import lax
from jax.experimental import pallas as pl
from jax.experimental.pallas import tpu as pltpu
from jax.sharding import PartitionSpec as P

CG_ITERS = 8
MESH = pl.DeviceIdType.MESH
AXES = ("gx", "gy", "gz")
SIZES = (8, 8, 4)
F32 = jnp.float32
BF16 = jnp.bfloat16

ALL26 = sorted((o for o in itertools.product((-1, 0, 1), repeat=3) if o != (0, 0, 0)),
               key=lambda o: -sum(map(abs, o)))
XY8 = [o for o in ALL26 if o[2] == 0]
XY4 = [o for o in XY8 if o[0] * o[1] == 0]
CORNERS = [o for o in XY8 if o[0] * o[1] != 0]
X6 = [o for o in XY8 if o[0] != 0]
RING7 = [(k, 0, 0) for k in range(1, 8)]
ROW3 = [(0, 0, k) for k in range(1, 4)]
CHIPS3 = [(0, j, 0) for j in (2, 4, 6)]
SAME15 = sorted(((0, j, k) for j in (0, 2, 4, 6) for k in range(4) if (j, k) != (0, 0)),
                key=lambda o: min(o[1], 8 - o[1]) // 2 + min(o[2], 4 - o[2]))


def canonical(offset):
    return tuple(o % n for o, n in zip(offset, SIZES))


PARTNERS = sorted({canonical(o) for o in ALL26 + RING7 + [(0, 4, 0)]})


def source_span(d, start, count, halo):
    if d == 0:
        return pl.ds(start, count)
    return pl.ds(start + count - halo, halo) if d > 0 else pl.ds(start, halo)


def target_span(d, start, count, halo):
    if d == 0:
        return pl.ds(start, count)
    return pl.ds(start - halo, halo) if d > 0 else pl.ds(start + count, halo)


def iota(shape, dim):
    return lax.broadcasted_iota(jnp.int32, shape, dim)


def loop(lo, hi, body, init, unroll):
    def chunk(k, carry):
        for j in range(unroll):
            carry = body(lo + k * unroll + j, carry)
        return carry

    return lax.fori_loop(0, (hi - lo) // unroll, chunk, init)


def pick(values, matrix):
    high = values.astype(BF16)
    rest = values - high.astype(F32)
    middle = rest.astype(BF16)
    low = (rest - middle.astype(F32)).astype(BF16)
    out = jnp.dot(low, matrix, preferred_element_type=F32)
    out = out + jnp.dot(middle, matrix, preferred_element_type=F32)
    return out + jnp.dot(high, matrix, preferred_element_type=F32)


def roll(value, shift):
    shift = shift % 128
    return value if shift == 0 else pltpu.roll(value, shift, 1)


def kernel(f_in, u_in, s_in, b_in, x_out, r_out, E0, M0, MX, RZ0, CP, CR, V0, PB0, A0, D0, DG0, FD0,
           C1, R1s, RZ1, S1, M1, ZR1, PS, V1, PB1, A1, D1, DG1, FD1,
           EU, MU, ZU, T16, T8, T4, X16, XB, GC, GS, S2, B2, A2, DG2, PD, RM, AP, XL,
           sem_in, s_e0, r_e0, s_c1z, r_c1z, s_c1, r_c1, s_e2, r_e2, s_uz, r_uz, s_u, r_u,
           s_ps, r_ps, s_gc1, r_gc1, s_gc2, r_gc2, s_gs1, r_gs1, s_gs2, r_gs2,
           s_gc3, r_gc3, s_gc4, r_gc4, s_gs3, r_gs3, s_c1b, r_c1b,
           s_z0, r_z0, s_mx, r_mx):
    gx, gy, gz = (lax.axis_index(a) for a in AXES)
    me = (gx, gy, gz)
    core = lax.rem(gy, 2)
    twin = (gx, gy + 1 - 2 * core, gz)

    def device(offset):
        return tuple(lax.rem(m + (o % n), n) if o % n else m for m, o, n in zip(me, offset, SIZES))

    def send(src, dst, ssem, rsem, offset=None):
        copy = pltpu.make_async_remote_copy(src_ref=src, dst_ref=dst, send_sem=ssem, recv_sem=rsem,
                                            device_id=twin if offset is None else device(offset),
                                            device_id_type=MESH)
        copy.start()
        return copy

    def wait(copies):
        for copy in copies:
            copy.wait()

    local = [pltpu.make_async_copy(src, E0.at[k, pl.ds(6, 16), pl.ds(8, 16)], sem_in.at[k])
             for k, src in enumerate((f_in, s_in, u_in, b_in))]
    for copy in local:
        copy.start()
    barrier = pltpu.get_barrier_semaphore()
    for offset in PARTNERS:
        pl.semaphore_signal(barrier, inc=1, device_id=device(offset), device_id_type=MESH)

    q24 = (iota((24, 128), 0) + iota((24, 128), 1)) % 2 == 1
    q32 = (iota((32, 128), 0) + iota((32, 128), 1)) % 2 == 1
    q16 = (iota((16, 128), 0) + iota((16, 128), 1)) % 2 == 1
    lane24 = iota((24, 128), 1)
    one, zero = jnp.float32(1.0), jnp.float32(0.0)

    def y_mask(rows, own_start, own_count):
        row = iota((rows, 128), 0)
        low = jnp.where(gy == 0, zero, one)
        high = jnp.where(gy == 7, zero, one)
        return jnp.where(row < own_start, low, jnp.where(row >= own_start + own_count, high, one))

    def z_mask(rows, low_at, high_at):
        lane = iota((rows, 128), 1)
        low = jnp.where(gz == 0, zero, one)
        high = jnp.where(gz == 3, zero, one)
        return jnp.where(low_at(lane), low, jnp.where(high_at(lane), high, one))

    y32 = y_mask(32, 8, 16)
    mask0 = (y32, y32 * z_mask(32, lambda l: l >= 64, lambda l: l < 64))
    mask1 = (y_mask(40, 16, 8) * z_mask(40, lambda l: l < 32, lambda l: l >= 96),)

    def x_scalar(p, low_end, high_start):
        outside = ((gx == 0) & (p < low_end)) | ((gx == 7) & (p >= high_start))
        return jnp.where(outside, zero, one)

    row, col = iota((128, 128), 0), iota((128, 128), 1)
    to_one = jnp.where((col >= 32) & (col < 96) & (col - 32 == row // 2), 0.125, 0.0).astype(BF16)
    to_two = jnp.where((row >= 32) & (row < 96) & (col == (row - 32) // 2), 0.125, 0.0).astype(BF16)
    from_two = jnp.where((col - 32 + 64 * gz + 128) // 2 - 64 == row, 1.0, 0.0).astype(BF16)
    from_one = jnp.where(row - 32 == col // 2, 1.0, 0.0).astype(BF16)
    from_one_edge = jnp.where(
        ((col < 64) & (row == 96 + col // 2)) | ((col >= 64) & (row == col // 2 - 32)), 1.0, 0.0
    ).astype(BF16)

    def restrict_one(sums):
        T16[...] = sums
        folded = T16[:, pl.ds(0, 8, stride=2), :] + T16[:, pl.ds(1, 8, stride=2), :]
        return pick(folded.reshape(64, 128), to_one).reshape(8, 8, 128)

    def restrict_two(sums):
        T8[...] = sums
        total = None
        for x in range(4):
            folded = T8[x, pl.ds(0, 4, stride=2), :] + T8[x, pl.ds(1, 4, stride=2), :]
            T4[x, 0:4] = folded
        full = pick(T4[...].reshape(32, 128), to_two).reshape(4, 8, 128)
        for x in range(4):
            term = roll(full[x], 32 * x)
            total = term if total is None else total + term
        return total[0:4]

    for copy in local:
        copy.wait()
    upper = iota((8, 128), 0) < 4
    for n, (dx, dy, _) in enumerate(CORNERS):
        x, y = (18 if dx > 0 else 6), (16 if dy > 0 else 8)
        for a in range(4):
            for k in range(2):
                first, second = E0[a, x + 2 * k, pl.ds(y, 8), :], E0[a, x + 2 * k + 1, pl.ds(y, 8), :]
                if dy > 0:
                    first = pltpu.roll(first, 4, 0)
                else:
                    second = pltpu.roll(second, 4, 0)
                CP[n, a, k] = jnp.where(upper, first, second)

    lane16 = iota((16, 128), 1)
    group = lane16 // 16

    def pack_rows(k, carry):
        total = jnp.zeros((16, 128), F32)
        for odd in range(2):
            for a in range(4):
                value = E0[a, 6 + 2 * k + odd, pl.ds(8, 16), :]
                total = jnp.where(group == 4 * odd + a, roll(value, 8 + 16 * a + 64 * odd), total)
        M0[k] = total
        return carry

    loop(0, 8, pack_rows, 0, 4)
    pl.semaphore_wait(barrier, len(PARTNERS))
    z0 = [send(M0, RZ0.at[n], s_z0.at[n], r_z0.at[n], (0, 0, 1 if n == 0 else -1)) for n in range(2)]
    e0 = [send(E0.at[:, source_span(dx, 6, 16, 5), source_span(dy, 8, 16, 8)],
               E0.at[:, target_span(dx, 6, 16, 5), target_span(dy, 8, 16, 8)],
               s_e0.at[n], r_e0.at[n], (dx, dy, 0)) for n, (dx, dy, _) in enumerate(XY4)]
    for n, (dx, dy, _) in enumerate(CORNERS):
        e0.append(send(CP.at[n], CR.at[n], s_e0.at[4 + n], r_e0.at[4 + n], (dx, dy, 0)))

    for k, a in ((0, 1), (1, 3)):
        sums = jnp.stack([E0[a, 6 + 2 * x, pl.ds(8, 16), :] + E0[a, 7 + 2 * x, pl.ds(8, 16), :] for x in range(8)])
        C1[k, pl.ds(8, 8), pl.ds(8, 8)] = restrict_one(sums)
        for x in range(8):
            R1s[k, x] = roll(C1[k, 8 + x, pl.ds(8, 8), :], 64)
    c1z = [send(R1s, RZ1.at[n], s_c1z.at[n], r_c1z.at[n], (0, 0, 1 if n == 0 else -1)) for n in range(2)]
    mine = gy * 4 + gz
    for k in range(2):
        sums = jnp.stack([C1[k, 8 + 2 * x, pl.ds(8, 8), :] + C1[k, 9 + 2 * x, pl.ds(8, 8), :] for x in range(4)])
        GC[mine, gx, k] = restrict_two(sums)
    gc1 = [send(GC.at[mine, gx], GC.at[mine, gx], s_gc1.at[n], r_gc1.at[n], o) for n, o in enumerate(RING7)]
    wait(z0)
    for k in range(8):
        MX[2 + k, pl.ds(8, 16)] = jnp.where(lane16 % 16 < 8, RZ0[0, k], RZ0[1, k])
    mx = [send(MX.at[source_span(dx, 2, 8, 2), source_span(dy, 8, 16, 8)],
               MX.at[target_span(dx, 2, 8, 2), target_span(dy, 8, 16, 8)],
               s_mx.at[n], r_mx.at[n], (dx, dy, 0)) for n, (dx, dy, _) in enumerate(XY8)]
    wait(c1z)
    lane8 = iota((8, 128), 1)
    for k in range(2):
        for x in range(8):
            own = C1[k, 8 + x, pl.ds(8, 8), :]
            C1[k, 8 + x, pl.ds(8, 8), :] = jnp.where(
                lane8 < 32, RZ1[0, k, x], jnp.where(lane8 < 96, own, RZ1[1, k, x]))
    def around(O, tiles, c, i, r0, q):
        out = []
        centre = [O[t, 1 - c, i + 1, pl.ds(r0, 24), :] for t in range(tiles)]
        ups = [roll(v, -1) for v in centre]
        downs = [roll(v, 1) for v in centre]
        for t in range(tiles):
            low = O[t, 1 - c, i, pl.ds(r0, 24), :]
            high = O[t, 1 - c, i + 2, pl.ds(r0, 24), :]
            other = jnp.where(q, high, low) if c == 0 else jnp.where(q, low, high)
            yp = O[t, 1 - c, i + 1, pl.ds(r0 + 1, 24), :]
            ym = O[t, 1 - c, i + 1, pl.ds(r0 - 1, 24), :]
            if tiles == 2:
                zp = jnp.where(lane24 == 127, ups[1 - t], ups[t])
                zm = jnp.where(lane24 == 0, downs[1 - t], downs[t])
            else:
                zp, zm = ups[0], downs[0]
            out.append((centre[t], other, yp, ym, zp, zm))
        return out

    def coefficients(PB, A, D, DG, tiles, r0, scale, shift_of, mask, x_of, lo=0, hi=12):
        for c in range(2):
            def body(i, carry):
                near = around(PB, tiles, c, i, r0, q24)
                for t in range(tiles):
                    b = PB[t, c, i + 1, pl.ds(r0, 24), :]
                    total = shift_of(t, c, i)
                    weights = [(0.5 * scale) * (b + v) for v in near[t]]
                    for w in weights:
                        total = total + w
                    inverse = (1.0 / total) * (mask[t][r0:r0 + 24] * x_of(i + 1))
                    DG[t, c, i] = total
                    D[t, c, i] = inverse
                    for k, w in enumerate(weights):
                        A[t, c, k, i] = w * inverse
                return carry
            loop(lo, hi, body, 0, 4)

    def relaxed(V, A, FD, tiles, c, i, r0):
        near = around(V, tiles, c, i, r0, q24)
        out = []
        for t in range(tiles):
            total = FD[t, c, i]
            for k, v in enumerate(near[t]):
                total = total + A[t, c, k, i] * v
            out.append(total)
        return out

    def half(V, A, FD, tiles, c, r0, lo, hi, unroll):

        def body(k, carry):
            first = lo + k * unroll
            news = [relaxed(V, A, FD, tiles, c, first + j, r0) for j in range(unroll)]
            for j, new in enumerate(news):
                for t in range(tiles):
                    V[t, c, first + j + 1, pl.ds(r0, 24), :] = new[t]
            return carry
        lax.fori_loop(0, (hi - lo) // unroll, body, 0)

    def sweeps(V, A, FD, tiles, r0, spans, first=0):
        for step in range(first, 4):
            half(V, A, FD, tiles, step % 2, r0, *spans[step // 2])

    def residual_pair(V, A, FD, DG, tiles, i, r0):
        out = []
        for c in range(2):
            new = relaxed(V, A, FD, tiles, c, i, r0)[0]
            out.append(DG[0, c, i] * (new - V[0, c, i + 1, pl.ds(r0, 24), :]))
        return out

    def unpack(red, black, q):
        return jnp.where(q, black, red), jnp.where(q, red, black)

    PD[...] = jnp.zeros_like(PD)
    B2[...] = jnp.zeros_like(B2)
    V1[...] = jnp.zeros_like(V1)
    PB1[...] = jnp.zeros_like(PB1)
    wait(e0)
    for n, (dx, dy, _) in enumerate(CORNERS):
        x, y = (2 if dx > 0 else 22), (4 if dy > 0 else 24)
        for a in range(4):
            for k in range(4):
                E0[a, x + k, pl.ds(y, 4), :] = CR[n, a, k // 2, pl.ds(4 * (k % 2), 4), :]
    wait(mx)
    c1 = [send(C1.at[:, source_span(dx, 8, 8, 4), source_span(dy, 8, 8, 8)],
               C1.at[:, target_span(dx, 8, 8, 4), target_span(dy, 8, 8, 8)],
               s_c1.at[n], r_c1.at[n], (dx, dy, 0)) for n, (dx, dy, _) in enumerate(XY8)]

    lane32 = iota((32, 128), 1)

    def edge_of(a, p):
        merged = MX[p - 1]
        return roll(merged, -(16 * a + 8)), roll(merged, -(16 * a + 72))

    x0 = lambda p: x_scalar(p, 3, 11)
    x1 = lambda p: x_scalar(p, 5, 9)

    def pack0(p, carry):
        xs = x0(p)
        for dst, a in ((V0, 2), (PB0, 3)):
            even, odd = E0[a, 2 * p], E0[a, 2 * p + 1]
            m = mask0[0] * xs
            dst[0, 0, p] = jnp.where(q32, odd, even) * m
            dst[0, 1, p] = jnp.where(q32, even, odd) * m
        return carry

    loop(0, 14, pack0, 0, 7)
    for p in (0, 13):
        for dst in (V0, PB0):
            for c in range(2):
                dst[1, c, p] = jnp.zeros((32, 128), F32)

    def pack0_edge(p, carry):
        xs = x0(p)
        for dst, a in ((V0, 2), (PB0, 3)):
            even, odd = edge_of(a, p)
            m = mask0[1] * xs
            dst[1, 0, p] = jnp.where(q32, odd, even) * m
            dst[1, 1, p] = jnp.where(q32, even, odd) * m
        for dst, a in ((FD0, 0), (DG0, 1)):
            even, odd = edge_of(a, p)
            dst[1, 0, p - 1] = jnp.where(q32, odd, even)[4:28]
            dst[1, 1, p - 1] = jnp.where(q32, even, odd)[4:28]
            even, odd = E0[a, 2 * p, pl.ds(4, 24), :], E0[a, 2 * p + 1, pl.ds(4, 24), :]
            dst[0, 0, p - 1] = jnp.where(q24, odd, even)
            dst[0, 1, p - 1] = jnp.where(q24, even, odd)
        return carry

    loop(1, 13, pack0_edge, 0, 6)
    coefficients(PB0, A0, D0, DG0, 2, 4, 1.0, lambda t, c, i: DG0[t, c, i], mask0, x0)

    def scale_rhs0(i, carry):
        for t in range(2):
            for c in range(2):
                FD0[t, c, i] = FD0[t, c, i] * D0[t, c, i]
        return carry

    loop(0, 12, scale_rhs0, 0, 4)
    wait(gc1)
    gc2 = [send(GC.at[mine], GC.at[mine], s_gc2.at[n], r_gc2.at[n], o) for n, o in enumerate(ROW3)]
    sweeps(V0, A0, FD0, 2, 4, ((0, 12, 4), (1, 11, 5)))

    sums = []
    for i in range(2, 10):
        red, black = residual_pair(V0, A0, FD0, DG0, 2, i, 4)
        sums.append((red + black)[4:20])
    own = restrict_one(jnp.stack(sums))
    wait(c1)

    def pack1(p, carry):
        xs = x1(p)
        m = mask1[0][8:32] * xs
        even, odd = C1[1, 2 * p - 2], C1[1, 2 * p - 1]
        PB1[0, 0, p, pl.ds(8, 24), :] = jnp.where(q24, odd, even) * m
        PB1[0, 1, p, pl.ds(8, 24), :] = jnp.where(q24, even, odd) * m
        even, odd = C1[0, 2 * p - 2], C1[0, 2 * p - 1]
        DG1[0, 0, p - 1] = jnp.where(q24, odd, even)
        DG1[0, 1, p - 1] = jnp.where(q24, even, odd)
        return carry

    def coefficients1(lo, hi):
        loop(lo + 1, hi + 1, pack1, 0, 4)
        coefficients(PB1, A1, D1, DG1, 1, 8, 0.25, lambda t, c, i: DG1[t, c, i], mask1, x1, lo, hi)

    coefficients1(2, 10)
    q8 = (iota((8, 128), 0) + iota((8, 128), 1)) % 2 == 1
    for i in range(4, 8):
        even, odd = own[2 * i - 8], own[2 * i - 7]
        red = jnp.where(q8, odd, even) * D1[0, 0, i, pl.ds(8, 8), :]
        black = jnp.where(q8, even, odd) * D1[0, 1, i, pl.ds(8, 8), :]
        S1[2 * i, pl.ds(8, 8)], S1[2 * i + 1, pl.ds(8, 8)] = unpack(red, black, q8)
    slot = iota((8, 128), 1) // 16
    for g in range(2):
        total = jnp.zeros((8, 128), F32)
        for k in range(4):
            value = roll(S1[8 + 4 * g + k, pl.ds(8, 8), :], 64 + 32 * k)
            total = jnp.where((slot == 1 + 2 * k) | (slot == (6 + 2 * k) % 8), value, total)
        M1[g] = total
    e2 = []
    for n, (dx, dy, dz) in enumerate(ALL26):
        if dz == 0:
            e2.append(send(S1.at[source_span(dx, 8, 8, 4), source_span(dy, 8, 8, 8)],
                           S1.at[target_span(dx, 8, 8, 4), target_span(dy, 8, 8, 8)],
                           s_e2.at[n], r_e2.at[n], (dx, dy, dz)))
        else:
            side = 0 if dz > 0 else 1
            e2.append(send(M1.at[source_span(dx, 0, 2, 1), source_span(dy, 0, 8, 8)],
                           ZR1.at[side, target_span(dx, 1, 2, 1), target_span(dy, 8, 8, 8)],
                           s_e2.at[n], r_e2.at[n], (dx, dy, dz)))

    for i in range(2, 10):
        red, black = V0[0, 0, i + 1, pl.ds(8, 16), :], V0[0, 1, i + 1, pl.ds(8, 16), :]
        EU[0, 2 * i + 2, pl.ds(8, 16)], EU[0, 2 * i + 3, pl.ds(8, 16)] = unpack(red, black, q16)
    for g in range(2):
        total = jnp.zeros((16, 128), F32)
        for k in range(8):
            total = jnp.where(group == k, roll(EU[0, 6 + 8 * g + k, pl.ds(8, 16), :], 8 + 16 * k), total)
        MU[g] = total
    uz = [send(MU, ZU.at[n], s_uz.at[n], r_uz.at[n], (0, 0, 1 if n == 0 else -1)) for n in range(2)]

    wait(gc2)
    row_of = GC.at[pl.ds(gy * 4, 4)]
    gc3 = [send(row_of, row_of, s_gc3.at[n], r_gc3.at[n], o) for n, o in enumerate(CHIPS3)]
    c1b = [send(C1.at[:, source_span(-dx, 8, 8, 4), source_span(dy, 8, 8, 8)],
                C1.at[:, pl.ds(0 if dx > 0 else 20, 4), target_span(dy, 8, 8, 8)],
                s_c1b.at[n], r_c1b.at[n], (dx, dy, 0)) for n, (dx, dy, _) in enumerate(X6)]
    wait(e2)
    slot24 = lane24 // 16
    for x in range(4, 20):
        g = (x - 4) // 4
        merged = jnp.where(slot24 % 2 == 1, ZR1[0, g], ZR1[1, g])
        halo = roll(merged, -32 * (x % 4))
        S1[x] = jnp.where((lane24 >= 32) & (lane24 < 96), S1[x], halo)
    PS[1, pl.ds(8, 8), pl.ds(8, 8)] = S1[pl.ds(8, 8), pl.ds(8, 8)]

    def rhs1(source, lo, hi):
        def body(i, carry):
            even, odd = source[2 * i], source[2 * i + 1]
            m = mask1[0][8:32] * x1(i + 1)
            FD1[0, 0, i] = jnp.where(q24, odd, even) * m
            FD1[0, 1, i] = jnp.where(q24, even, odd) * m
            return carry
        loop(lo, hi, body, 0, 4)

    rhs1(S1, 2, 10)
    for i in range(2, 10):
        V1[0, 0, i + 1, pl.ds(8, 24), :] = FD1[0, 0, i]
    sweeps(V1, A1, FD1, 1, 8, ((2, 10, 4), (3, 9, 6)), first=1)
    sums = []
    for i in range(4, 8):
        red, black = residual_pair(V1, A1, FD1, DG1, 1, i, 8)
        sums.append((red + black)[8:16])
    GS[mine, gx] = restrict_two(jnp.stack(sums))
    gs1 = [send(GS.at[mine, gx], GS.at[mine, gx], s_gs1.at[n], r_gs1.at[n], o) for n, o in enumerate(RING7)]

    wait(gc3)
    gc4 = []
    for n in range(4):
        rows = GC.at[pl.ds((core + 2 * n) * 4, 4)]
        gc4.append(send(rows, rows, s_gc4.at[n], r_gc4.at[n]))
    for i in range(4, 8):
        red, black = V1[0, 0, i + 1, pl.ds(16, 8), :], V1[0, 1, i + 1, pl.ds(16, 8), :]
        PS[0, 2 * i, pl.ds(8, 8)], PS[0, 2 * i + 1, pl.ds(8, 8)] = unpack(red, black, q8)
    wait(uz)
    for x in range(16):
        merged = jnp.where(lane16 % 16 < 8, ZU[0, x // 8], ZU[1, x // 8])
        EU[1, 6 + x, pl.ds(8, 16)] = roll(merged, -(16 * (x % 8) + 8))
    wait(gs1)
    gs2 = [send(GS.at[mine], GS.at[mine], s_gs2.at[n], r_gs2.at[n], o) for n, o in enumerate(SAME15)]
    gs3 = [send(GS.at[mine], GS.at[mine], s_gs3.at[15], r_gs3.at[15])]
    ps = [send(PS.at[:, source_span(dx, 8, 8, 8), source_span(dy, 8, 8, 8)],
               PS.at[:, target_span(dx, 8, 8, 8), target_span(dy, 8, 8, 8)],
               s_ps.at[n], r_ps.at[n], (dx, dy, 0)) for n, (dx, dy, _) in enumerate(XY8)]

    lane_group = lane8 // 32

    def spread(load, store):
        def body(g, carry):
            for pair in range(4):
                blocks = [jnp.concatenate([load(8 * pair + k, g), load(8 * pair + 4 + k, g)], axis=0)
                          for k in range(4)]
                for x in range(4):
                    total = roll(blocks[0], -32 * x)
                    for k in range(1, 4):
                        total = jnp.where(lane_group == k, roll(blocks[k], 32 * (k - x)), total)
                    store(4 * g + x, 8 * pair, total)
            return carry
        loop(0, 8, body, 0, 4)

    def store_s2(x, y, v):
        S2[x, pl.ds(y, 8), :] = v

    def store_b2(x, y, v):
        B2[x + 4, pl.ds(y + 8, 8), :] = v

    def store_source(x, y, v):
        PD[x + 4, pl.ds(y + 8, 8), :] = v
        RM[x, pl.ds(y, 8), :] = v

    wait(gc4)
    spread(lambda j, g: GC[j, g, 0], store_s2)
    spread(lambda j, g: GC[j, g, 1], store_b2)

    def shifts(O, x):
        centre = O[x + 4, pl.ds(8, 32), :]
        return (centre, (O[x + 5, pl.ds(8, 32), :], O[x + 3, pl.ds(8, 32), :], O[x + 4, pl.ds(9, 32), :],
                         O[x + 4, pl.ds(7, 32), :], roll(centre, -1), roll(centre, 1)))

    def weights2(x, carry):
        b, near = shifts(B2, x)
        total = S2[x]
        for k, v in enumerate(near):
            if k == 4:
                v = jnp.where(lane32 == 127, 0.0, v)
            if k == 5:
                v = jnp.where(lane32 == 0, 0.0, v)
            w = (0.5 * 0.0625) * (b + v)
            total = total + w
            if k == 4:
                w = jnp.where(lane32 == 127, 0.0, w)
            if k == 5:
                w = jnp.where(lane32 == 0, 0.0, w)
            A2[k, x] = w
        DG2[x] = total
        return carry

    loop(0, 32, weights2, 0, 8)

    wait(c1b)
    coefficients1(0, 12)

    for n, (_, j, k) in enumerate(SAME15):
        gs2[n].wait()
        came = GS.at[lax.rem(gy + 8 - j, 8) * 4 + lax.rem(gz + 4 - k, 4)]
        gs3.append(send(came, came, s_gs3.at[n], r_gs3.at[n]))
    wait(gs3)
    eu = [send(EU.at[:, source_span(dx, 6, 16, 5), source_span(dy, 8, 16, 8)],
               EU.at[:, target_span(dx, 6, 16, 5), target_span(dy, 8, 16, 8)],
               s_u.at[n], r_u.at[n], (dx, dy, 0)) for n, (dx, dy, _) in enumerate(XY8)]
    spread(lambda j, g: GS[j, g], store_source)
    XL[...] = jnp.zeros_like(XL)

    def whole(total):
        return jnp.sum(jnp.sum(total, axis=0, keepdims=True), axis=1, keepdims=True)

    def square(x, total):
        return total + RM[x] * RM[x]

    acc = jnp.zeros((32, 128), F32)
    RM[32] = acc
    rr = whole(loop(0, 32, square, acc, 8))
    for step in range(CG_ITERS):
        def plane(x):
            value = PD[x + 4, pl.ds(8, 32), :]
            if step:
                value = RM[x] + ratio * value
                PD[x + 4, pl.ds(8, 32), :] = value
            return value

        if step:
            plane(0)

        def image(g, total):
            start = 16 * g
            before = PD[start + 3, pl.ds(8, 32), :]
            weight = A2[1, start]
            p = PD[start + 4, pl.ds(8, 32), :]
            for j in range(16):
                x = start + j
                after = plane(x + 1)
                value = DG2[x] * p - weight * before
                weight = A2[0, x]
                value = value - weight * after
                value = value - A2[2, x] * PD[x + 4, pl.ds(9, 32), :]
                value = value - A2[3, x] * PD[x + 4, pl.ds(7, 32), :]
                value = value - A2[4, x] * roll(p, -1) - A2[5, x] * roll(p, 1)
                AP[x] = value
                total = total + p * value
                before, p = p, after
            return total

        alpha = rr / whole(lax.fori_loop(0, 32 // 16, image, acc))

        def gain(x, carry):
            XL[x] = XL[x] + alpha * PD[4 * gx + x, pl.ds(4 * gy + 4, 16), :]
            return carry

        loop(0, 12, gain, 0, 12)
        if step < CG_ITERS - 1:
            def update(x, total):
                value = RM[x] - alpha * AP[x]
                RM[x] = value
                return total + value * value

            new = whole(loop(0, 32, update, acc, 16))
            ratio = new / rr

            rr = new

    wait(ps)

    def pack1_post(p, carry):
        m = mask1[0][8:32] * x1(p)
        even, odd = PS[0, 2 * p - 2], PS[0, 2 * p - 1]
        V1[0, 0, p, pl.ds(8, 24), :] = jnp.where(q24, odd, even) * m
        V1[0, 1, p, pl.ds(8, 24), :] = jnp.where(q24, even, odd) * m
        return carry

    loop(1, 13, pack1_post, 0, 4)
    rhs1(PS.at[1], 0, 12)

    wait(eu)

    def pack0_post(p, carry):
        xs = x0(p)
        for t in range(2):
            m = mask0[t] * xs
            even, odd = EU[t, 2 * p], EU[t, 2 * p + 1]
            V0[t, 0, p] = jnp.where(q32, odd, even) * m
            V0[t, 1, p] = jnp.where(q32, even, odd) * m
        return carry

    loop(0, 14, pack0_post, 0, 2)

    fine = pick(XL[...].reshape(192, 128), from_two).reshape(12, 16, 128)
    X16[:, pl.ds(0, 16, stride=2), :] = fine
    X16[:, pl.ds(1, 16, stride=2), :] = fine

    def correct1(i, carry):
        for c in range(2):
            V1[0, c, i + 1, pl.ds(8, 24), :] = V1[0, c, i + 1, pl.ds(8, 24), :] + X16[i, 0:24]
        return carry

    loop(0, 12, correct1, 0, 12)
    sweeps(V1, A1, FD1, 1, 8, ((1, 11, 5), (2, 10, 4)))

    planes = []
    for p in range(14):
        k = (p + 7) // 2
        red, black = V1[0, 0, k, pl.ds(12, 16), :], V1[0, 1, k, pl.ds(12, 16), :]
        planes.append(unpack(red, black, q16)[0 if p % 2 else 1])
    coarse = jnp.stack(planes).reshape(224, 128)
    for t, matrix in enumerate((from_one, from_one_edge)):
        fine = pick(coarse, matrix).reshape(14, 16, 128)
        XB[:, pl.ds(0, 16, stride=2), :] = fine
        XB[:, pl.ds(1, 16, stride=2), :] = fine

        def correct0(p, carry):
            for c in range(2):
                V0[t, c, p] = V0[t, c, p] + XB[p]
            return carry

        loop(0, 14, correct0, 0, 7)
    sweeps(V0, A0, FD0, 2, 4, ((0, 12, 4), (1, 11, 5)))

    def finish(i, carry):
        red, black = residual_pair(V0, A0, FD0, DG0, 2, i, 4)
        even, odd = unpack(red, black, q24)
        r_out[2 * i - 4] = even[4:20]
        r_out[2 * i - 3] = odd[4:20]
        even, odd = unpack(V0[0, 0, i + 1, pl.ds(8, 16), :], V0[0, 1, i + 1, pl.ds(8, 16), :], q16)
        x_out[2 * i - 4] = even
        x_out[2 * i - 3] = odd
        return carry

    loop(2, 10, finish, 0, 4)


def vmem(*shape):
    return pltpu.VMEM(shape, F32)


def dma(*shape):
    return pltpu.SemaphoreType.DMA(shape)


SCRATCH = [
    vmem(4, 28, 32, 128), vmem(8, 16, 128), vmem(12, 32, 128), vmem(2, 8, 16, 128),
    vmem(4, 4, 2, 8, 128), vmem(4, 4, 2, 8, 128),
    vmem(2, 2, 14, 32, 128), vmem(2, 2, 14, 32, 128), vmem(2, 2, 6, 12, 24, 128),
    vmem(2, 2, 12, 24, 128), vmem(2, 2, 12, 24, 128), vmem(2, 2, 12, 24, 128),
    vmem(2, 24, 24, 128), vmem(2, 8, 8, 128), vmem(2, 2, 8, 8, 128),
    vmem(24, 24, 128), vmem(2, 8, 128), vmem(2, 4, 24, 128), vmem(2, 24, 24, 128),
    vmem(1, 2, 14, 40, 128), vmem(1, 2, 14, 40, 128), vmem(1, 2, 6, 12, 24, 128),
    vmem(1, 2, 12, 24, 128), vmem(1, 2, 12, 24, 128), vmem(1, 2, 12, 24, 128),
    vmem(2, 28, 32, 128), vmem(2, 16, 128), vmem(2, 2, 16, 128),
    vmem(8, 16, 128), vmem(4, 8, 128), vmem(4, 8, 128), vmem(12, 32, 128), vmem(14, 32, 128),
    vmem(32, 8, 2, 4, 128), vmem(32, 8, 4, 128),
    vmem(32, 32, 128), vmem(40, 48, 128), vmem(6, 32, 32, 128), vmem(32, 32, 128),
    vmem(40, 48, 128), vmem(33, 32, 128), vmem(32, 32, 128), vmem(12, 16, 128),
    dma(4), dma(8), dma(8), dma(2), dma(2), dma(8), dma(8), dma(26), dma(26), dma(2), dma(2), dma(8), dma(8),
    dma(8), dma(8), dma(7), dma(7), dma(3), dma(3), dma(7), dma(7), dma(15), dma(15),
    dma(3), dma(3), dma(4), dma(4), dma(16), dma(16), dma(6), dma(6),
    dma(2), dma(2), dma(8), dma(8),
]


def solution(mesh):
    def local(right_side, initial, shift, beta):
        shape = jax.ShapeDtypeStruct(right_side.shape, F32)
        return pl.pallas_call(
            kernel,
            out_shape=(shape, shape),
            in_specs=[pl.BlockSpec(memory_space=pl.ANY)] * 4,
            out_specs=(pl.BlockSpec(memory_space=pltpu.VMEM),) * 2,
            scratch_shapes=SCRATCH,
            compiler_params=pltpu.CompilerParams(
                collective_id=0, has_side_effects=True, vmem_limit_bytes=56 * 2**20),
        )(right_side, initial, shift, beta)

    spec = P(*AXES)
    return jax.shard_map(local, mesh=mesh, in_specs=(spec,) * 4, out_specs=(spec, spec), check_vma=False)
```

```python
import itertools

import jax
import jax.numpy as jnp
from jax import lax
from jax.experimental import pallas as pl
from jax.experimental.pallas import tpu as pltpu
from jax.sharding import PartitionSpec as P

CG_ITERS = 8
MESH = pl.DeviceIdType.MESH
AXES = ("gx", "gy", "gz")
SIZES = (8, 8, 4)
F32 = jnp.float32
BF16 = jnp.bfloat16

ALL26 = sorted((o for o in itertools.product((-1, 0, 1), repeat=3) if o != (0, 0, 0)),
               key=lambda o: -sum(map(abs, o)))
XY8 = [o for o in ALL26 if o[2] == 0]
XY4 = [o for o in XY8 if o[0] * o[1] == 0]
CORNERS = [o for o in XY8 if o[0] * o[1] != 0]
RING7 = [(k, 0, 0) for k in range(1, 8)]
ROW3 = [(0, 0, k) for k in range(1, 4)]
CHIPS3 = [(0, j, 0) for j in (2, 4, 6)]
SAME15 = sorted(((0, j, k) for j in (0, 2, 4, 6) for k in range(4) if (j, k) != (0, 0)),
                key=lambda o: min(o[1], 8 - o[1]) // 2 + min(o[2], 4 - o[2]))


def canonical(offset):
    return tuple(o % n for o, n in zip(offset, SIZES))


PARTNERS = sorted({canonical(o) for o in ALL26 + RING7 + [(0, 4, 0)]})


def source_span(d, start, count, halo):
    if d == 0:
        return pl.ds(start, count)
    return pl.ds(start + count - halo, halo) if d > 0 else pl.ds(start, halo)


def target_span(d, start, count, halo):
    if d == 0:
        return pl.ds(start, count)
    return pl.ds(start - halo, halo) if d > 0 else pl.ds(start + count, halo)


def iota(shape, dim):
    return lax.broadcasted_iota(jnp.int32, shape, dim)


def loop(lo, hi, body, init, unroll):
    def chunk(k, carry):
        for j in range(unroll):
            carry = body(lo + k * unroll + j, carry)
        return carry

    return lax.fori_loop(0, (hi - lo) // unroll, chunk, init)


def pick(values, matrix):
    high = values.astype(BF16)
    rest = values - high.astype(F32)
    middle = rest.astype(BF16)
    low = (rest - middle.astype(F32)).astype(BF16)
    out = jnp.dot(low, matrix, preferred_element_type=F32)
    out = out + jnp.dot(middle, matrix, preferred_element_type=F32)
    return out + jnp.dot(high, matrix, preferred_element_type=F32)


def roll(value, shift):
    shift = shift % 128
    return value if shift == 0 else pltpu.roll(value, shift, 1)


def kernel(f_in, u_in, s_in, b_in, x_out, r_out, E0, M0, MX, RZ0, CP, CR, V0, PB0, A0, D0, DG0, FD0,
           C1, R1s, RZ1, S1, M1, ZR1, PS, V1, PB1, A1, D1, DG1, FD1,
           EU, MU, ZU, T16, T8, T4, X16, XB, GC, GS, S2, B2, A2, DG2, PD, RM, AP, XL,
           sem_in, s_e0, r_e0, s_c1z, r_c1z, s_c1, r_c1, s_e2, r_e2, s_uz, r_uz, s_u, r_u,
           s_ps, r_ps, s_gc1, r_gc1, s_gc2, r_gc2, s_gs1, r_gs1, s_gs2, r_gs2,
           s_gc3, r_gc3, s_gc4, r_gc4, s_gs3, r_gs3,
           s_z0, r_z0, s_mx, r_mx):
    gx, gy, gz = (lax.axis_index(a) for a in AXES)
    me = (gx, gy, gz)
    core = lax.rem(gy, 2)
    twin = (gx, gy + 1 - 2 * core, gz)

    def device(offset):
        return tuple(lax.rem(m + (o % n), n) if o % n else m for m, o, n in zip(me, offset, SIZES))

    def send(src, dst, ssem, rsem, offset=None):
        copy = pltpu.make_async_remote_copy(src_ref=src, dst_ref=dst, send_sem=ssem, recv_sem=rsem,
                                            device_id=twin if offset is None else device(offset),
                                            device_id_type=MESH)
        copy.start()
        return copy

    def wait(copies):
        for copy in copies:
            copy.wait()

    local = [pltpu.make_async_copy(src, E0.at[k, pl.ds(6, 16), pl.ds(8, 16)], sem_in.at[k])
             for k, src in enumerate((f_in, s_in, u_in, b_in))]
    for copy in local:
        copy.start()
    barrier = pltpu.get_barrier_semaphore()
    for offset in PARTNERS:
        pl.semaphore_signal(barrier, inc=1, device_id=device(offset), device_id_type=MESH)

    q24 = (iota((24, 128), 0) + iota((24, 128), 1)) % 2 == 1
    q32 = (iota((32, 128), 0) + iota((32, 128), 1)) % 2 == 1
    q16 = (iota((16, 128), 0) + iota((16, 128), 1)) % 2 == 1
    lane24 = iota((24, 128), 1)
    one, zero = jnp.float32(1.0), jnp.float32(0.0)

    def y_mask(rows, own_start, own_count):
        row = iota((rows, 128), 0)
        low = jnp.where(gy == 0, zero, one)
        high = jnp.where(gy == 7, zero, one)
        return jnp.where(row < own_start, low, jnp.where(row >= own_start + own_count, high, one))

    def z_mask(rows, low_at, high_at):
        lane = iota((rows, 128), 1)
        low = jnp.where(gz == 0, zero, one)
        high = jnp.where(gz == 3, zero, one)
        return jnp.where(low_at(lane), low, jnp.where(high_at(lane), high, one))

    y32 = y_mask(32, 8, 16)
    mask0 = (y32, y32 * z_mask(32, lambda l: l >= 64, lambda l: l < 64))
    mask1 = (y_mask(40, 16, 8) * z_mask(40, lambda l: l < 32, lambda l: l >= 96),)

    def x_scalar(p, low_end, high_start):
        outside = ((gx == 0) & (p < low_end)) | ((gx == 7) & (p >= high_start))
        return jnp.where(outside, zero, one)

    row, col = iota((128, 128), 0), iota((128, 128), 1)
    to_one = jnp.where((col >= 32) & (col < 96) & (col - 32 == row // 2), 0.125, 0.0).astype(BF16)
    to_two = jnp.where((row >= 32) & (row < 96) & (col == (row - 32) // 2), 0.125, 0.0).astype(BF16)
    from_two = jnp.where((col - 32 + 64 * gz + 128) // 2 - 64 == row, 1.0, 0.0).astype(BF16)
    from_one = jnp.where(row - 32 == col // 2, 1.0, 0.0).astype(BF16)
    from_one_edge = jnp.where(
        ((col < 64) & (row == 96 + col // 2)) | ((col >= 64) & (row == col // 2 - 32)), 1.0, 0.0
    ).astype(BF16)

    def restrict_one(sums):
        T16[...] = sums
        folded = T16[:, pl.ds(0, 8, stride=2), :] + T16[:, pl.ds(1, 8, stride=2), :]
        return pick(folded.reshape(64, 128), to_one).reshape(8, 8, 128)

    def restrict_two(sums):
        T8[0:4] = sums
        total = None
        for x in range(4):
            folded = T8[x, pl.ds(0, 4, stride=2), :] + T8[x, pl.ds(1, 4, stride=2), :]
            T4[x, 0:4] = folded
        full = pick(T4[...].reshape(32, 128), to_two).reshape(4, 8, 128)
        for x in range(4):
            term = roll(full[x], 32 * x)
            total = term if total is None else total + term
        return total[0:4]

    for copy in local:
        copy.wait()
    upper = iota((8, 128), 0) < 4
    for n, (dx, dy, _) in enumerate(CORNERS):
        x, y = (18 if dx > 0 else 6), (16 if dy > 0 else 8)
        for a in range(4):
            for k in range(2):
                first, second = E0[a, x + 2 * k, pl.ds(y, 8), :], E0[a, x + 2 * k + 1, pl.ds(y, 8), :]
                if dy > 0:
                    first = pltpu.roll(first, 4, 0)
                else:
                    second = pltpu.roll(second, 4, 0)
                CP[n, a, k] = jnp.where(upper, first, second)

    lane16 = iota((16, 128), 1)
    group = lane16 // 16

    def pack_rows(k, carry):
        total = jnp.zeros((16, 128), F32)
        for odd in range(2):
            for a in range(4):
                value = E0[a, 6 + 2 * k + odd, pl.ds(8, 16), :]
                total = jnp.where(group == 4 * odd + a, roll(value, 8 + 16 * a + 64 * odd), total)
        M0[k] = total
        return carry

    loop(0, 8, pack_rows, 0, 4)
    pl.semaphore_wait(barrier, len(PARTNERS))
    z0 = [send(M0, RZ0.at[n], s_z0.at[n], r_z0.at[n], (0, 0, 1 if n == 0 else -1)) for n in range(2)]
    e0 = [send(E0.at[:, source_span(dx, 6, 16, 5), source_span(dy, 8, 16, 8)],
               E0.at[:, target_span(dx, 6, 16, 5), target_span(dy, 8, 16, 8)],
               s_e0.at[n], r_e0.at[n], (dx, dy, 0)) for n, (dx, dy, _) in enumerate(XY4)]
    for n, (dx, dy, _) in enumerate(CORNERS):
        e0.append(send(CP.at[n], CR.at[n], s_e0.at[4 + n], r_e0.at[4 + n], (dx, dy, 0)))

    for k, a in ((0, 1), (1, 3)):
        sums = jnp.stack([E0[a, 6 + 2 * x, pl.ds(8, 16), :] + E0[a, 7 + 2 * x, pl.ds(8, 16), :] for x in range(8)])
        C1[k, pl.ds(8, 8), pl.ds(8, 8)] = restrict_one(sums)
        for x in range(8):
            R1s[k, x] = roll(C1[k, 8 + x, pl.ds(8, 8), :], 64)
    c1z = [send(R1s, RZ1.at[n], s_c1z.at[n], r_c1z.at[n], (0, 0, 1 if n == 0 else -1)) for n in range(2)]
    mine = gy * 4 + gz
    for k in range(2):
        sums = jnp.stack([C1[k, 8 + 2 * x, pl.ds(8, 8), :] + C1[k, 9 + 2 * x, pl.ds(8, 8), :] for x in range(4)])
        GC[mine, gx, k] = restrict_two(sums)
    gc1 = [send(GC.at[mine, gx], GC.at[mine, gx], s_gc1.at[n], r_gc1.at[n], o) for n, o in enumerate(RING7)]
    wait(z0)
    for k in range(8):
        MX[2 + k, pl.ds(8, 16)] = jnp.where(lane16 % 16 < 8, RZ0[0, k], RZ0[1, k])
    mx = [send(MX.at[source_span(dx, 2, 8, 2), source_span(dy, 8, 16, 8)],
               MX.at[target_span(dx, 2, 8, 2), target_span(dy, 8, 16, 8)],
               s_mx.at[n], r_mx.at[n], (dx, dy, 0)) for n, (dx, dy, _) in enumerate(XY8)]
    wait(c1z)
    lane8 = iota((8, 128), 1)
    for k in range(2):
        for x in range(8):
            own = C1[k, 8 + x, pl.ds(8, 8), :]
            C1[k, 8 + x, pl.ds(8, 8), :] = jnp.where(
                lane8 < 32, RZ1[0, k, x], jnp.where(lane8 < 96, own, RZ1[1, k, x]))
    def around(O, tiles, c, i, r0, q):
        out = []
        centre = [O[t, 1 - c, i + 1, pl.ds(r0, 24), :] for t in range(tiles)]
        ups = [roll(v, -1) for v in centre]
        downs = [roll(v, 1) for v in centre]
        for t in range(tiles):
            low = O[t, 1 - c, i, pl.ds(r0, 24), :]
            high = O[t, 1 - c, i + 2, pl.ds(r0, 24), :]
            other = jnp.where(q, high, low) if c == 0 else jnp.where(q, low, high)
            yp = O[t, 1 - c, i + 1, pl.ds(r0 + 1, 24), :]
            ym = O[t, 1 - c, i + 1, pl.ds(r0 - 1, 24), :]
            if tiles == 2:
                zp = jnp.where(lane24 == 127, ups[1 - t], ups[t])
                zm = jnp.where(lane24 == 0, downs[1 - t], downs[t])
            else:
                zp, zm = ups[0], downs[0]
            out.append((centre[t], other, yp, ym, zp, zm))
        return out

    def coefficients(PB, A, D, DG, tiles, r0, scale, shift_of, mask, x_of, lo=0, hi=12):
        for c in range(2):
            def body(i, carry):
                near = around(PB, tiles, c, i, r0, q24)
                for t in range(tiles):
                    b = PB[t, c, i + 1, pl.ds(r0, 24), :]
                    total = shift_of(t, c, i)
                    weights = [(0.5 * scale) * (b + v) for v in near[t]]
                    for w in weights:
                        total = total + w
                    inverse = (1.0 / total) * (mask[t][r0:r0 + 24] * x_of(i + 1))
                    DG[t, c, i] = total
                    D[t, c, i] = inverse
                    for k, w in enumerate(weights):
                        A[t, c, k, i] = w * inverse
                return carry
            loop(lo, hi, body, 0, 4)

    def relaxed(V, A, FD, tiles, c, i, r0):
        near = around(V, tiles, c, i, r0, q24)
        out = []
        for t in range(tiles):
            total = FD[t, c, i]
            for k, v in enumerate(near[t]):
                total = total + A[t, c, k, i] * v
            out.append(total)
        return out

    def half(V, A, FD, tiles, c, r0, lo, hi, unroll):

        def body(k, carry):
            first = lo + k * unroll
            news = [relaxed(V, A, FD, tiles, c, first + j, r0) for j in range(unroll)]
            for j, new in enumerate(news):
                for t in range(tiles):
                    V[t, c, first + j + 1, pl.ds(r0, 24), :] = new[t]
            return carry
        lax.fori_loop(0, (hi - lo) // unroll, body, 0)

    def sweeps(V, A, FD, tiles, r0, spans, first=0):
        for step in range(first, 4):
            half(V, A, FD, tiles, step % 2, r0, *spans[step // 2])

    def residual_pair(V, A, FD, DG, tiles, i, r0):
        out = []
        for c in range(2):
            new = relaxed(V, A, FD, tiles, c, i, r0)[0]
            out.append(DG[0, c, i] * (new - V[0, c, i + 1, pl.ds(r0, 24), :]))
        return out

    def unpack(red, black, q):
        return jnp.where(q, black, red), jnp.where(q, red, black)

    PD[...] = jnp.zeros_like(PD)
    B2[...] = jnp.zeros_like(B2)
    V1[...] = jnp.zeros_like(V1)
    PB1[...] = jnp.zeros_like(PB1)
    wait(e0)
    for n, (dx, dy, _) in enumerate(CORNERS):
        x, y = (2 if dx > 0 else 22), (4 if dy > 0 else 24)
        for a in range(4):
            for k in range(2):
                tile = CR[n, a, k]
                E0[a, x + 2 * k, pl.ds(y, 4), :] = tile[0:4]
                E0[a, x + 2 * k + 1, pl.ds(y, 4), :] = tile[4:8]
    wait(mx)
    c1 = [send(C1.at[:, source_span(dx, 8, 8, 8), source_span(dy, 8, 8, 8)],
               C1.at[:, target_span(dx, 8, 8, 8), target_span(dy, 8, 8, 8)],
               s_c1.at[n], r_c1.at[n], (dx, dy, 0)) for n, (dx, dy, _) in enumerate(XY8)]

    lane32 = iota((32, 128), 1)

    def edge_of(a, p):
        merged = MX[p - 1]
        return roll(merged, -(16 * a + 8)), roll(merged, -(16 * a + 72))

    x0 = lambda p: x_scalar(p, 3, 11)
    x1 = lambda p: x_scalar(p, 5, 9)

    def pack0(p, carry):
        xs = x0(p)
        for dst, a in ((V0, 2), (PB0, 3)):
            even, odd = E0[a, 2 * p], E0[a, 2 * p + 1]
            m = mask0[0] * xs
            dst[0, 0, p] = jnp.where(q32, odd, even) * m
            dst[0, 1, p] = jnp.where(q32, even, odd) * m
        return carry

    loop(0, 14, pack0, 0, 7)
    for p in (0, 13):
        for dst in (V0, PB0):
            for c in range(2):
                dst[1, c, p] = jnp.zeros((32, 128), F32)

    def pack0_edge(p, carry):
        xs = x0(p)
        for dst, a in ((V0, 2), (PB0, 3)):
            even, odd = edge_of(a, p)
            m = mask0[1] * xs
            dst[1, 0, p] = jnp.where(q32, odd, even) * m
            dst[1, 1, p] = jnp.where(q32, even, odd) * m
        for dst, a in ((FD0, 0), (DG0, 1)):
            even, odd = edge_of(a, p)
            dst[1, 0, p - 1] = jnp.where(q32, odd, even)[4:28]
            dst[1, 1, p - 1] = jnp.where(q32, even, odd)[4:28]
            even, odd = E0[a, 2 * p, pl.ds(4, 24), :], E0[a, 2 * p + 1, pl.ds(4, 24), :]
            dst[0, 0, p - 1] = jnp.where(q24, odd, even)
            dst[0, 1, p - 1] = jnp.where(q24, even, odd)
        return carry

    loop(1, 13, pack0_edge, 0, 6)
    coefficients(PB0, A0, D0, DG0, 2, 4, 1.0, lambda t, c, i: DG0[t, c, i], mask0, x0)

    def scale_rhs0(i, carry):
        for t in range(2):
            for c in range(2):
                FD0[t, c, i] = FD0[t, c, i] * D0[t, c, i]
        return carry

    loop(0, 12, scale_rhs0, 0, 4)
    wait(gc1)
    gc2 = [send(GC.at[mine], GC.at[mine], s_gc2.at[n], r_gc2.at[n], o) for n, o in enumerate(ROW3)]
    sweeps(V0, A0, FD0, 2, 4, ((0, 12, 4), (1, 11, 5)))

    sums = []
    for i in range(2, 10):
        red, black = residual_pair(V0, A0, FD0, DG0, 2, i, 4)
        sums.append((red + black)[4:20])
    S1[pl.ds(8, 8), pl.ds(8, 8)] = restrict_one(jnp.stack(sums))
    slot = iota((8, 128), 1) // 16
    for g in range(2):
        total = jnp.zeros((8, 128), F32)
        for k in range(4):
            value = roll(S1[8 + 4 * g + k, pl.ds(8, 8), :], 64 + 32 * k)
            total = jnp.where((slot == 1 + 2 * k) | (slot == (6 + 2 * k) % 8), value, total)
        M1[g] = total
    e2 = []
    for n, (dx, dy, dz) in enumerate(ALL26):
        if dz == 0:
            e2.append(send(S1.at[source_span(dx, 8, 8, 4), source_span(dy, 8, 8, 8)],
                           S1.at[target_span(dx, 8, 8, 4), target_span(dy, 8, 8, 8)],
                           s_e2.at[n], r_e2.at[n], (dx, dy, dz)))
        else:
            side = 0 if dz > 0 else 1
            e2.append(send(M1.at[source_span(dx, 0, 2, 1), source_span(dy, 0, 8, 8)],
                           ZR1.at[side, target_span(dx, 1, 2, 1), target_span(dy, 8, 8, 8)],
                           s_e2.at[n], r_e2.at[n], (dx, dy, dz)))

    for i in range(2, 10):
        red, black = V0[0, 0, i + 1, pl.ds(8, 16), :], V0[0, 1, i + 1, pl.ds(8, 16), :]
        EU[0, 2 * i + 2, pl.ds(8, 16)], EU[0, 2 * i + 3, pl.ds(8, 16)] = unpack(red, black, q16)
    for g in range(2):
        total = jnp.zeros((16, 128), F32)
        for k in range(8):
            total = jnp.where(group == k, roll(EU[0, 6 + 8 * g + k, pl.ds(8, 16), :], 8 + 16 * k), total)
        MU[g] = total
    uz = [send(MU, ZU.at[n], s_uz.at[n], r_uz.at[n], (0, 0, 1 if n == 0 else -1)) for n in range(2)]

    wait(gc2)
    row_of = GC.at[pl.ds(gy * 4, 4)]
    gc3 = [send(row_of, row_of, s_gc3.at[n], r_gc3.at[n], o) for n, o in enumerate(CHIPS3)]
    wait(c1)

    def pack1(p, carry):
        xs = x1(p)
        m = mask1[0][8:32] * xs
        even, odd = C1[1, 2 * p - 2], C1[1, 2 * p - 1]
        PB1[0, 0, p, pl.ds(8, 24), :] = jnp.where(q24, odd, even) * m
        PB1[0, 1, p, pl.ds(8, 24), :] = jnp.where(q24, even, odd) * m
        even, odd = C1[0, 2 * p - 2], C1[0, 2 * p - 1]
        DG1[0, 0, p - 1] = jnp.where(q24, odd, even)
        DG1[0, 1, p - 1] = jnp.where(q24, even, odd)
        return carry

    def coefficients1(lo, hi):
        loop(lo + 1, hi + 1, pack1, 0, 4)
        coefficients(PB1, A1, D1, DG1, 1, 8, 0.25, lambda t, c, i: DG1[t, c, i], mask1, x1, lo, hi)

    coefficients1(0, 12)
    wait(e2)
    slot24 = lane24 // 16
    for x in range(4, 20):
        g = (x - 4) // 4
        merged = jnp.where(slot24 % 2 == 1, ZR1[0, g], ZR1[1, g])
        halo = roll(merged, -32 * (x % 4))
        S1[x] = jnp.where((lane24 >= 32) & (lane24 < 96), S1[x], halo)
    PS[1, pl.ds(8, 8), pl.ds(8, 8)] = S1[pl.ds(8, 8), pl.ds(8, 8)]

    def rhs1(source, lo, hi):
        def body(i, carry):
            even, odd = source[2 * i], source[2 * i + 1]
            FD1[0, 0, i] = jnp.where(q24, odd, even) * D1[0, 0, i]
            FD1[0, 1, i] = jnp.where(q24, even, odd) * D1[0, 1, i]
            return carry
        loop(lo, hi, body, 0, 4)

    rhs1(S1, 2, 10)
    for i in range(2, 10):
        V1[0, 0, i + 1, pl.ds(8, 24), :] = FD1[0, 0, i]
    sweeps(V1, A1, FD1, 1, 8, ((2, 10, 4), (3, 9, 6)), first=1)
    sums = []
    for i in range(4, 8):
        red, black = residual_pair(V1, A1, FD1, DG1, 1, i, 8)
        sums.append((red + black)[8:16])
    GS[mine, gx] = restrict_two(jnp.stack(sums))
    gs1 = [send(GS.at[mine, gx], GS.at[mine, gx], s_gs1.at[n], r_gs1.at[n], o) for n, o in enumerate(RING7)]

    wait(gc3)
    gc4 = []
    for n in range(4):
        rows = GC.at[pl.ds((core + 2 * n) * 4, 4)]
        gc4.append(send(rows, rows, s_gc4.at[n], r_gc4.at[n]))
    q8 = (iota((8, 128), 0) + iota((8, 128), 1)) % 2 == 1
    for i in range(4, 8):
        red, black = V1[0, 0, i + 1, pl.ds(16, 8), :], V1[0, 1, i + 1, pl.ds(16, 8), :]
        PS[0, 2 * i, pl.ds(8, 8)], PS[0, 2 * i + 1, pl.ds(8, 8)] = unpack(red, black, q8)
    wait(uz)
    for x in range(16):
        merged = jnp.where(lane16 % 16 < 8, ZU[0, x // 8], ZU[1, x // 8])
        EU[1, 6 + x, pl.ds(8, 16)] = roll(merged, -(16 * (x % 8) + 8))
    wait(gs1)
    gs2 = [send(GS.at[mine], GS.at[mine], s_gs2.at[n], r_gs2.at[n], o) for n, o in enumerate(SAME15)]
    gs3 = [send(GS.at[mine], GS.at[mine], s_gs3.at[15], r_gs3.at[15])]
    ps = [send(PS.at[:, source_span(dx, 8, 8, 8), source_span(dy, 8, 8, 8)],
               PS.at[:, target_span(dx, 8, 8, 8), target_span(dy, 8, 8, 8)],
               s_ps.at[n], r_ps.at[n], (dx, dy, 0)) for n, (dx, dy, _) in enumerate(XY8)]

    lane_group = lane8 // 32

    def spread(load, store):
        def body(g, carry):
            for pair in range(4):
                blocks = [jnp.concatenate([load(8 * pair + k, g), load(8 * pair + 4 + k, g)], axis=0)
                          for k in range(4)]
                for x in range(4):
                    total = roll(blocks[0], -32 * x)
                    for k in range(1, 4):
                        total = jnp.where(lane_group == k, roll(blocks[k], 32 * (k - x)), total)
                    store(4 * g + x, 8 * pair, total)
            return carry
        loop(0, 8, body, 0, 4)

    def store_s2(x, y, v):
        S2[x, pl.ds(y, 8), :] = v

    def store_b2(x, y, v):
        B2[x + 4, pl.ds(y + 8, 8), :] = v

    def store_source(x, y, v):
        PD[x + 4, pl.ds(y + 8, 8), :] = v
        RM[x, pl.ds(y, 8), :] = v

    wait(gc4)
    spread(lambda j, g: GC[j, g, 0], store_s2)
    spread(lambda j, g: GC[j, g, 1], store_b2)

    def shifts(O, x):
        centre = O[x + 4, pl.ds(8, 32), :]
        return (centre, (O[x + 5, pl.ds(8, 32), :], O[x + 3, pl.ds(8, 32), :], O[x + 4, pl.ds(9, 32), :],
                         O[x + 4, pl.ds(7, 32), :], roll(centre, -1), roll(centre, 1)))

    def weights2(x, carry):
        b, near = shifts(B2, x)
        total = S2[x]
        for k, v in enumerate(near):
            if k == 4:
                v = jnp.where(lane32 == 127, 0.0, v)
            if k == 5:
                v = jnp.where(lane32 == 0, 0.0, v)
            w = (0.5 * 0.0625) * (b + v)
            total = total + w
            if k == 4:
                w = jnp.where(lane32 == 127, 0.0, w)
            if k == 5:
                w = jnp.where(lane32 == 0, 0.0, w)
            A2[k, x] = w
        DG2[x] = total
        return carry

    loop(0, 32, weights2, 0, 8)


    for n, (_, j, k) in enumerate(SAME15):
        gs2[n].wait()
        came = GS.at[lax.rem(gy + 8 - j, 8) * 4 + lax.rem(gz + 4 - k, 4)]
        gs3.append(send(came, came, s_gs3.at[n], r_gs3.at[n]))
    wait(gs3)
    eu = [send(EU.at[:, source_span(dx, 6, 16, 5), source_span(dy, 8, 16, 8)],
               EU.at[:, target_span(dx, 6, 16, 5), target_span(dy, 8, 16, 8)],
               s_u.at[n], r_u.at[n], (dx, dy, 0)) for n, (dx, dy, _) in enumerate(XY8)]
    spread(lambda j, g: GS[j, g], store_source)
    XL[...] = jnp.zeros_like(XL)

    def whole(total):
        return jnp.sum(jnp.sum(total, axis=0, keepdims=True), axis=1, keepdims=True)

    def square(x, total):
        return total + RM[x] * RM[x]

    acc = jnp.zeros((32, 128), F32)
    RM[32] = acc
    rr = whole(loop(0, 32, square, acc, 8))
    for step in range(CG_ITERS):
        def plane(x):
            value = PD[x + 4, pl.ds(8, 32), :]
            if step:
                value = RM[x] + ratio * value
                PD[x + 4, pl.ds(8, 32), :] = value
            return value

        if step:
            plane(0)

        def image(g, total):
            start = 16 * g
            before = PD[start + 3, pl.ds(8, 32), :]
            weight = A2[1, start]
            p = PD[start + 4, pl.ds(8, 32), :]
            for j in range(16):
                x = start + j
                after = plane(x + 1)
                value = DG2[x] * p - weight * before
                weight = A2[0, x]
                value = value - weight * after
                value = value - A2[2, x] * PD[x + 4, pl.ds(9, 32), :]
                value = value - A2[3, x] * PD[x + 4, pl.ds(7, 32), :]
                value = value - A2[4, x] * roll(p, -1) - A2[5, x] * roll(p, 1)
                AP[x] = value
                total = total + p * value
                before, p = p, after
            return total

        alpha = rr / whole(lax.fori_loop(0, 32 // 16, image, acc))

        def gain(x, carry):
            XL[x] = XL[x] + alpha * PD[4 * gx + x, pl.ds(4 * gy + 4, 16), :]
            return carry

        loop(0, 12, gain, 0, 12)
        if step < CG_ITERS - 1:
            def update(x, total):
                value = RM[x] - alpha * AP[x]
                RM[x] = value
                return total + value * value

            new = whole(loop(0, 32, update, acc, 16))
            ratio = new / rr

            rr = new

    wait(ps)

    def pack1_post(p, carry):
        m = mask1[0][8:32] * x1(p)
        even, odd = PS[0, 2 * p - 2], PS[0, 2 * p - 1]
        V1[0, 0, p, pl.ds(8, 24), :] = jnp.where(q24, odd, even) * m
        V1[0, 1, p, pl.ds(8, 24), :] = jnp.where(q24, even, odd) * m
        return carry

    loop(1, 13, pack1_post, 0, 4)
    rhs1(PS.at[1], 0, 12)

    wait(eu)

    def pack0_post(p, carry):
        xs = x0(p)
        for t in range(2):
            m = mask0[t] * xs
            even, odd = EU[t, 2 * p], EU[t, 2 * p + 1]
            V0[t, 0, p] = jnp.where(q32, odd, even) * m
            V0[t, 1, p] = jnp.where(q32, even, odd) * m
        return carry

    loop(0, 14, pack0_post, 0, 2)

    fine = pick(XL[...].reshape(192, 128), from_two).reshape(12, 16, 128)
    X16[:, pl.ds(0, 16, stride=2), :] = fine
    X16[:, pl.ds(1, 16, stride=2), :] = fine

    def correct1(i, carry):
        for c in range(2):
            V1[0, c, i + 1, pl.ds(8, 24), :] = V1[0, c, i + 1, pl.ds(8, 24), :] + X16[i, 0:24]
        return carry

    loop(0, 12, correct1, 0, 12)
    sweeps(V1, A1, FD1, 1, 8, ((1, 11, 5), (2, 10, 4)))

    planes = []
    for p in range(14):
        k = (p + 7) // 2
        red, black = V1[0, 0, k, pl.ds(12, 16), :], V1[0, 1, k, pl.ds(12, 16), :]
        planes.append(unpack(red, black, q16)[0 if p % 2 else 1])
    coarse = jnp.stack(planes).reshape(224, 128)
    for t, matrix in enumerate((from_one, from_one_edge)):
        fine = pick(coarse, matrix).reshape(14, 16, 128)
        XB[:, pl.ds(0, 16, stride=2), :] = fine
        XB[:, pl.ds(1, 16, stride=2), :] = fine

        def correct0(p, carry):
            for c in range(2):
                V0[t, c, p] = V0[t, c, p] + XB[p]
            return carry

        loop(0, 14, correct0, 0, 7)
    sweeps(V0, A0, FD0, 2, 4, ((0, 12, 4), (1, 11, 5)))

    def finish(i, carry):
        red, black = residual_pair(V0, A0, FD0, DG0, 2, i, 4)
        even, odd = unpack(red, black, q24)
        r_out[2 * i - 4] = even[4:20]
        r_out[2 * i - 3] = odd[4:20]
        even, odd = unpack(V0[0, 0, i + 1, pl.ds(8, 16), :], V0[0, 1, i + 1, pl.ds(8, 16), :], q16)
        x_out[2 * i - 4] = even
        x_out[2 * i - 3] = odd
        return carry

    loop(2, 10, finish, 0, 4)


def vmem(*shape):
    return pltpu.VMEM(shape, F32)


def dma(*shape):
    return pltpu.SemaphoreType.DMA(shape)


SCRATCH = [
    vmem(4, 28, 32, 128), vmem(8, 16, 128), vmem(12, 32, 128), vmem(2, 8, 16, 128),
    vmem(4, 4, 2, 8, 128), vmem(4, 4, 2, 8, 128),
    vmem(2, 2, 14, 32, 128), vmem(2, 2, 14, 32, 128), vmem(2, 2, 6, 12, 24, 128),
    vmem(2, 2, 12, 24, 128), vmem(2, 2, 12, 24, 128), vmem(2, 2, 12, 24, 128),
    vmem(2, 24, 24, 128), vmem(2, 8, 8, 128), vmem(2, 2, 8, 8, 128),
    vmem(24, 24, 128), vmem(2, 8, 128), vmem(2, 4, 24, 128), vmem(2, 24, 24, 128),
    vmem(1, 2, 14, 40, 128), vmem(1, 2, 14, 40, 128), vmem(1, 2, 6, 12, 24, 128),
    vmem(1, 2, 12, 24, 128), vmem(1, 2, 12, 24, 128), vmem(1, 2, 12, 24, 128),
    vmem(2, 28, 32, 128), vmem(2, 16, 128), vmem(2, 2, 16, 128),
    vmem(8, 16, 128), vmem(6, 8, 128), vmem(4, 8, 128), vmem(12, 32, 128), vmem(14, 32, 128),
    vmem(33, 8, 2, 4, 128), vmem(33, 8, 4, 128),
    vmem(32, 32, 128), vmem(40, 48, 128), vmem(6, 32, 32, 128), vmem(32, 32, 128),
    vmem(40, 48, 128), vmem(33, 32, 128), vmem(32, 32, 128), vmem(12, 16, 128),
    dma(4), dma(8), dma(8), dma(2), dma(2), dma(8), dma(8), dma(26), dma(26), dma(2), dma(2), dma(8), dma(8),
    dma(8), dma(8), dma(7), dma(7), dma(3), dma(3), dma(7), dma(7), dma(15), dma(15),
    dma(3), dma(3), dma(4), dma(4), dma(16), dma(16),
    dma(2), dma(2), dma(8), dma(8),
]


def solution(mesh):
    def local(right_side, initial, shift, beta):
        shape = jax.ShapeDtypeStruct(right_side.shape, F32)
        return pl.pallas_call(
            kernel,
            out_shape=(shape, shape),
            in_specs=[pl.BlockSpec(memory_space=pl.ANY)] * 4,
            out_specs=(pl.BlockSpec(memory_space=pltpu.VMEM),) * 2,
            scratch_shapes=SCRATCH,
            compiler_params=pltpu.CompilerParams(
                collective_id=0, has_side_effects=True, vmem_limit_bytes=56 * 2**20),
        )(right_side, initial, shift, beta)

    spec = P(*AXES)
    return jax.shard_map(local, mesh=mesh, in_specs=(spec,) * 4, out_specs=(spec, spec), check_vma=False)
```

```python
import itertools

import jax
import jax.numpy as jnp
from jax import lax
from jax.experimental import pallas as pl
from jax.experimental.pallas import tpu as pltpu
from jax.sharding import PartitionSpec as P

CG_ITERS = 8
MESH = pl.DeviceIdType.MESH
AXES = ("gx", "gy", "gz")
SIZES = (8, 8, 4)
F32 = jnp.float32
BF16 = jnp.bfloat16

ALL26 = sorted((o for o in itertools.product((-1, 0, 1), repeat=3) if o != (0, 0, 0)),
               key=lambda o: -sum(map(abs, o)))
XY8 = [o for o in ALL26 if o[2] == 0]
XY4 = [o for o in XY8 if o[0] * o[1] == 0]
CORNERS = [o for o in XY8 if o[0] * o[1] != 0]
RING7 = [(k, 0, 0) for k in range(1, 8)]
ROW3 = [(0, 0, k) for k in range(1, 4)]
CHIPS3 = [(0, j, 0) for j in (2, 4, 6)]
SAME15 = sorted(((0, j, k) for j in (0, 2, 4, 6) for k in range(4) if (j, k) != (0, 0)),
                key=lambda o: min(o[1], 8 - o[1]) // 2 + min(o[2], 4 - o[2]))


def canonical(offset):
    return tuple(o % n for o, n in zip(offset, SIZES))


PARTNERS = sorted({canonical(o) for o in ALL26 + RING7 + [(0, 4, 0)]})


def source_span(d, start, count, halo):
    if d == 0:
        return pl.ds(start, count)
    return pl.ds(start + count - halo, halo) if d > 0 else pl.ds(start, halo)


def target_span(d, start, count, halo):
    if d == 0:
        return pl.ds(start, count)
    return pl.ds(start - halo, halo) if d > 0 else pl.ds(start + count, halo)


def iota(shape, dim):
    return lax.broadcasted_iota(jnp.int32, shape, dim)


def loop(lo, hi, body, init, unroll):
    def chunk(k, carry):
        for j in range(unroll):
            carry = body(lo + k * unroll + j, carry)
        return carry

    return lax.fori_loop(0, (hi - lo) // unroll, chunk, init)


def pick(values, matrix):
    high = values.astype(BF16)
    rest = values - high.astype(F32)
    middle = rest.astype(BF16)
    low = (rest - middle.astype(F32)).astype(BF16)
    out = jnp.dot(low, matrix, preferred_element_type=F32)
    out = out + jnp.dot(middle, matrix, preferred_element_type=F32)
    return out + jnp.dot(high, matrix, preferred_element_type=F32)


def roll(value, shift):
    shift = shift % 128
    return value if shift == 0 else pltpu.roll(value, shift, 1)


def kernel(f_in, u_in, s_in, b_in, x_out, r_out, E0, M0, MX, RZ0, CP, CR, V0, PB0, A0, D0, DG0, FD0,
           C1, R1s, RZ1, S1, M1, ZR1, PS, V1, PB1, A1, D1, DG1, FD1,
           EU, MU, ZU, T16, T8, T4, X16, XB, GC, GS, S2, B2, A2, DG2, PD, RM, AP, XL,
           sem_in, s_e0, r_e0, s_c1z, r_c1z, s_c1, r_c1, s_e2, r_e2, s_uz, r_uz, s_u, r_u,
           s_ps, r_ps, s_gc1, r_gc1, s_gc2, r_gc2, s_gs1, r_gs1, s_gs2, r_gs2,
           s_gc3, r_gc3, s_gc4, r_gc4, s_gs3, r_gs3,
           s_z0, r_z0, s_mx, r_mx):
    gx, gy, gz = (lax.axis_index(a) for a in AXES)
    me = (gx, gy, gz)
    core = lax.rem(gy, 2)
    twin = (gx, gy + 1 - 2 * core, gz)

    def device(offset):
        return tuple(lax.rem(m + (o % n), n) if o % n else m for m, o, n in zip(me, offset, SIZES))

    def send(src, dst, ssem, rsem, offset=None):
        copy = pltpu.make_async_remote_copy(src_ref=src, dst_ref=dst, send_sem=ssem, recv_sem=rsem,
                                            device_id=twin if offset is None else device(offset),
                                            device_id_type=MESH)
        copy.start()
        return copy

    def wait(copies):
        for copy in copies:
            copy.wait()

    local = [pltpu.make_async_copy(src, E0.at[k, pl.ds(6, 16), pl.ds(8, 16)], sem_in.at[k])
             for k, src in enumerate((f_in, s_in, u_in, b_in))]
    for copy in local:
        copy.start()
    barrier = pltpu.get_barrier_semaphore()
    for offset in PARTNERS:
        pl.semaphore_signal(barrier, inc=1, device_id=device(offset), device_id_type=MESH)

    q24 = (iota((24, 128), 0) + iota((24, 128), 1)) % 2 == 1
    q32 = (iota((32, 128), 0) + iota((32, 128), 1)) % 2 == 1
    q16 = (iota((16, 128), 0) + iota((16, 128), 1)) % 2 == 1
    lane24 = iota((24, 128), 1)
    one, zero = jnp.float32(1.0), jnp.float32(0.0)

    def y_mask(rows, own_start, own_count):
        row = iota((rows, 128), 0)
        low = jnp.where(gy == 0, zero, one)
        high = jnp.where(gy == 7, zero, one)
        return jnp.where(row < own_start, low, jnp.where(row >= own_start + own_count, high, one))

    def z_mask(rows, low_at, high_at):
        lane = iota((rows, 128), 1)
        low = jnp.where(gz == 0, zero, one)
        high = jnp.where(gz == 3, zero, one)
        return jnp.where(low_at(lane), low, jnp.where(high_at(lane), high, one))

    y32 = y_mask(32, 8, 16)
    mask0 = (y32, y32 * z_mask(32, lambda l: l >= 64, lambda l: l < 64))
    mask1 = (y_mask(40, 16, 8) * z_mask(40, lambda l: l < 32, lambda l: l >= 96),)

    def x_scalar(p, low_end, high_start):
        outside = ((gx == 0) & (p < low_end)) | ((gx == 7) & (p >= high_start))
        return jnp.where(outside, zero, one)

    row, col = iota((128, 128), 0), iota((128, 128), 1)
    to_one = jnp.where((col >= 32) & (col < 96) & (col - 32 == row // 2), 0.125, 0.0).astype(BF16)
    to_two = jnp.where((row >= 32) & (row < 96) & (col == (row - 32) // 2), 0.125, 0.0).astype(BF16)
    from_two = jnp.where((col - 32 + 64 * gz + 128) // 2 - 64 == row, 1.0, 0.0).astype(BF16)
    from_one = jnp.where(row - 32 == col // 2, 1.0, 0.0).astype(BF16)
    from_one_edge = jnp.where(
        ((col < 64) & (row == 96 + col // 2)) | ((col >= 64) & (row == col // 2 - 32)), 1.0, 0.0
    ).astype(BF16)

    def restrict_one(sums):
        T16[...] = sums
        folded = T16[:, pl.ds(0, 8, stride=2), :] + T16[:, pl.ds(1, 8, stride=2), :]
        return pick(folded.reshape(64, 128), to_one).reshape(8, 8, 128)

    def restrict_two(sums):
        T8[0:4] = sums
        total = None
        for x in range(4):
            folded = T8[x, pl.ds(0, 4, stride=2), :] + T8[x, pl.ds(1, 4, stride=2), :]
            T4[x, 0:4] = folded
        full = pick(T4[...].reshape(32, 128), to_two).reshape(4, 8, 128)
        for x in range(4):
            term = roll(full[x], 32 * x)
            total = term if total is None else total + term
        return total[0:4]

    for copy in local:
        copy.wait()
    upper = iota((8, 128), 0) < 4
    for n, (dx, dy, _) in enumerate(CORNERS):
        x, y = (18 if dx > 0 else 6), (16 if dy > 0 else 8)
        for a in range(4):
            for k in range(2):
                first, second = E0[a, x + 2 * k, pl.ds(y, 8), :], E0[a, x + 2 * k + 1, pl.ds(y, 8), :]
                if dy > 0:
                    first = pltpu.roll(first, 4, 0)
                else:
                    second = pltpu.roll(second, 4, 0)
                CP[n, a, k] = jnp.where(upper, first, second)

    lane16 = iota((16, 128), 1)
    group = lane16 // 16

    def pack_rows(k, carry):
        total = jnp.zeros((16, 128), F32)
        for odd in range(2):
            for a in range(4):
                value = E0[a, 6 + 2 * k + odd, pl.ds(8, 16), :]
                total = jnp.where(group == 4 * odd + a, roll(value, 8 + 16 * a + 64 * odd), total)
        M0[k] = total
        return carry

    loop(0, 8, pack_rows, 0, 4)
    pl.semaphore_wait(barrier, len(PARTNERS))
    z0 = [send(M0, RZ0.at[n], s_z0.at[n], r_z0.at[n], (0, 0, 1 if n == 0 else -1)) for n in range(2)]
    e0 = [send(E0.at[:, source_span(dx, 6, 16, 5), source_span(dy, 8, 16, 8)],
               E0.at[:, target_span(dx, 6, 16, 5), target_span(dy, 8, 16, 8)],
               s_e0.at[n], r_e0.at[n], (dx, dy, 0)) for n, (dx, dy, _) in enumerate(XY4)]
    for n, (dx, dy, _) in enumerate(CORNERS):
        e0.append(send(CP.at[n], CR.at[n], s_e0.at[4 + n], r_e0.at[4 + n], (dx, dy, 0)))

    for k, a in ((0, 1), (1, 3)):
        sums = jnp.stack([E0[a, 6 + 2 * x, pl.ds(8, 16), :] + E0[a, 7 + 2 * x, pl.ds(8, 16), :] for x in range(8)])
        C1[k, pl.ds(8, 8), pl.ds(8, 8)] = restrict_one(sums)
        for x in range(8):
            R1s[k, x] = roll(C1[k, 8 + x, pl.ds(8, 8), :], 64)
    c1z = [send(R1s, RZ1.at[n], s_c1z.at[n], r_c1z.at[n], (0, 0, 1 if n == 0 else -1)) for n in range(2)]
    mine = gy * 4 + gz
    for k in range(2):
        sums = jnp.stack([C1[k, 8 + 2 * x, pl.ds(8, 8), :] + C1[k, 9 + 2 * x, pl.ds(8, 8), :] for x in range(4)])
        GC[mine, gx, k] = restrict_two(sums)
    gc1 = [send(GC.at[mine, gx], GC.at[mine, gx], s_gc1.at[n], r_gc1.at[n], o) for n, o in enumerate(RING7)]
    wait(z0)
    for k in range(8):
        MX[2 + k, pl.ds(8, 16)] = jnp.where(lane16 % 16 < 8, RZ0[0, k], RZ0[1, k])
    mx = [send(MX.at[source_span(dx, 2, 8, 2), source_span(dy, 8, 16, 8)],
               MX.at[target_span(dx, 2, 8, 2), target_span(dy, 8, 16, 8)],
               s_mx.at[n], r_mx.at[n], (dx, dy, 0)) for n, (dx, dy, _) in enumerate(XY8)]
    wait(c1z)
    lane8 = iota((8, 128), 1)
    for k in range(2):
        for x in range(8):
            own = C1[k, 8 + x, pl.ds(8, 8), :]
            C1[k, 8 + x, pl.ds(8, 8), :] = jnp.where(
                lane8 < 32, RZ1[0, k, x], jnp.where(lane8 < 96, own, RZ1[1, k, x]))
    def around(O, tiles, c, i, r0, q):
        out = []
        centre = [O[t, 1 - c, i + 1, pl.ds(r0, 24), :] for t in range(tiles)]
        ups = [roll(v, -1) for v in centre]
        downs = [roll(v, 1) for v in centre]
        for t in range(tiles):
            low = O[t, 1 - c, i, pl.ds(r0, 24), :]
            high = O[t, 1 - c, i + 2, pl.ds(r0, 24), :]
            other = jnp.where(q, high, low) if c == 0 else jnp.where(q, low, high)
            yp = O[t, 1 - c, i + 1, pl.ds(r0 + 1, 24), :]
            ym = O[t, 1 - c, i + 1, pl.ds(r0 - 1, 24), :]
            if tiles == 2:
                zp = jnp.where(lane24 == 127, ups[1 - t], ups[t])
                zm = jnp.where(lane24 == 0, downs[1 - t], downs[t])
            else:
                zp, zm = ups[0], downs[0]
            out.append((centre[t], other, yp, ym, zp, zm))
        return out

    def coefficients(PB, A, D, DG, tiles, r0, scale, shift_of, mask, x_of, lo=0, hi=12):
        for c in range(2):
            def body(i, carry):
                near = around(PB, tiles, c, i, r0, q24)
                for t in range(tiles):
                    b = PB[t, c, i + 1, pl.ds(r0, 24), :]
                    total = shift_of(t, c, i)
                    weights = [(0.5 * scale) * (b + v) for v in near[t]]
                    for w in weights:
                        total = total + w
                    inverse = (1.0 / total) * (mask[t][r0:r0 + 24] * x_of(i + 1))
                    DG[t, c, i] = total
                    D[t, c, i] = inverse
                    for k, w in enumerate(weights):
                        A[t, c, k, i] = w * inverse
                return carry
            loop(lo, hi, body, 0, 4)

    def relaxed(V, A, FD, tiles, c, i, r0):
        near = around(V, tiles, c, i, r0, q24)
        out = []
        for t in range(tiles):
            total = FD[t, c, i]
            for k, v in enumerate(near[t]):
                total = total + A[t, c, k, i] * v
            out.append(total)
        return out

    def half(V, A, FD, tiles, c, r0, lo, hi, unroll):

        def body(k, carry):
            first = lo + k * unroll
            news = [relaxed(V, A, FD, tiles, c, first + j, r0) for j in range(unroll)]
            for j, new in enumerate(news):
                for t in range(tiles):
                    V[t, c, first + j + 1, pl.ds(r0, 24), :] = new[t]
            return carry
        lax.fori_loop(0, (hi - lo) // unroll, body, 0)

    def sweeps(V, A, FD, tiles, r0, spans, first=0):
        for step in range(first, 4):
            half(V, A, FD, tiles, step % 2, r0, *spans[step // 2])

    def residual_pair(V, A, FD, DG, tiles, i, r0):
        out = []
        for c in range(2):
            new = relaxed(V, A, FD, tiles, c, i, r0)[0]
            out.append(DG[0, c, i] * (new - V[0, c, i + 1, pl.ds(r0, 24), :]))
        return out

    def unpack(red, black, q):
        return jnp.where(q, black, red), jnp.where(q, red, black)

    PD[...] = jnp.zeros_like(PD)
    B2[...] = jnp.zeros_like(B2)
    V1[...] = jnp.zeros_like(V1)
    PB1[...] = jnp.zeros_like(PB1)
    wait(e0)
    for n, (dx, dy, _) in enumerate(CORNERS):
        x, y = (2 if dx > 0 else 22), (4 if dy > 0 else 24)
        for a in range(4):
            for k in range(2):
                tile = CR[n, a, k]
                E0[a, x + 2 * k, pl.ds(y, 4), :] = tile[0:4]
                E0[a, x + 2 * k + 1, pl.ds(y, 4), :] = tile[4:8]
    wait(mx)
    c1 = [send(C1.at[:, source_span(dx, 8, 8, 8), source_span(dy, 8, 8, 8)],
               C1.at[:, target_span(dx, 8, 8, 8), target_span(dy, 8, 8, 8)],
               s_c1.at[n], r_c1.at[n], (dx, dy, 0)) for n, (dx, dy, _) in enumerate(XY8)]

    lane32 = iota((32, 128), 1)

    def edge_of(a, p):
        merged = MX[p - 1]
        return roll(merged, -(16 * a + 8)), roll(merged, -(16 * a + 72))

    x0 = lambda p: x_scalar(p, 3, 11)
    x1 = lambda p: x_scalar(p, 5, 9)

    def pack0(p, carry):
        xs = x0(p)
        for dst, a in ((V0, 2), (PB0, 3)):
            even, odd = E0[a, 2 * p], E0[a, 2 * p + 1]
            m = mask0[0] * xs
            dst[0, 0, p] = jnp.where(q32, odd, even) * m
            dst[0, 1, p] = jnp.where(q32, even, odd) * m
        return carry

    loop(0, 14, pack0, 0, 7)
    for p in (0, 13):
        for dst in (V0, PB0):
            for c in range(2):
                dst[1, c, p] = jnp.zeros((32, 128), F32)

    def pack0_edge(p, carry):
        xs = x0(p)
        for dst, a in ((V0, 2), (PB0, 3)):
            even, odd = edge_of(a, p)
            m = mask0[1] * xs
            dst[1, 0, p] = jnp.where(q32, odd, even) * m
            dst[1, 1, p] = jnp.where(q32, even, odd) * m
        for dst, a in ((FD0, 0), (DG0, 1)):
            even, odd = edge_of(a, p)
            dst[1, 0, p - 1] = jnp.where(q32, odd, even)[4:28]
            dst[1, 1, p - 1] = jnp.where(q32, even, odd)[4:28]
            even, odd = E0[a, 2 * p, pl.ds(4, 24), :], E0[a, 2 * p + 1, pl.ds(4, 24), :]
            dst[0, 0, p - 1] = jnp.where(q24, odd, even)
            dst[0, 1, p - 1] = jnp.where(q24, even, odd)
        return carry

    loop(1, 13, pack0_edge, 0, 6)
    coefficients(PB0, A0, D0, DG0, 2, 4, 1.0, lambda t, c, i: DG0[t, c, i], mask0, x0)

    def scale_rhs0(i, carry):
        for t in range(2):
            for c in range(2):
                FD0[t, c, i] = FD0[t, c, i] * D0[t, c, i]
        return carry

    loop(0, 12, scale_rhs0, 0, 4)
    wait(gc1)
    gc2 = [send(GC.at[mine], GC.at[mine], s_gc2.at[n], r_gc2.at[n], o) for n, o in enumerate(ROW3)]
    sweeps(V0, A0, FD0, 2, 4, ((0, 12, 4), (1, 11, 5)))

    sums = []
    for i in range(2, 10):
        red, black = residual_pair(V0, A0, FD0, DG0, 2, i, 4)
        sums.append((red + black)[4:20])
    S1[pl.ds(8, 8), pl.ds(8, 8)] = restrict_one(jnp.stack(sums))
    slot = iota((8, 128), 1) // 16
    for g in range(2):
        total = jnp.zeros((8, 128), F32)
        for k in range(4):
            value = roll(S1[8 + 4 * g + k, pl.ds(8, 8), :], 64 + 32 * k)
            total = jnp.where((slot == 1 + 2 * k) | (slot == (6 + 2 * k) % 8), value, total)
        M1[g] = total
    e2 = []
    for n, (dx, dy, dz) in enumerate(ALL26):
        if dz == 0:
            e2.append(send(S1.at[source_span(dx, 8, 8, 4), source_span(dy, 8, 8, 8)],
                           S1.at[target_span(dx, 8, 8, 4), target_span(dy, 8, 8, 8)],
                           s_e2.at[n], r_e2.at[n], (dx, dy, dz)))
        else:
            side = 0 if dz > 0 else 1
            e2.append(send(M1.at[source_span(dx, 0, 2, 1), source_span(dy, 0, 8, 8)],
                           ZR1.at[side, target_span(dx, 1, 2, 1), target_span(dy, 8, 8, 8)],
                           s_e2.at[n], r_e2.at[n], (dx, dy, dz)))

    for i in range(2, 10):
        red, black = V0[0, 0, i + 1, pl.ds(8, 16), :], V0[0, 1, i + 1, pl.ds(8, 16), :]
        EU[0, 2 * i + 2, pl.ds(8, 16)], EU[0, 2 * i + 3, pl.ds(8, 16)] = unpack(red, black, q16)
    for g in range(2):
        total = jnp.zeros((16, 128), F32)
        for k in range(8):
            total = jnp.where(group == k, roll(EU[0, 6 + 8 * g + k, pl.ds(8, 16), :], 8 + 16 * k), total)
        MU[g] = total
    uz = [send(MU, ZU.at[n], s_uz.at[n], r_uz.at[n], (0, 0, 1 if n == 0 else -1)) for n in range(2)]

    wait(gc2)
    row_of = GC.at[pl.ds(gy * 4, 4)]
    gc3 = [send(row_of, row_of, s_gc3.at[n], r_gc3.at[n], o) for n, o in enumerate(CHIPS3)]
    wait(c1)

    def pack1(p, carry):
        xs = x1(p)
        m = mask1[0][8:32] * xs
        even, odd = C1[1, 2 * p - 2], C1[1, 2 * p - 1]
        PB1[0, 0, p, pl.ds(8, 24), :] = jnp.where(q24, odd, even) * m
        PB1[0, 1, p, pl.ds(8, 24), :] = jnp.where(q24, even, odd) * m
        even, odd = C1[0, 2 * p - 2], C1[0, 2 * p - 1]
        DG1[0, 0, p - 1] = jnp.where(q24, odd, even)
        DG1[0, 1, p - 1] = jnp.where(q24, even, odd)
        return carry

    def coefficients1(lo, hi):
        loop(lo + 1, hi + 1, pack1, 0, 4)
        coefficients(PB1, A1, D1, DG1, 1, 8, 0.25, lambda t, c, i: DG1[t, c, i], mask1, x1, lo, hi)

    coefficients1(0, 12)
    wait(e2)
    slot24 = lane24 // 16
    for x in range(4, 20):
        g = (x - 4) // 4
        merged = jnp.where(slot24 % 2 == 1, ZR1[0, g], ZR1[1, g])
        halo = roll(merged, -32 * (x % 4))
        S1[x] = jnp.where((lane24 >= 32) & (lane24 < 96), S1[x], halo)
    PS[1, pl.ds(8, 8), pl.ds(8, 8)] = S1[pl.ds(8, 8), pl.ds(8, 8)]

    def rhs1(source, lo, hi):
        def body(i, carry):
            even, odd = source[2 * i], source[2 * i + 1]
            FD1[0, 0, i] = jnp.where(q24, odd, even) * D1[0, 0, i]
            FD1[0, 1, i] = jnp.where(q24, even, odd) * D1[0, 1, i]
            return carry
        loop(lo, hi, body, 0, 4)

    rhs1(S1, 2, 10)
    for i in range(2, 10):
        V1[0, 0, i + 1, pl.ds(8, 24), :] = FD1[0, 0, i]
    sweeps(V1, A1, FD1, 1, 8, ((2, 10, 4), (3, 9, 6)), first=1)
    sums = []
    for i in range(4, 8):
        red, black = residual_pair(V1, A1, FD1, DG1, 1, i, 8)
        sums.append((red + black)[8:16])
    GS[mine, gx] = restrict_two(jnp.stack(sums))
    gs1 = [send(GS.at[mine, gx], GS.at[mine, gx], s_gs1.at[n], r_gs1.at[n], o) for n, o in enumerate(RING7)]

    wait(gc3)
    gc4 = []
    for n in range(4):
        rows = GC.at[pl.ds((core + 2 * n) * 4, 4)]
        gc4.append(send(rows, rows, s_gc4.at[n], r_gc4.at[n]))
    q8 = (iota((8, 128), 0) + iota((8, 128), 1)) % 2 == 1
    for i in range(4, 8):
        red, black = V1[0, 0, i + 1, pl.ds(16, 8), :], V1[0, 1, i + 1, pl.ds(16, 8), :]
        PS[0, 2 * i, pl.ds(8, 8)], PS[0, 2 * i + 1, pl.ds(8, 8)] = unpack(red, black, q8)
    wait(uz)
    for x in range(16):
        merged = jnp.where(lane16 % 16 < 8, ZU[0, x // 8], ZU[1, x // 8])
        EU[1, 6 + x, pl.ds(8, 16)] = roll(merged, -(16 * (x % 8) + 8))
    wait(gs1)
    gs2 = [send(GS.at[mine], GS.at[mine], s_gs2.at[n], r_gs2.at[n], o) for n, o in enumerate(SAME15)]
    gs3 = [send(GS.at[mine], GS.at[mine], s_gs3.at[15], r_gs3.at[15])]
    ps = [send(PS.at[:, source_span(dx, 8, 8, 8), source_span(dy, 8, 8, 8)],
               PS.at[:, target_span(dx, 8, 8, 8), target_span(dy, 8, 8, 8)],
               s_ps.at[n], r_ps.at[n], (dx, dy, 0)) for n, (dx, dy, _) in enumerate(XY8)]

    lane_group = lane8 // 32

    def spread(load, store):
        def body(g, carry):
            for pair in range(4):
                blocks = [jnp.concatenate([load(8 * pair + k, g), load(8 * pair + 4 + k, g)], axis=0)
                          for k in range(4)]
                for x in range(4):
                    total = roll(blocks[0], -32 * x)
                    for k in range(1, 4):
                        total = jnp.where(lane_group == k, roll(blocks[k], 32 * (k - x)), total)
                    store(4 * g + x, 8 * pair, total)
            return carry
        loop(0, 8, body, 0, 4)

    def store_s2(x, y, v):
        S2[x, pl.ds(y, 8), :] = v

    def store_b2(x, y, v):
        B2[x + 4, pl.ds(y + 8, 8), :] = v

    def store_source(x, y, v):
        PD[x + 4, pl.ds(y + 8, 8), :] = v
        RM[x, pl.ds(y, 8), :] = v

    wait(gc4)
    spread(lambda j, g: GC[j, g, 0], store_s2)
    spread(lambda j, g: GC[j, g, 1], store_b2)

    def shifts(O, x):
        centre = O[x + 4, pl.ds(8, 32), :]
        return (centre, (O[x + 5, pl.ds(8, 32), :], O[x + 3, pl.ds(8, 32), :], O[x + 4, pl.ds(9, 32), :],
                         O[x + 4, pl.ds(7, 32), :], roll(centre, -1), roll(centre, 1)))

    def weights2(x, carry):
        b, near = shifts(B2, x)
        total = S2[x]
        for k, v in enumerate(near):
            if k == 4:
                v = jnp.where(lane32 == 127, 0.0, v)
            if k == 5:
                v = jnp.where(lane32 == 0, 0.0, v)
            w = (0.5 * 0.0625) * (b + v)
            total = total + w
            if k == 4:
                w = jnp.where(lane32 == 127, 0.0, w)
            if k == 5:
                w = jnp.where(lane32 == 0, 0.0, w)
            A2[k, x] = w
        DG2[x] = total
        return carry

    loop(0, 32, weights2, 0, 8)


    for n, (_, j, k) in enumerate(SAME15):
        gs2[n].wait()
        came = GS.at[lax.rem(gy + 8 - j, 8) * 4 + lax.rem(gz + 4 - k, 4)]
        gs3.append(send(came, came, s_gs3.at[n], r_gs3.at[n]))
    eu = [send(EU.at[:, source_span(dx, 6, 16, 5), source_span(dy, 8, 16, 8)],
               EU.at[:, target_span(dx, 6, 16, 5), target_span(dy, 8, 16, 8)],
               s_u.at[n], r_u.at[n], (dx, dy, 0)) for n, (dx, dy, _) in enumerate(XY8)]
    wait(gs3)
    spread(lambda j, g: GS[j, g], store_source)
    XL[...] = jnp.zeros_like(XL)

    def whole(total):
        return jnp.sum(jnp.sum(total, axis=0, keepdims=True), axis=1, keepdims=True)

    def square(x, total):
        return total + RM[x] * RM[x]

    acc = jnp.zeros((32, 128), F32)
    RM[32] = acc
    rr = whole(loop(0, 32, square, acc, 8))
    for step in range(CG_ITERS):
        def plane(x):
            value = PD[x + 4, pl.ds(8, 32), :]
            if step:
                value = RM[x] + ratio * value
                PD[x + 4, pl.ds(8, 32), :] = value
            return value

        if step:
            plane(0)

        def image(g, total):
            start = 16 * g
            before = PD[start + 3, pl.ds(8, 32), :]
            weight = A2[1, start]
            p = PD[start + 4, pl.ds(8, 32), :]
            for j in range(16):
                x = start + j
                after = plane(x + 1)
                value = DG2[x] * p - weight * before
                weight = A2[0, x]
                value = value - weight * after
                value = value - A2[2, x] * PD[x + 4, pl.ds(9, 32), :]
                value = value - A2[3, x] * PD[x + 4, pl.ds(7, 32), :]
                value = value - A2[4, x] * roll(p, -1) - A2[5, x] * roll(p, 1)
                AP[x] = value
                total = total + p * value
                before, p = p, after
            return total

        alpha = rr / whole(lax.fori_loop(0, 32 // 16, image, acc))

        def gain(x, carry):
            XL[x] = XL[x] + alpha * PD[4 * gx + x, pl.ds(4 * gy + 4, 16), :]
            return carry

        loop(0, 12, gain, 0, 12)
        if step < CG_ITERS - 1:
            def update(x, total):
                value = RM[x] - alpha * AP[x]
                RM[x] = value
                return total + value * value

            new = whole(loop(0, 32, update, acc, 16))
            ratio = new / rr

            rr = new

    wait(ps)

    def pack1_post(p, carry):
        m = mask1[0][8:32] * x1(p)
        even, odd = PS[0, 2 * p - 2], PS[0, 2 * p - 1]
        V1[0, 0, p, pl.ds(8, 24), :] = jnp.where(q24, odd, even) * m
        V1[0, 1, p, pl.ds(8, 24), :] = jnp.where(q24, even, odd) * m
        return carry

    loop(1, 13, pack1_post, 0, 4)
    rhs1(PS.at[1], 0, 12)

    wait(eu)

    def pack0_post(p, carry):
        xs = x0(p)
        for t in range(2):
            m = mask0[t] * xs
            even, odd = EU[t, 2 * p], EU[t, 2 * p + 1]
            V0[t, 0, p] = jnp.where(q32, odd, even) * m
            V0[t, 1, p] = jnp.where(q32, even, odd) * m
        return carry

    loop(0, 14, pack0_post, 0, 2)

    fine = pick(XL[...].reshape(192, 128), from_two).reshape(12, 16, 128)
    X16[:, pl.ds(0, 16, stride=2), :] = fine
    X16[:, pl.ds(1, 16, stride=2), :] = fine

    def correct1(i, carry):
        for c in range(2):
            V1[0, c, i + 1, pl.ds(8, 24), :] = V1[0, c, i + 1, pl.ds(8, 24), :] + X16[i, 0:24]
        return carry

    loop(0, 12, correct1, 0, 12)
    sweeps(V1, A1, FD1, 1, 8, ((1, 11, 5), (2, 10, 4)))

    planes = []
    for p in range(14):
        k = (p + 7) // 2
        red, black = V1[0, 0, k, pl.ds(12, 16), :], V1[0, 1, k, pl.ds(12, 16), :]
        planes.append(unpack(red, black, q16)[0 if p % 2 else 1])
    coarse = jnp.stack(planes).reshape(224, 128)
    for t, matrix in enumerate((from_one, from_one_edge)):
        fine = pick(coarse, matrix).reshape(14, 16, 128)
        XB[:, pl.ds(0, 16, stride=2), :] = fine
        XB[:, pl.ds(1, 16, stride=2), :] = fine

        def correct0(p, carry):
            for c in range(2):
                V0[t, c, p] = V0[t, c, p] + XB[p]
            return carry

        loop(0, 14, correct0, 0, 7)
    sweeps(V0, A0, FD0, 2, 4, ((0, 12, 4), (1, 11, 5)))

    def finish(i, carry):
        red, black = residual_pair(V0, A0, FD0, DG0, 2, i, 4)
        even, odd = unpack(red, black, q24)
        r_out[2 * i - 4] = even[4:20]
        r_out[2 * i - 3] = odd[4:20]
        even, odd = unpack(V0[0, 0, i + 1, pl.ds(8, 16), :], V0[0, 1, i + 1, pl.ds(8, 16), :], q16)
        x_out[2 * i - 4] = even
        x_out[2 * i - 3] = odd
        return carry

    loop(2, 10, finish, 0, 4)


def vmem(*shape):
    return pltpu.VMEM(shape, F32)


def dma(*shape):
    return pltpu.SemaphoreType.DMA(shape)


SCRATCH = [
    vmem(4, 28, 32, 128), vmem(8, 16, 128), vmem(12, 32, 128), vmem(2, 8, 16, 128),
    vmem(4, 4, 2, 8, 128), vmem(4, 4, 2, 8, 128),
    vmem(2, 2, 14, 32, 128), vmem(2, 2, 14, 32, 128), vmem(2, 2, 6, 12, 24, 128),
    vmem(2, 2, 12, 24, 128), vmem(2, 2, 12, 24, 128), vmem(2, 2, 12, 24, 128),
    vmem(2, 24, 24, 128), vmem(2, 8, 8, 128), vmem(2, 2, 8, 8, 128),
    vmem(24, 24, 128), vmem(2, 8, 128), vmem(2, 4, 24, 128), vmem(2, 24, 24, 128),
    vmem(1, 2, 14, 40, 128), vmem(1, 2, 14, 40, 128), vmem(1, 2, 6, 12, 24, 128),
    vmem(1, 2, 12, 24, 128), vmem(1, 2, 12, 24, 128), vmem(1, 2, 12, 24, 128),
    vmem(2, 28, 32, 128), vmem(2, 16, 128), vmem(2, 2, 16, 128),
    vmem(8, 16, 128), vmem(6, 8, 128), vmem(4, 8, 128), vmem(12, 32, 128), vmem(14, 32, 128),
    vmem(33, 8, 2, 4, 128), vmem(33, 8, 4, 128),
    vmem(32, 32, 128), vmem(40, 48, 128), vmem(6, 32, 32, 128), vmem(32, 32, 128),
    vmem(40, 48, 128), vmem(33, 32, 128), vmem(32, 32, 128), vmem(12, 16, 128),
    dma(4), dma(8), dma(8), dma(2), dma(2), dma(8), dma(8), dma(26), dma(26), dma(2), dma(2), dma(8), dma(8),
    dma(8), dma(8), dma(7), dma(7), dma(3), dma(3), dma(7), dma(7), dma(15), dma(15),
    dma(3), dma(3), dma(4), dma(4), dma(16), dma(16),
    dma(2), dma(2), dma(8), dma(8),
]


def solution(mesh):
    def local(right_side, initial, shift, beta):
        shape = jax.ShapeDtypeStruct(right_side.shape, F32)
        return pl.pallas_call(
            kernel,
            out_shape=(shape, shape),
            in_specs=[pl.BlockSpec(memory_space=pl.ANY)] * 4,
            out_specs=(pl.BlockSpec(memory_space=pltpu.VMEM),) * 2,
            scratch_shapes=SCRATCH,
            compiler_params=pltpu.CompilerParams(
                collective_id=0, has_side_effects=True, vmem_limit_bytes=56 * 2**20),
        )(right_side, initial, shift, beta)

    spec = P(*AXES)
    return jax.shard_map(local, mesh=mesh, in_specs=(spec,) * 4, out_specs=(spec, spec), check_vma=False)
```
